512 devices in a mesh: dp: 32 (over x, z_lo, core), mp: 16 (over z_hi, y).
Axes of the slice: x: 4, y: 8, z: 8 (z_hi: 2, z_lo: 4; z = z_hi * 4 + z_lo), core: 2. Of those that a mesh axis runs over, the one named last changes fastest.
Arguments:
- inputs: bfloat16 [2, 4096, 8192], P(None, 'dp'), may hold values from -100 to 100, as said below
- weight: bfloat16 [8192, 4096], P('dp', 'mp'), may hold values from -0.0625 to 0.0625
Outputs:
- weight_gradient: float32 [8192, 4096], P('dp', 'mp')
The draws below stay inside these ranges and needn't reach their ends.
Inputs may be any that keep to these rules, and one draw needn't show every extreme that they name: `inputs`: bfloat16 activations of two views of the same images.
All inputs are finite; a program needn't handle non-finite values.
Results may differ from the reference program's by a relative error of at most 0.0075.
Values may be sent and summed in bfloat16 or wider, within the bound.
No kernel may reach another device: no remote copies, remote signals or barrier semaphores. Data moves between devices by JAX's collectives and lax.ppermute only.
A program may use at most 64 MiB of HBM per device.

```python
import jax
import jax.numpy as jnp
from jax import lax

D = 8192
E = 4096
BATCH = 4096
N_DP = 32
N_MP = 16


def draw_inputs(key, part):
    key = jax.random.fold_in(key, 11)
    subkeys = jax.random.split(key, 6)
    position = jnp.arange(BATCH, dtype=jnp.float32) / max(BATCH - 1, 1)
    row_scale = 10.0 ** (0.48 * position + 0.52 * jax.random.uniform(subkeys[0], (BATCH,), jnp.float32))
    col_scale = 10.0 ** jax.random.uniform(subkeys[1], (D,), jnp.float32)
    magnitude = 0.1 * row_scale[:, None] * col_scale[None, :]
    common = jnp.clip(jax.random.normal(subkeys[2], (BATCH, D), jnp.float32), -4.0, 4.0)
    jitter = jnp.clip(jax.random.normal(subkeys[3], (BATCH, D), jnp.float32), -4.0, 4.0)
    ramp = 0.5 + position
    column_offset = jnp.clip(jax.random.normal(subkeys[5], (D,), jnp.float32), -2.5, 2.5)
    shifted = ramp[:, None] * (column_offset * col_scale)[None, :]
    first = common * magnitude + shifted
    second = (common + 0.5 * jitter) * magnitude + shifted
    return jnp.clip(jnp.stack([first, second]), -100.0, 100.0).astype(jnp.bfloat16)


def steps_of(own_key, dims, shards, low, largest):
    level, own = 1.0, jax.random.fold_in(own_key, 6)
    for dim, shards_of in shards:
        draws = jnp.exp(jax.random.uniform(jax.random.fold_in(own, dim), (shards_of,), jnp.float32, low / len(shards), largest / len(shards)))
        level = level * jnp.repeat(draws, dims[dim] // shards_of).reshape([-1 if axis == dim else 1 for axis in range(len(dims))])
    return level


def centred(own_key, extent, scale, reach, cuts=(), kind=jnp.bfloat16):
    entries = scale * jax.random.normal(own_key, extent, jnp.float32)
    if cuts:
        entries = entries * steps_of(own_key, extent, cuts, -0.22, 0.18)
    return jnp.clip(entries, -reach, reach).astype(kind)


def setup_inputs(seed: int = 0) -> dict:
    keys = jax.random.split(jax.random.key(seed), 3)
    inputs = draw_inputs(jax.random.fold_in(keys[2], 71), 0)
    weight = centred(keys[1], (D, E), D ** -0.5, 0.0625, ((0, 32), (1, 16)))
    return dict(inputs=inputs, weight=weight)


epsilon = 1e-05
redundancy_weight = 0.0051
loss_scale = 512.0

def reference(inputs, weight):
    projected = jnp.stack([jnp.dot(inputs[0], weight, preferred_element_type=jnp.float32), jnp.dot(inputs[1], weight, preferred_element_type=jnp.float32)])
    average = lax.optimization_barrier(jnp.sum(projected, axis=1, keepdims=True)) / BATCH
    centered = projected - average
    variance = lax.optimization_barrier(jnp.sum(centered * centered, axis=1, keepdims=True)) / BATCH
    inverse = lax.rsqrt(variance + epsilon)
    normed = (centered * inverse).astype(jnp.bfloat16)
    correlation = jnp.dot(normed[0].T, normed[1], preferred_element_type=jnp.float32) / BATCH
    identity_matrix = jnp.eye(E, dtype=jnp.float32)
    grad_corr = (loss_scale * (2.0 * redundancy_weight * correlation + identity_matrix * (2.0 * (correlation - 1.0) - 2.0 * redundancy_weight * correlation))).astype(jnp.bfloat16)
    local_feat = E // N_MP
    block_feat = E // (N_MP * N_DP)
    group_width = N_MP * block_feat
    second_view = normed[1].reshape(BATCH, N_MP, N_DP, block_feat).transpose(2, 0, 1, 3).reshape(N_DP, BATCH, group_width)
    gradient_columns = grad_corr.reshape(E, N_MP, N_DP, block_feat).transpose(2, 0, 1, 3).reshape(N_DP, E, group_width)

    def add_first(carry, pair):
        term = jnp.dot(pair[0], pair[1].T, preferred_element_type=jnp.float32) / BATCH
        return (carry + term.astype(jnp.bfloat16).astype(jnp.float32), None)
    grad_first, _ = lax.scan(add_first, jnp.zeros((BATCH, E), jnp.float32), (second_view, gradient_columns))
    first_view = normed[0].reshape(BATCH, N_MP, local_feat).transpose(1, 0, 2)
    grad_rows = grad_corr.reshape(N_MP, local_feat, E)

    def add_second(carry, pair):
        term = jnp.dot(pair[0], pair[1], preferred_element_type=jnp.float32) / BATCH
        return (carry + term.astype(jnp.bfloat16).astype(jnp.float32), None)
    grad_second, _ = lax.scan(add_second, jnp.zeros((BATCH, E), jnp.float32), (first_view, grad_rows))
    grads = jnp.stack([grad_first, grad_second])
    normalized_wide_rows = normed.astype(jnp.float32)
    grad_mean = lax.optimization_barrier(jnp.sum(grads, axis=1, keepdims=True)) / BATCH
    cross_mean = lax.optimization_barrier(jnp.sum(grads * normalized_wide_rows, axis=1, keepdims=True)) / BATCH
    grad_proj = ((grads - grad_mean - normalized_wide_rows * cross_mean) * inverse).astype(jnp.bfloat16)
    return jnp.dot(inputs[0].T, grad_proj[0], preferred_element_type=jnp.float32) + jnp.dot(inputs[1].T, grad_proj[1], preferred_element_type=jnp.float32)
```

```python
import jax
import jax.numpy as jnp
from jax import lax
from jax.sharding import PartitionSpec as P

epsilon = 1e-05
redundancy_weight = 0.0051
loss_scale = 512.0


def spread(block, axis, count):
    copies = jnp.broadcast_to(block[None], (count,) + block.shape)
    return lax.all_to_all(copies, axis, split_axis=0, concat_axis=0)


def per_device(inputs, weight):
    views, images, width = inputs.shape
    dp = lax.axis_size("dp")
    mp = lax.axis_size("mp")
    total = images * dp
    data_index = lax.axis_index("dp")
    feat = weight.shape[1]
    block = feat // dp
    rows = width // dp

    pieces = inputs.reshape(views, images, dp, rows).transpose(2, 0, 1, 3)
    columns = lax.all_to_all(pieces, "dp", split_axis=0, concat_axis=0)

    full_weight = lax.all_gather(weight, "dp", axis=0, tiled=True)
    projected = lax.dot_general(
        full_weight,
        inputs.reshape(views * images, width),
        (((0,), (1,)), ((), ())),
        preferred_element_type=jnp.float32,
    )
    own = lax.all_to_all(
        projected.reshape(dp, block, views * images), "dp", split_axis=0, concat_axis=0
    ).reshape(dp, block, views, images)
    average = jnp.sum(own, axis=(0, 3), keepdims=True) / total
    centered = own - average
    variance = jnp.sum(centered * centered, axis=(0, 3), keepdims=True) / total
    inverse = lax.rsqrt(variance + epsilon)
    normed = (centered * inverse).astype(jnp.bfloat16)
    first = normed[:, :, 0].transpose(1, 0, 2).reshape(block, total)
    second = normed[:, :, 1].transpose(1, 0, 2).reshape(block, total)

    rows_a = lax.all_gather(first, "dp", axis=0, tiled=True)
    columns_b = spread(second, "mp", mp).reshape(mp * block, total)
    correlation = (
        lax.dot_general(rows_a, columns_b, (((1,), (1,)), ((), ())), preferred_element_type=jnp.float32)
        / total
    )
    row_ids = lax.broadcasted_iota(jnp.int32, (feat, 1), 0)
    column = lax.broadcasted_iota(jnp.int32, (1, mp * block), 1)
    own_columns = column // block == lax.axis_index("mp")
    diagonal = (own_columns & (row_ids == data_index * block + column % block)).astype(jnp.float32)
    grad_corr = (
        loss_scale
        * (
            2.0 * redundancy_weight * correlation
            + diagonal * (2.0 * (correlation - 1.0) - 2.0 * redundancy_weight * correlation)
        )
    ).astype(jnp.bfloat16)
    terms_b = (
        lax.dot_general(grad_corr, rows_a, (((0,), (0,)), ((), ())), preferred_element_type=jnp.float32)
        / total
    ).astype(jnp.bfloat16)
    terms_a = (
        lax.dot_general(grad_corr, columns_b, (((1,), (0,)), ((), ())), preferred_element_type=jnp.float32)
        / total
    ).astype(jnp.bfloat16)
    terms_a = lax.all_to_all(terms_a.reshape(dp, block, total), "dp", split_axis=0, concat_axis=0)
    terms_b = lax.all_to_all(terms_b.reshape(mp, block, total), "mp", split_axis=0, concat_axis=0)
    grads = jnp.stack(
        [
            jnp.sum(terms.astype(jnp.float32), axis=0).reshape(block, dp, images)
            for terms in (terms_a, terms_b)
        ],
        axis=2,
    )
    wide = normed.transpose(1, 0, 2, 3).astype(jnp.float32)
    grad_mean = jnp.sum(grads, axis=(1, 3), keepdims=True) / total
    cross_mean = jnp.sum(grads * wide, axis=(1, 3), keepdims=True) / total
    grad_proj = (
        (grads - grad_mean - wide * cross_mean) * inverse.transpose(1, 0, 2, 3)
    ).astype(jnp.bfloat16)
    gathered = lax.all_gather(
        grad_proj.reshape(block, dp * views * images), "dp", axis=0, tiled=True
    )
    return lax.dot_general(
        columns.reshape(dp * views * images, rows),
        gathered,
        (((0,), (1,)), ((), ())),
        preferred_element_type=jnp.float32,
    )


def solution(mesh):
    placed = (P(None, "dp", None), P("dp", "mp"))
    return jax.shard_map(
        per_device, mesh=mesh, in_specs=placed, out_specs=P("dp", "mp"), check_vma=False
    )
```

```python
import jax
import jax.numpy as jnp
from jax import lax
from jax.experimental import pallas as pl
from jax.experimental.pallas import tpu as pltpu
from jax.sharding import PartitionSpec as P

epsilon = 1e-05
redundancy_weight = 0.0051
loss_scale = 512.0
DP = 32
MP = 16
Y = 8


def swap(array, step):
    return lax.ppermute(array, "dp", [(i, i ^ step) for i in range(DP)])


def gather_dp(block):
    along_z = jnp.stack([block] + [swap(block, 2 * k) for k in (1, 2, 3)])
    along_x = jnp.stack([along_z] + [swap(along_z, 8 * k) for k in (1, 2, 3)])
    return along_x, swap(along_x, 1)


def add_dp(own, other):
    both = (own + swap(other, 1).astype(jnp.float32)).astype(jnp.bfloat16)
    parts = [both[0]] + [swap(both[k], 8 * k) for k in (1, 2, 3)]
    along_x = sum(part.astype(jnp.float32) for part in parts).astype(jnp.bfloat16)
    parts = [along_x[0]] + [swap(along_x[k], 2 * k) for k in (1, 2, 3)]
    return sum(part.astype(jnp.float32) for part in parts)


def copy_kernel(order_ref, source_ref, out_ref):
    out_ref[...] = source_ref[...]


def take_columns(array, order, width):
    rows, columns = array.shape
    return pl.pallas_call(
        copy_kernel,
        grid_spec=pltpu.PrefetchScalarGridSpec(
            num_scalar_prefetch=1,
            grid=(columns // width,),
            in_specs=[pl.BlockSpec((rows, width), lambda k, order: (0, order[k]))],
            out_specs=pl.BlockSpec((rows, width), lambda k, order: (0, k)),
        ),
        out_shape=jax.ShapeDtypeStruct(array.shape, array.dtype),
    )(order, array)


def weight_kernel(order_ref, own_ref, other_ref, columns_ref, out_ref, total_ref, placed_ref):
    step = pl.program_id(0)
    half = own_ref.shape[0]

    @pl.when(step == 0)
    def _():
        total_ref[...] = jnp.zeros_like(total_ref)

    total_ref[:half] += jnp.dot(own_ref[...], columns_ref[...], preferred_element_type=jnp.float32)
    total_ref[half:] += jnp.dot(other_ref[...], columns_ref[...], preferred_element_type=jnp.float32)

    @pl.when(step == pl.num_programs(0) - 1)
    def _():
        for block in range(DP):
            start = pl.multiple_of(order_ref[block] * 8, 8)
            placed_ref[block * 8 : block * 8 + 8] = total_ref[pl.ds(start, 8)]
        out_ref[...] = placed_ref[...].T


def weight_gradient(order, own, other, columns):
    depth, rows = columns.shape
    half = own.shape[0]
    tile = 1024
    return pl.pallas_call(
        weight_kernel,
        grid_spec=pltpu.PrefetchScalarGridSpec(
            num_scalar_prefetch=1,
            grid=(depth // tile,),
            in_specs=[
                pl.BlockSpec((half, tile), lambda k, order: (0, k)),
                pl.BlockSpec((half, tile), lambda k, order: (0, k)),
                pl.BlockSpec((tile, rows), lambda k, order: (k, 0)),
            ],
            out_specs=pl.BlockSpec((rows, 2 * half), lambda k, order: (0, 0)),
            scratch_shapes=[
                pltpu.VMEM((2 * half, rows), jnp.float32),
                pltpu.VMEM((2 * half, rows), jnp.float32),
            ],
        ),
        out_shape=jax.ShapeDtypeStruct((rows, 2 * half), jnp.float32),
    )(order, own, other, columns)


def per_device(inputs, weight):
    views, images, width = inputs.shape
    total = images * DP
    data_index = lax.axis_index("dp")
    model_index = lax.axis_index("mp")
    feat = weight.shape[1]
    block = feat // DP
    rows = width // DP
    flat = inputs.reshape(views * images, width)

    place = jnp.arange(DP, dtype=jnp.int32)
    distance = (place >> 4) | ((place >> 2) & 3) << 3 | (place & 3) << 1
    order = data_index ^ distance
    relative = place ^ data_index
    position = (relative & 1) << 4 | (relative >> 3) << 2 | ((relative >> 1) & 3)

    share = views * images // Y
    mine = lax.dynamic_slice_in_dim(flat, lax.rem(model_index, Y) * share, share, axis=0)
    pieces = mine.reshape(share, DP, rows).transpose(1, 0, 2)
    slices = lax.all_to_all(pieces, "dp", split_axis=0, concat_axis=0)

    weight_own, weight_other = gather_dp(weight)
    ordered = take_columns(flat, order, rows)
    projected = lax.dot_general(
        weight_own.reshape(width // 2, feat),
        ordered[:, : width // 2],
        (((0,), (1,)), ((), ())),
        preferred_element_type=jnp.float32,
    ) + lax.dot_general(
        weight_other.reshape(width // 2, feat),
        ordered[:, width // 2 :],
        (((0,), (1,)), ((), ())),
        preferred_element_type=jnp.float32,
    )
    projected, slices = lax.optimization_barrier((projected, slices))
    groups = [list(range(Y)), list(range(Y, MP))]
    columns = lax.all_gather(slices, "mp", axis=0, axis_index_groups=groups)
    columns = columns.reshape(views, Y // views, DP, share, rows).transpose(0, 2, 1, 3, 4)
    columns = columns.reshape(views * total, rows)

    own = lax.all_to_all(
        projected.reshape(DP, block, views * images), "dp", split_axis=0, concat_axis=0
    ).reshape(DP, block, views, images)
    average = jnp.sum(own, axis=(0, 3), keepdims=True) / total
    centered = own - average
    variance = jnp.sum(centered * centered, axis=(0, 3), keepdims=True) / total
    inverse = lax.rsqrt(variance + epsilon)
    normed = (centered * inverse).astype(jnp.bfloat16).transpose(2, 1, 0, 3).reshape(views, block, total)
    inverse = inverse.reshape(block, views).T[:, :, None]

    copies = jnp.broadcast_to(normed[1][None], (MP, block, total))
    columns_b = lax.all_to_all(copies, "mp", split_axis=0, concat_axis=0).reshape(MP * block, total)
    rows_own, rows_other = (part.reshape(feat // 2, total) for part in gather_dp(normed[0]))

    def gradient_of(rows_a, with_diagonal):
        correlation = (
            lax.dot_general(rows_a, columns_b, (((1,), (1,)), ((), ())), preferred_element_type=jnp.float32)
            / total
        )
        inner = 2.0 * redundancy_weight * correlation
        if with_diagonal:
            row = lax.broadcasted_iota(jnp.int32, correlation.shape, 0)
            column = lax.broadcasted_iota(jnp.int32, correlation.shape, 1)
            diagonal = (row < block) & (column == model_index * block + row)
            inner = inner + diagonal.astype(jnp.float32) * (2.0 * (correlation - 1.0) - inner)
        return (loss_scale * inner).astype(jnp.bfloat16)

    corr_own = gradient_of(rows_own, True)
    corr_other = gradient_of(rows_other, False)
    corr_own, columns = lax.optimization_barrier((corr_own, columns))

    def times(lhs, rhs, dims):
        return lax.dot_general(lhs, rhs, (dims, ((), ())), preferred_element_type=jnp.float32) / total

    terms_other = times(corr_other, columns_b, ((1,), (0,))).astype(jnp.bfloat16)
    terms_b = (
        times(corr_own, rows_own, ((0,), (0,))) + times(corr_other, rows_other, ((0,), (0,)))
    ).astype(jnp.bfloat16)
    terms_own = times(corr_own, columns_b, ((1,), (0,)))
    terms_b = lax.all_to_all(terms_b.reshape(MP, block, total), "mp", split_axis=0, concat_axis=0)
    shape = (4, 4, block, total)
    grads = jnp.stack(
        [
            add_dp(terms_own.reshape(shape), terms_other.reshape(shape)),
            jnp.sum(terms_b.astype(jnp.float32), axis=0),
        ]
    )
    wide = normed.astype(jnp.float32)
    grad_mean = jnp.sum(grads, axis=2, keepdims=True) / total
    cross_mean = jnp.sum(grads * wide, axis=2, keepdims=True) / total
    grad_proj = ((grads - grad_mean - wide * cross_mean) * inverse).astype(jnp.bfloat16)
    grad_proj = grad_proj.transpose(1, 0, 2).reshape(block, views * total)
    grad_own, grad_other = gather_dp(grad_proj)
    return weight_gradient(
        position,
        grad_own.reshape(feat // 2, views * total),
        grad_other.reshape(feat // 2, views * total),
        columns,
    )


def solution(mesh):
    placed = (P(None, "dp", None), P("dp", "mp"))
    return jax.shard_map(
        per_device, mesh=mesh, in_specs=placed, out_specs=P("dp", "mp"), check_vma=False
    )
```

```python
import functools

import jax
import jax.numpy as jnp
from jax import lax
from jax.experimental import pallas as pl
from jax.experimental.pallas import tpu as pltpu
from jax.sharding import PartitionSpec as P

epsilon = 1e-05
redundancy_weight = 0.0051
loss_scale = 512.0
DP = 32
MP = 16
Y = 8


def swap(array, step):
    return lax.ppermute(array, "dp", [(i, i ^ step) for i in range(DP)])


def gather_dp(block):
    along_z = jnp.stack([block] + [swap(block, 2 * k) for k in (1, 2, 3)])
    along_x = jnp.stack([along_z] + [swap(along_z, 8 * k) for k in (1, 2, 3)])
    return along_x, swap(along_x, 1)


def add_dp(own, other):
    both = (own + swap(other, 1).astype(jnp.float32)).astype(jnp.bfloat16)
    parts = [both[0]] + [swap(both[k], 8 * k) for k in (1, 2, 3)]
    along_x = sum(part.astype(jnp.float32) for part in parts).astype(jnp.bfloat16)
    parts = [along_x[0]] + [swap(along_x[k], 2 * k) for k in (1, 2, 3)]
    return sum(part.astype(jnp.float32) for part in parts)


def project_kernel(last, order_ref, inputs_ref, weight_ref, *refs):
    out_ref = refs[-1]
    blocks, depth, _ = weight_ref.shape
    result = refs[0][...] if last else None
    for k in range(blocks):
        columns = pl.ds(pl.multiple_of(order_ref[k] * depth, depth), depth)
        part = jnp.dot(inputs_ref[:, columns], weight_ref[k], preferred_element_type=jnp.float32)
        result = part if result is None else result + part
    out_ref[...] = result.T if last else result


def project(order, inputs, weight, before=None):
    rows, feat = inputs.shape[0], weight.shape[2]
    operands = (inputs, weight) if before is None else (inputs, weight, before)
    return pl.pallas_call(
        functools.partial(project_kernel, before is not None),
        in_specs=[pl.BlockSpec(memory_space=pltpu.SMEM)]
        + [pl.BlockSpec(memory_space=pltpu.VMEM)] * len(operands),
        out_specs=pl.BlockSpec(memory_space=pltpu.VMEM),
        out_shape=jax.ShapeDtypeStruct((rows, feat) if before is None else (feat, rows), jnp.float32),
        compiler_params=pltpu.CompilerParams(vmem_limit_bytes=32 * 1024 * 1024),
        cost_estimate=pl.CostEstimate(
            flops=2 * rows * feat * weight.shape[0] * weight.shape[1],
            bytes_accessed=6 * 1024 * 1024,
            transcendentals=0,
        ),
    )(order, *operands)


def weight_kernel(last, grad_ref, columns_ref, *refs):
    total_ref = refs[-1]
    step = pl.program_id(0) * pl.num_programs(1) + pl.program_id(1)

    @pl.when(step == 0)
    def _():
        total_ref[...] = jnp.zeros_like(total_ref)

    quarters, devices, share, rows = columns_ref.shape
    pieces = [columns_ref[:, d].reshape(quarters * share, rows) for d in range(devices)]
    columns = jnp.concatenate(pieces, axis=0)
    total_ref[...] += jnp.dot(grad_ref[...], columns, preferred_element_type=jnp.float32)

    if last:
        position_ref, own_ref, out_ref, placed_ref = refs[:4]
        half = own_ref.shape[0]

        @pl.when(step == pl.num_programs(0) * pl.num_programs(1) - 1)
        def _():
            placed_ref[:half] = own_ref[...]
            placed_ref[half:] = total_ref[...]
            blocks = [
                placed_ref[pl.ds(pl.multiple_of(position_ref[block] * 8, 8), 8)] for block in range(DP)
            ]
            out_ref[...] = jnp.concatenate(blocks, axis=0).T


def weight_half(grad, columns, position=None, own=None):
    half, depth = grad.shape
    slices, devices, share, rows = columns.shape
    quarters, group = slices // 2, 8
    last = own is not None
    in_specs = [
        pl.BlockSpec((half, group * quarters * share), lambda v, d: (0, v * (devices // group) + d)),
        pl.BlockSpec((quarters, group, share, rows), lambda v, d: (v, d, 0, 0)),
    ]
    scratch = [pltpu.VMEM((half, rows), jnp.float32)]
    if last:
        in_specs += [
            pl.BlockSpec(memory_space=pltpu.SMEM),
            pl.BlockSpec((half, rows), lambda v, d: (0, 0)),
        ]
        scratch = [pltpu.VMEM((2 * half, rows), jnp.float32)] + scratch
    return pl.pallas_call(
        functools.partial(weight_kernel, last),
        grid=(2, devices // group),
        in_specs=in_specs,
        out_specs=pl.BlockSpec((rows, 2 * half) if last else (half, rows), lambda v, d: (0, 0)),
        out_shape=jax.ShapeDtypeStruct((rows, 2 * half) if last else (half, rows), jnp.float32),
        scratch_shapes=scratch if last else [],
        compiler_params=pltpu.CompilerParams(vmem_limit_bytes=32 * 1024 * 1024),
        cost_estimate=pl.CostEstimate(
            flops=2 * half * depth * rows, bytes_accessed=6 * 1024 * 1024, transcendentals=0
        ),
    )(grad, columns, *((position, own) if last else ()))


def per_device(inputs, weight):
    views, images, width = inputs.shape
    total = images * DP
    data_index = lax.axis_index("dp")
    model_index = lax.axis_index("mp")
    feat = weight.shape[1]
    block = feat // DP
    rows = width // DP
    flat = inputs.reshape(views * images, width)

    place = jnp.arange(DP, dtype=jnp.int32)
    distance = (place >> 4) | ((place >> 2) & 3) << 3 | (place & 3) << 1
    order = data_index ^ distance
    relative = place ^ data_index
    position = (relative & 1) << 4 | (relative >> 3) << 2 | ((relative >> 1) & 3)

    share = views * images // Y
    mine = lax.dynamic_slice_in_dim(flat, lax.rem(model_index, Y) * share, share, axis=0)
    pieces = mine.reshape(share, DP, rows).transpose(1, 0, 2)
    slices = lax.all_to_all(pieces, "dp", split_axis=0, concat_axis=0)

    along_z = jnp.stack([weight] + [swap(weight, 2 * k) for k in (1, 2, 3)])
    weight_own = jnp.stack([along_z] + [swap(along_z, 8 * k) for k in (1, 2, 3)])
    weight_own, slices = lax.optimization_barrier((weight_own, slices))
    weight_other = swap(weight_own, 1)
    half = (DP // 2, rows, feat)
    projected = project(order[: DP // 2], flat, weight_own.reshape(half))
    projected = project(order[DP // 2 :], flat, weight_other.reshape(half), projected)

    own = lax.all_to_all(
        projected.reshape(DP, block, views * images), "dp", split_axis=0, concat_axis=0
    ).reshape(DP, block, views, images)
    average = jnp.sum(own, axis=(0, 3), keepdims=True) / total
    centered = own - average
    variance = jnp.sum(centered * centered, axis=(0, 3), keepdims=True) / total
    inverse = lax.rsqrt(variance + epsilon)
    normed = (centered * inverse).astype(jnp.bfloat16).transpose(2, 1, 0, 3).reshape(views, block, total)
    inverse = inverse.reshape(block, views).T[:, :, None]

    copies = jnp.broadcast_to(normed[1][None], (MP, block, total))
    columns_b = lax.all_to_all(copies, "mp", split_axis=0, concat_axis=0).reshape(MP * block, total)
    rows_own, rows_other = (part.reshape(feat // 2, total) for part in gather_dp(normed[0]))

    def gradient_of(rows_a, with_diagonal):
        correlation = (
            lax.dot_general(rows_a, columns_b, (((1,), (1,)), ((), ())), preferred_element_type=jnp.float32)
            / total
        )
        inner = 2.0 * redundancy_weight * correlation
        if with_diagonal:
            row = lax.broadcasted_iota(jnp.int32, correlation.shape, 0)
            column = lax.broadcasted_iota(jnp.int32, correlation.shape, 1)
            diagonal = (row < block) & (column == model_index * block + row)
            inner = inner + diagonal.astype(jnp.float32) * (2.0 * (correlation - 1.0) - inner)
        return (loss_scale * inner).astype(jnp.bfloat16)

    corr_own = gradient_of(rows_own, True)
    corr_other = gradient_of(rows_other, False)

    def times(lhs, rhs, dims):
        return lax.dot_general(lhs, rhs, (dims, ((), ())), preferred_element_type=jnp.float32) / total

    terms_other = times(corr_other, columns_b, ((1,), (0,))).astype(jnp.bfloat16)
    terms_b = (
        times(corr_own, rows_own, ((0,), (0,))) + times(corr_other, rows_other, ((0,), (0,)))
    ).astype(jnp.bfloat16)
    terms_own = times(corr_own, columns_b, ((1,), (0,)))
    terms_b = lax.all_to_all(terms_b.reshape(MP, block, total), "mp", split_axis=0, concat_axis=0)
    terms_b, slices = lax.optimization_barrier((terms_b, slices))
    groups = [list(range(Y)), list(range(Y, MP))]
    columns = lax.all_gather(slices, "mp", axis=0, axis_index_groups=groups)
    shape = (4, 4, block, total)
    grads = jnp.stack(
        [
            add_dp(terms_own.reshape(shape), terms_other.reshape(shape)),
            jnp.sum(terms_b.astype(jnp.float32), axis=0),
        ]
    )
    wide = normed.astype(jnp.float32)
    grad_mean = jnp.sum(grads, axis=2, keepdims=True) / total
    cross_mean = jnp.sum(grads * wide, axis=2, keepdims=True) / total
    grad_proj = ((grads - grad_mean - wide * cross_mean) * inverse).astype(jnp.bfloat16)
    grad_proj = grad_proj.transpose(1, 0, 2).reshape(block, views * total)
    grad_own, grad_other = gather_dp(grad_proj)
    part = weight_half(grad_own.reshape(feat // 2, views * total), columns)
    return weight_half(grad_other.reshape(feat // 2, views * total), columns, position, part)


def solution(mesh):
    placed = (P(None, "dp", None), P("dp", "mp"))
    return jax.shard_map(
        per_device, mesh=mesh, in_specs=placed, out_specs=P("dp", "mp"), check_vma=False
    )
```

```python
import functools

import jax
import jax.numpy as jnp
from jax import lax
from jax.experimental import pallas as pl
from jax.experimental.pallas import tpu as pltpu
from jax.sharding import PartitionSpec as P

epsilon = 1e-05
redundancy_weight = 0.0051
loss_scale = 512.0
DP = 32
MP = 16
Y = 8
GROUPS = [list(range(Y)), list(range(Y, MP))]


def swap(array, step):
    return lax.ppermute(array, "dp", [(i, i ^ step) for i in range(DP)])


def partner(array):
    return lax.ppermute(array, "mp", [(i, i ^ Y) for i in range(MP)])


def gather_dp(block):
    along_z = jnp.stack([block] + [swap(block, 2 * k) for k in (1, 2, 3)])
    along_x = jnp.stack([along_z] + [swap(along_z, 8 * k) for k in (1, 2, 3)])
    return along_x, swap(along_x, 1)


def add_dp(own, other, later):
    both = (own + swap(other, 1).astype(jnp.float32)).astype(jnp.bfloat16)
    parts = [both[0]] + [swap(both[k], 8 * k) for k in (1, 2, 3)]
    along_x = sum(part.astype(jnp.float32) for part in parts).astype(jnp.bfloat16)
    along_x, later = lax.optimization_barrier((along_x, later))
    parts = [along_x[0]] + [swap(along_x[k], 2 * k) for k in (1, 2, 3)]
    return sum(part.astype(jnp.float32) for part in parts), later


def project_kernel(last, order_ref, inputs_ref, weight_ref, *refs):
    out_ref = refs[-1]
    blocks, depth, _ = weight_ref.shape
    result = refs[0][...] if last else None
    for k in range(blocks):
        columns = pl.ds(pl.multiple_of(order_ref[k] * depth, depth), depth)
        part = jnp.dot(inputs_ref[:, columns], weight_ref[k], preferred_element_type=jnp.float32)
        result = part if result is None else result + part
    out_ref[...] = result.T if last else result


def project(order, inputs, weight, before=None):
    rows, feat = inputs.shape[0], weight.shape[2]
    operands = (inputs, weight) if before is None else (inputs, weight, before)
    return pl.pallas_call(
        functools.partial(project_kernel, before is not None),
        in_specs=[pl.BlockSpec(memory_space=pltpu.SMEM)]
        + [pl.BlockSpec(memory_space=pltpu.VMEM)] * len(operands),
        out_specs=pl.BlockSpec(memory_space=pltpu.VMEM),
        out_shape=jax.ShapeDtypeStruct((rows, feat) if before is None else (feat, rows), jnp.float32),
        compiler_params=pltpu.CompilerParams(vmem_limit_bytes=32 * 1024 * 1024),
        cost_estimate=pl.CostEstimate(
            flops=2 * rows * feat * weight.shape[0] * weight.shape[1],
            bytes_accessed=6 * 1024 * 1024,
            transcendentals=0,
        ),
    )(order, *operands)


def weight_kernel(last, grad_ref, columns_ref, *refs):
    total_ref = refs[-1]
    step = pl.program_id(0) * pl.num_programs(1) + pl.program_id(1)

    @pl.when(step == 0)
    def _():
        total_ref[...] = jnp.zeros_like(total_ref)

    quarters, devices, share, rows = columns_ref.shape
    pieces = [columns_ref[:, d].reshape(quarters * share, rows) for d in range(devices)]
    columns = jnp.concatenate(pieces, axis=0)
    total_ref[...] += jnp.dot(grad_ref[...], columns, preferred_element_type=jnp.float32)

    if last:
        position_ref, own_ref, out_ref, placed_ref = refs[:4]
        half = own_ref.shape[0]

        @pl.when(step == pl.num_programs(0) * pl.num_programs(1) - 1)
        def _():
            placed_ref[:half] = own_ref[...]
            placed_ref[half:] = total_ref[...]
            blocks = [
                placed_ref[pl.ds(pl.multiple_of(position_ref[block] * 8, 8), 8)] for block in range(DP)
            ]
            out_ref[...] = jnp.concatenate(blocks, axis=0).T


def weight_half(grad, columns, position=None, own=None):
    half, depth = grad.shape
    slices, devices, share, rows = columns.shape
    quarters, group = slices // 2, 8
    last = own is not None
    in_specs = [
        pl.BlockSpec((half, group * quarters * share), lambda v, d: (0, v * (devices // group) + d)),
        pl.BlockSpec((quarters, group, share, rows), lambda v, d: (v, d, 0, 0)),
    ]
    scratch = [pltpu.VMEM((half, rows), jnp.float32)]
    if last:
        in_specs += [
            pl.BlockSpec(memory_space=pltpu.SMEM),
            pl.BlockSpec((half, rows), lambda v, d: (0, 0)),
        ]
        scratch = [pltpu.VMEM((2 * half, rows), jnp.float32)] + scratch
    return pl.pallas_call(
        functools.partial(weight_kernel, last),
        grid=(2, devices // group),
        in_specs=in_specs,
        out_specs=pl.BlockSpec((rows, 2 * half) if last else (half, rows), lambda v, d: (0, 0)),
        out_shape=jax.ShapeDtypeStruct((rows, 2 * half) if last else (half, rows), jnp.float32),
        scratch_shapes=scratch if last else [],
        compiler_params=pltpu.CompilerParams(vmem_limit_bytes=32 * 1024 * 1024),
        cost_estimate=pl.CostEstimate(
            flops=2 * half * depth * rows, bytes_accessed=6 * 1024 * 1024, transcendentals=0
        ),
    )(grad, columns, *((position, own) if last else ()))


def per_device(inputs, weight):
    views, images, width = inputs.shape
    total = images * DP
    data_index = lax.axis_index("dp")
    model_index = lax.axis_index("mp")
    feat = weight.shape[1]
    block = feat // DP
    rows = width // DP
    flat = inputs.reshape(views * images, width)

    place = jnp.arange(DP, dtype=jnp.int32)
    distance = (place >> 4) | ((place >> 2) & 3) << 3 | (place & 3) << 1
    order = data_index ^ distance
    relative = place ^ data_index
    position = (relative & 1) << 4 | (relative >> 3) << 2 | ((relative >> 1) & 3)

    share = views * images // Y
    mine = lax.dynamic_slice_in_dim(flat, lax.rem(model_index, Y) * share, share, axis=0)
    pieces = mine.reshape(share, DP, rows).transpose(1, 0, 2)
    along_z = jnp.stack([weight] + [swap(weight, 2 * k) for k in (1, 2, 3)])
    weight_own = jnp.stack([along_z] + [swap(along_z, 8 * k) for k in (1, 2, 3)])
    weight_other = swap(weight_own, 1)
    half = (DP // 2, rows, feat)
    projected = project(order[: DP // 2], flat, weight_own.reshape(half))
    projected = project(order[DP // 2 :], flat, weight_other.reshape(half), projected)

    own = lax.all_to_all(
        projected.reshape(DP, block, views * images), "dp", split_axis=0, concat_axis=0
    ).reshape(DP, block, views, images)
    average = jnp.sum(own, axis=(0, 3), keepdims=True) / total
    centered = own - average
    variance = jnp.sum(centered * centered, axis=(0, 3), keepdims=True) / total
    inverse = lax.rsqrt(variance + epsilon)
    normed = (centered * inverse).astype(jnp.bfloat16).transpose(2, 1, 0, 3).reshape(views, block, total)
    inverse = inverse.reshape(block, views).T[:, :, None]

    first, second, pieces = lax.optimization_barrier((normed[0], normed[1], pieces))
    slices = lax.all_to_all(pieces, "dp", split_axis=0, concat_axis=0)
    pair = jnp.stack([second, partner(second)])
    columns_b = lax.all_gather(pair, "mp", axis=0, axis_index_groups=GROUPS)
    columns_b = columns_b.reshape(MP * block, total)
    rows_own, rows_other = (part.reshape(feat // 2, total) for part in gather_dp(first))

    def gradient_of(rows_a, with_diagonal):
        correlation = (
            lax.dot_general(rows_a, columns_b, (((1,), (1,)), ((), ())), preferred_element_type=jnp.float32)
            / total
        )
        inner = 2.0 * redundancy_weight * correlation
        if with_diagonal:
            row = lax.broadcasted_iota(jnp.int32, correlation.shape, 0)
            column = lax.broadcasted_iota(jnp.int32, correlation.shape, 1)
            diagonal = (row < block) & (column == lax.rem(model_index, Y) * 2 * block + row)
            inner = inner + diagonal.astype(jnp.float32) * (2.0 * (correlation - 1.0) - inner)
        return (loss_scale * inner).astype(jnp.bfloat16)

    corr_own = gradient_of(rows_own, True)
    corr_other = gradient_of(rows_other, False)
    corr_other, slices = lax.optimization_barrier((corr_other, slices))

    def times(lhs, rhs, dims):
        return lax.dot_general(lhs, rhs, (dims, ((), ())), preferred_element_type=jnp.float32) / total

    terms_other = times(corr_other, columns_b, ((1,), (0,))).astype(jnp.bfloat16)
    terms_b = (
        times(corr_own, rows_own, ((0,), (0,))) + times(corr_other, rows_other, ((0,), (0,)))
    ).astype(jnp.bfloat16)
    terms_own = times(corr_own, columns_b, ((1,), (0,)))
    terms_b = lax.all_to_all(
        terms_b.reshape(Y, 2, block, total), "mp", split_axis=0, concat_axis=0, axis_index_groups=GROUPS
    )
    shape = (4, 4, block, total)
    grad_a, slices = add_dp(terms_own.reshape(shape), terms_other.reshape(shape), slices)
    columns = lax.all_gather(slices, "mp", axis=0, axis_index_groups=GROUPS)
    terms_b = jnp.sum(terms_b.astype(jnp.float32), axis=0)
    grad_b = terms_b[0] + partner(terms_b[1].astype(jnp.bfloat16)).astype(jnp.float32)
    grads = jnp.stack([grad_a, grad_b])
    wide = normed.astype(jnp.float32)
    grad_mean = jnp.sum(grads, axis=2, keepdims=True) / total
    cross_mean = jnp.sum(grads * wide, axis=2, keepdims=True) / total
    grad_proj = ((grads - grad_mean - wide * cross_mean) * inverse).astype(jnp.bfloat16)
    grad_proj = grad_proj.transpose(1, 0, 2).reshape(block, views * total)
    grad_own, grad_other = gather_dp(grad_proj)
    part = weight_half(grad_own.reshape(feat // 2, views * total), columns)
    return weight_half(grad_other.reshape(feat // 2, views * total), columns, position, part)


def solution(mesh):
    placed = (P(None, "dp", None), P("dp", "mp"))
    return jax.shard_map(
        per_device, mesh=mesh, in_specs=placed, out_specs=P("dp", "mp"), check_vma=False
    )
```

```python
import functools

import jax
import jax.numpy as jnp
from jax import lax
from jax.experimental import pallas as pl
from jax.experimental.pallas import tpu as pltpu
from jax.sharding import PartitionSpec as P

epsilon = 1e-05
redundancy_weight = 0.0051
loss_scale = 512.0
DP = 32
MP = 16
Y = 8
GROUPS = [list(range(Y)), list(range(Y, MP))]


def swap(array, step):
    return lax.ppermute(array, "dp", [(i, i ^ step) for i in range(DP)])


def partner(array):
    return lax.ppermute(array, "mp", [(i, i ^ Y) for i in range(MP)])


def gather_z(block):
    return jnp.stack([block] + [swap(block, 2 * k) for k in (1, 2, 3)])


def gather_x(block):
    return jnp.stack([block] + [swap(block, 8 * k) for k in (1, 2, 3)])


def add_dp(own, other, *later):
    both = (own + swap(other, 1).astype(jnp.float32)).astype(jnp.bfloat16)
    parts = [both[0]] + [swap(both[k], 8 * k) for k in (1, 2, 3)]
    along_x = sum(part.astype(jnp.float32) for part in parts).astype(jnp.bfloat16)
    along_x, *later = lax.optimization_barrier((along_x, *later))
    parts = [along_x[0]] + [swap(along_x[k], 2 * k) for k in (1, 2, 3)]
    return sum(part.astype(jnp.float32) for part in parts), *later


def project_kernel(last, order_ref, inputs_ref, weight_ref, *refs):
    out_ref = refs[-1]
    blocks, depth, _ = weight_ref.shape
    result = refs[0][...] if last else None
    for k in range(blocks):
        columns = pl.ds(pl.multiple_of(order_ref[k] * depth, depth), depth)
        part = jnp.dot(inputs_ref[:, columns], weight_ref[k], preferred_element_type=jnp.float32)
        result = part if result is None else result + part
    out_ref[...] = result.T if last else result


def project(order, inputs, weight, before=None):
    rows, feat = inputs.shape[0], weight.shape[2]
    operands = (inputs, weight) if before is None else (inputs, weight, before)
    return pl.pallas_call(
        functools.partial(project_kernel, before is not None),
        in_specs=[pl.BlockSpec(memory_space=pltpu.SMEM)]
        + [pl.BlockSpec(memory_space=pltpu.VMEM)] * len(operands),
        out_specs=pl.BlockSpec(memory_space=pltpu.VMEM),
        out_shape=jax.ShapeDtypeStruct((rows, feat) if before is None else (feat, rows), jnp.float32),
        compiler_params=pltpu.CompilerParams(vmem_limit_bytes=32 * 1024 * 1024),
        cost_estimate=pl.CostEstimate(
            flops=2 * rows * feat * weight.shape[0] * weight.shape[1],
            bytes_accessed=6 * 1024 * 1024,
            transcendentals=0,
        ),
    )(order, *operands)


def weight_kernel(last, grad_ref, columns_ref, *refs):
    total_ref = refs[-1]
    step = pl.program_id(0) * pl.num_programs(1) + pl.program_id(1)

    @pl.when(step == 0)
    def _():
        total_ref[...] = jnp.zeros_like(total_ref)

    quarters, devices, share, rows = columns_ref.shape
    pieces = [columns_ref[:, d].reshape(quarters * share, rows) for d in range(devices)]
    columns = jnp.concatenate(pieces, axis=0)
    total_ref[...] += jnp.dot(grad_ref[...], columns, preferred_element_type=jnp.float32)

    if last:
        position_ref, own_ref, out_ref, placed_ref = refs[:4]
        half = own_ref.shape[0]

        @pl.when(step == pl.num_programs(0) * pl.num_programs(1) - 1)
        def _():
            placed_ref[:half] = own_ref[...]
            placed_ref[half:] = total_ref[...]
            blocks = [
                placed_ref[pl.ds(pl.multiple_of(position_ref[block] * 8, 8), 8)] for block in range(DP)
            ]
            out_ref[...] = jnp.concatenate(blocks, axis=0).T


def weight_half(grad, columns, position=None, own=None):
    half, depth = grad.shape
    slices, devices, share, rows = columns.shape
    quarters, group = slices // 2, 8
    last = own is not None
    in_specs = [
        pl.BlockSpec((half, group * quarters * share), lambda v, d: (0, v * (devices // group) + d)),
        pl.BlockSpec((quarters, group, share, rows), lambda v, d: (v, d, 0, 0)),
    ]
    scratch = [pltpu.VMEM((half, rows), jnp.float32)]
    if last:
        in_specs += [
            pl.BlockSpec(memory_space=pltpu.SMEM),
            pl.BlockSpec((half, rows), lambda v, d: (0, 0)),
        ]
        scratch = [pltpu.VMEM((2 * half, rows), jnp.float32)] + scratch
    return pl.pallas_call(
        functools.partial(weight_kernel, last),
        grid=(2, devices // group),
        in_specs=in_specs,
        out_specs=pl.BlockSpec((rows, 2 * half) if last else (half, rows), lambda v, d: (0, 0)),
        out_shape=jax.ShapeDtypeStruct((rows, 2 * half) if last else (half, rows), jnp.float32),
        scratch_shapes=scratch if last else [],
        compiler_params=pltpu.CompilerParams(vmem_limit_bytes=32 * 1024 * 1024),
        cost_estimate=pl.CostEstimate(
            flops=2 * half * depth * rows, bytes_accessed=6 * 1024 * 1024, transcendentals=0
        ),
    )(grad, columns, *((position, own) if last else ()))


def per_device(inputs, weight):
    views, images, width = inputs.shape
    total = images * DP
    data_index = lax.axis_index("dp")
    model_index = lax.axis_index("mp")
    feat = weight.shape[1]
    block = feat // DP
    rows = width // DP
    flat = inputs.reshape(views * images, width)

    place = jnp.arange(DP, dtype=jnp.int32)
    distance = (place >> 4) | ((place >> 2) & 3) << 3 | (place & 3) << 1
    order = data_index ^ distance
    relative = place ^ data_index
    position = (relative & 1) << 4 | (relative >> 3) << 2 | ((relative >> 1) & 3)

    share = views * images // Y
    mine = lax.dynamic_slice_in_dim(flat, lax.rem(model_index, Y) * share, share, axis=0)
    pieces = mine.reshape(share, DP, rows).transpose(1, 0, 2)
    weight_own = gather_x(gather_z(weight))
    weight_other = swap(weight_own, 1)
    half = (DP // 2, rows, feat)
    projected = project(order[: DP // 2], flat, weight_own.reshape(half))
    projected = project(order[DP // 2 :], flat, weight_other.reshape(half), projected)

    own = lax.all_to_all(
        projected.reshape(DP, block, views * images), "dp", split_axis=0, concat_axis=0
    ).reshape(DP, block, views, images)
    average = jnp.sum(own, axis=(0, 3), keepdims=True) / total
    centered = own - average
    variance = jnp.sum(centered * centered, axis=(0, 3), keepdims=True) / total
    inverse = lax.rsqrt(variance + epsilon)
    normed = (centered * inverse).astype(jnp.bfloat16).transpose(2, 1, 0, 3).reshape(views, block, total)
    inverse = inverse.reshape(block, views).T[:, :, None]

    first, second, pieces = lax.optimization_barrier((normed[0], normed[1], pieces))
    pair = jnp.stack([second, partner(second)])
    first, pair = lax.optimization_barrier((first, pair))
    columns_b = lax.all_gather(pair, "mp", axis=0, axis_index_groups=GROUPS)
    columns_b = columns_b.reshape(MP * block, total)
    along_z, pieces = lax.optimization_barrier((gather_z(first), pieces))
    slices = lax.all_to_all(pieces, "dp", split_axis=0, concat_axis=0)
    rows_own, slices = lax.optimization_barrier((gather_x(along_z), slices))
    rows_other = swap(rows_own, 1).reshape(feat // 2, total)
    rows_own = rows_own.reshape(feat // 2, total)

    def gradient_of(rows_a, with_diagonal):
        correlation = (
            lax.dot_general(rows_a, columns_b, (((1,), (1,)), ((), ())), preferred_element_type=jnp.float32)
            / total
        )
        inner = 2.0 * redundancy_weight * correlation
        if with_diagonal:
            row = lax.broadcasted_iota(jnp.int32, correlation.shape, 0)
            column = lax.broadcasted_iota(jnp.int32, correlation.shape, 1)
            diagonal = (row < block) & (column == lax.rem(model_index, Y) * 2 * block + row)
            inner = inner + diagonal.astype(jnp.float32) * (2.0 * (correlation - 1.0) - inner)
        return (loss_scale * inner).astype(jnp.bfloat16)

    corr_own = gradient_of(rows_own, True)
    corr_other = gradient_of(rows_other, False)

    def times(lhs, rhs, dims):
        return lax.dot_general(lhs, rhs, (dims, ((), ())), preferred_element_type=jnp.float32) / total

    terms_other = times(corr_other, columns_b, ((1,), (0,))).astype(jnp.bfloat16)
    terms_b = (
        times(corr_own, rows_own, ((0,), (0,))) + times(corr_other, rows_other, ((0,), (0,)))
    ).astype(jnp.bfloat16)
    terms_own = times(corr_own, columns_b, ((1,), (0,)))
    terms_b = lax.all_to_all(
        terms_b.reshape(Y, 2, block, total), "mp", split_axis=0, concat_axis=0, axis_index_groups=GROUPS
    )
    shape = (4, 4, block, total)
    grad_a, terms_b, slices = add_dp(
        terms_own.reshape(shape), terms_other.reshape(shape), terms_b, slices
    )
    columns = lax.all_gather(slices, "mp", axis=0, axis_index_groups=GROUPS)
    terms_b = jnp.sum(terms_b.astype(jnp.float32), axis=0)
    grad_b = terms_b[0] + partner(terms_b[1].astype(jnp.bfloat16)).astype(jnp.float32)
    grads = jnp.stack([grad_a, grad_b])
    wide = normed.astype(jnp.float32)
    grad_mean = jnp.sum(grads, axis=2, keepdims=True) / total
    cross_mean = jnp.sum(grads * wide, axis=2, keepdims=True) / total
    grad_proj = ((grads - grad_mean - wide * cross_mean) * inverse).astype(jnp.bfloat16)
    grad_proj = grad_proj.transpose(1, 0, 2).reshape(block, views * total)
    grad_own = gather_x(gather_z(grad_proj))
    grad_other = swap(grad_own, 1)
    part = weight_half(grad_own.reshape(feat // 2, views * total), columns)
    return weight_half(grad_other.reshape(feat // 2, views * total), columns, position, part)


def solution(mesh):
    placed = (P(None, "dp", None), P("dp", "mp"))
    return jax.shard_map(
        per_device, mesh=mesh, in_specs=placed, out_specs=P("dp", "mp"), check_vma=False
    )
```

```python
import functools

import jax
import jax.numpy as jnp
from jax import lax
from jax.experimental import pallas as pl
from jax.experimental.pallas import tpu as pltpu
from jax.sharding import PartitionSpec as P

epsilon = 1e-05
redundancy_weight = 0.0051
loss_scale = 512.0
DP = 32
MP = 16
Y = 8
GROUPS = [list(range(Y)), list(range(Y, MP))]
ALONG_X = [(8,), (16,), (24,)]
ALONG_Z = [(2,), (4,), (6,)]
STRIDED_Z = [(4,), (0, 8), (4, 8)]


def swap(array, data, model=0):
    mask = data * MP + model
    return lax.ppermute(array, ("dp", "mp"), [(i, i ^ mask) for i in range(DP * MP)])


def partner(array):
    return swap(array, 2)


def gather(block, masks):
    return jnp.stack([block] + [swap(block, *mask) for mask in masks])


def add(blocks, masks):
    parts = [blocks[0]] + [swap(blocks[k + 1], *mask) for k, mask in enumerate(masks)]
    return sum(part.astype(jnp.float32) for part in parts)


def project_kernel(last, order_ref, inputs_ref, weight_ref, *refs):
    out_ref = refs[-1]
    blocks, depth, _ = weight_ref.shape
    result = refs[0][...] if last else None
    for k in range(blocks):
        columns = pl.ds(pl.multiple_of(order_ref[k] * depth, depth), depth)
        part = jnp.dot(inputs_ref[:, columns], weight_ref[k], preferred_element_type=jnp.float32)
        result = part if result is None else result + part
    out_ref[...] = result.T if last else result


def project(order, inputs, weight, before=None):
    rows, feat = inputs.shape[0], weight.shape[2]
    operands = (inputs, weight) if before is None else (inputs, weight, before)
    return pl.pallas_call(
        functools.partial(project_kernel, before is not None),
        in_specs=[pl.BlockSpec(memory_space=pltpu.SMEM)]
        + [pl.BlockSpec(memory_space=pltpu.VMEM)] * len(operands),
        out_specs=pl.BlockSpec(memory_space=pltpu.VMEM),
        out_shape=jax.ShapeDtypeStruct((rows, feat) if before is None else (feat, rows), jnp.float32),
        compiler_params=pltpu.CompilerParams(vmem_limit_bytes=32 * 1024 * 1024),
        cost_estimate=pl.CostEstimate(
            flops=2 * rows * feat * weight.shape[0] * weight.shape[1],
            bytes_accessed=6 * 1024 * 1024,
            transcendentals=0,
        ),
    )(order, *operands)


def weight_kernel(last, grad_ref, columns_ref, *refs):
    total_ref = refs[-1]
    step = pl.program_id(0) * pl.num_programs(1) + pl.program_id(1)

    @pl.when(step == 0)
    def _():
        total_ref[...] = jnp.zeros_like(total_ref)

    quarters, devices, share, rows = columns_ref.shape
    pieces = [columns_ref[:, d].reshape(quarters * share, rows) for d in range(devices)]
    columns = jnp.concatenate(pieces, axis=0)
    total_ref[...] += jnp.dot(grad_ref[...], columns, preferred_element_type=jnp.float32)

    if last:
        position_ref, own_ref, out_ref, placed_ref = refs[:4]
        half = own_ref.shape[0]

        @pl.when(step == pl.num_programs(0) * pl.num_programs(1) - 1)
        def _():
            placed_ref[:half] = own_ref[...]
            placed_ref[half:] = total_ref[...]
            blocks = [
                placed_ref[pl.ds(pl.multiple_of(position_ref[block] * 8, 8), 8)] for block in range(DP)
            ]
            out_ref[...] = jnp.concatenate(blocks, axis=0).T


def weight_half(grad, columns, position=None, own=None):
    half, depth = grad.shape
    slices, devices, share, rows = columns.shape
    quarters, group = slices // 2, 8
    last = own is not None
    in_specs = [
        pl.BlockSpec((half, group * quarters * share), lambda v, d: (0, v * (devices // group) + d)),
        pl.BlockSpec((quarters, group, share, rows), lambda v, d: (v, d, 0, 0)),
    ]
    scratch = [pltpu.VMEM((half, rows), jnp.float32)]
    if last:
        in_specs += [
            pl.BlockSpec(memory_space=pltpu.SMEM),
            pl.BlockSpec((half, rows), lambda v, d: (0, 0)),
        ]
        scratch = [pltpu.VMEM((2 * half, rows), jnp.float32)] + scratch
    return pl.pallas_call(
        functools.partial(weight_kernel, last),
        grid=(2, devices // group),
        in_specs=in_specs,
        out_specs=pl.BlockSpec((rows, 2 * half) if last else (half, rows), lambda v, d: (0, 0)),
        out_shape=jax.ShapeDtypeStruct((rows, 2 * half) if last else (half, rows), jnp.float32),
        scratch_shapes=scratch if last else [],
        compiler_params=pltpu.CompilerParams(vmem_limit_bytes=32 * 1024 * 1024),
        cost_estimate=pl.CostEstimate(
            flops=2 * half * depth * rows, bytes_accessed=6 * 1024 * 1024, transcendentals=0
        ),
    )(grad, columns, *((position, own) if last else ()))


def per_device(inputs, weight):
    views, images, width = inputs.shape
    total = images * DP
    data_index = lax.axis_index("dp")
    model_index = lax.axis_index("mp")
    feat = weight.shape[1]
    block = feat // DP
    rows = width // DP
    flat = inputs.reshape(views * images, width)

    place = jnp.arange(DP, dtype=jnp.int32)
    distance = (place >> 4) | ((place >> 2) & 3) << 3 | (place & 3) << 1
    order = data_index ^ distance
    relative = place ^ data_index
    position = (relative & 1) << 4 | (relative >> 3) << 2 | ((relative >> 1) & 3)

    share = views * images // Y
    mine = lax.dynamic_slice_in_dim(flat, lax.rem(model_index, Y) * share, share, axis=0)
    pieces = mine.reshape(share, DP, rows).transpose(1, 0, 2)
    weight_own = gather(gather(weight, ALONG_Z), ALONG_X)
    weight_other = swap(weight_own, 1)
    half = (DP // 2, rows, feat)
    projected = project(order[: DP // 2], flat, weight_own.reshape(half))
    projected = project(order[DP // 2 :], flat, weight_other.reshape(half), projected)

    own = lax.all_to_all(
        projected.reshape(DP, block, views * images), "dp", split_axis=0, concat_axis=0
    ).reshape(DP, block, views, images)
    average = jnp.sum(own, axis=(0, 3), keepdims=True) / total
    centered = own - average
    variance = jnp.sum(centered * centered, axis=(0, 3), keepdims=True) / total
    inverse = lax.rsqrt(variance + epsilon)
    normed = (centered * inverse).astype(jnp.bfloat16).transpose(2, 1, 0, 3).reshape(views, block, total)
    inverse = inverse.reshape(block, views).T[:, :, None]

    first, second, pieces = lax.optimization_barrier((normed[0], normed[1], pieces))
    pair = jnp.stack([second, partner(second)])
    first, pair = lax.optimization_barrier((first, pair))
    columns_b = lax.all_gather(pair, "mp", axis=0, axis_index_groups=GROUPS)
    columns_b = columns_b.reshape(MP * block, total)
    along_z, pieces = lax.optimization_barrier((gather(first, STRIDED_Z), pieces))
    slices = lax.all_to_all(pieces, "dp", split_axis=0, concat_axis=0)
    rows_own, columns_b, slices = lax.optimization_barrier(
        (gather(along_z, ALONG_X), columns_b, slices)
    )
    rows_other = swap(rows_own, 1).reshape(feat // 2, total)
    rows_own = rows_own.reshape(feat // 2, total)

    def gradient_of(rows_a, with_diagonal):
        correlation = (
            lax.dot_general(rows_a, columns_b, (((1,), (1,)), ((), ())), preferred_element_type=jnp.float32)
            / total
        )
        inner = 2.0 * redundancy_weight * correlation
        if with_diagonal:
            row = lax.broadcasted_iota(jnp.int32, correlation.shape, 0)
            column = lax.broadcasted_iota(jnp.int32, correlation.shape, 1)
            diagonal = (row < block) & (column == lax.rem(model_index, Y) * 2 * block + row)
            inner = inner + diagonal.astype(jnp.float32) * (2.0 * (correlation - 1.0) - inner)
        return (loss_scale * inner).astype(jnp.bfloat16)

    corr_own = gradient_of(rows_own, True)
    corr_other = gradient_of(rows_other, False)

    def times(lhs, rhs, dims):
        return lax.dot_general(lhs, rhs, (dims, ((), ())), preferred_element_type=jnp.float32) / total

    terms_b = (
        times(corr_own, rows_own, ((0,), (0,))) + times(corr_other, rows_other, ((0,), (0,)))
    ).astype(jnp.bfloat16)
    corr_own, corr_other, terms_b = lax.optimization_barrier((corr_own, corr_other, terms_b))
    terms_b = lax.all_to_all(
        terms_b.reshape(Y, 2, block, total), "mp", split_axis=0, concat_axis=0, axis_index_groups=GROUPS
    )
    terms_other = times(corr_other, columns_b, ((1,), (0,))).astype(jnp.bfloat16)
    terms_own = times(corr_own, columns_b, ((1,), (0,)))
    shape = (4, 4, block, total)
    both = terms_own.reshape(shape) + swap(terms_other.reshape(shape), 1).astype(jnp.float32)
    along_x = add(both.astype(jnp.bfloat16), ALONG_X).astype(jnp.bfloat16)
    along_x, terms_b, slices = lax.optimization_barrier((along_x, terms_b, slices))
    columns = lax.all_gather(slices, "mp", axis=0, axis_index_groups=GROUPS)
    terms_b = jnp.sum(terms_b.astype(jnp.float32), axis=0)
    grad_b = terms_b[0] + partner(terms_b[1].astype(jnp.bfloat16)).astype(jnp.float32)
    grads = jnp.stack([add(along_x, STRIDED_Z), grad_b])
    wide = normed.astype(jnp.float32)
    grad_mean = jnp.sum(grads, axis=2, keepdims=True) / total
    cross_mean = jnp.sum(grads * wide, axis=2, keepdims=True) / total
    grad_proj = ((grads - grad_mean - wide * cross_mean) * inverse).astype(jnp.bfloat16)
    grad_proj = grad_proj.transpose(1, 0, 2).reshape(block, views * total)
    grad_own = gather(gather(grad_proj, ALONG_Z), ALONG_X)
    grad_own, columns = lax.optimization_barrier((grad_own, columns))
    grad_other = swap(grad_own, 1)
    part = weight_half(grad_own.reshape(feat // 2, views * total), columns)
    return weight_half(grad_other.reshape(feat // 2, views * total), columns, position, part)


def solution(mesh):
    placed = (P(None, "dp", None), P("dp", "mp"))
    return jax.shard_map(
        per_device, mesh=mesh, in_specs=placed, out_specs=P("dp", "mp"), check_vma=False
    )
```

```python
import functools

import jax
import jax.numpy as jnp
from jax import lax
from jax.experimental import pallas as pl
from jax.experimental.pallas import tpu as pltpu
from jax.sharding import PartitionSpec as P

epsilon = 1e-05
redundancy_weight = 0.0051
loss_scale = 512.0
DP = 32
MP = 16
Y = 8
GROUPS = [list(range(Y)), list(range(Y, MP))]
ALONG_X = [(8,), (16,), (24,)]
ARRIVAL = (0, 1, 3, 2)
ALONG_Z = [(2,), (4,), (6,)]
STRIDED_Z = [(4,), (0, 8), (4, 8)]


def swap(array, data, model=0):
    mask = data * MP + model
    return lax.ppermute(array, ("dp", "mp"), [(i, i ^ mask) for i in range(DP * MP)])


def partner(array):
    return swap(array, 2)


def gather(block, masks):
    return jnp.stack([block] + [swap(block, *mask) for mask in masks])


def add(blocks, masks):
    parts = [blocks[0]] + [swap(blocks[k + 1], *mask) for k, mask in enumerate(masks)]
    return sum(part.astype(jnp.float32) for part in parts)


def project_kernel(first, last, order_ref, inputs_ref, own_ref, other_ref, *refs):
    out_ref = refs[-1]
    blocks, depth, _ = own_ref.shape
    result = None if first else refs[0][...]
    for core, weight_ref in enumerate((own_ref, other_ref)):
        for k in range(blocks):
            start = pl.multiple_of(order_ref[core * blocks + k] * depth, depth)
            part = jnp.dot(
                inputs_ref[:, pl.ds(start, depth)], weight_ref[k], preferred_element_type=jnp.float32
            )
            result = part if result is None else result + part
    out_ref[...] = result.T if last else result


def project(order, inputs, own, other, before=None, last=False):
    rows, feat = inputs.shape[0], own.shape[2]
    operands = (inputs, own, other) if before is None else (inputs, own, other, before)
    return pl.pallas_call(
        functools.partial(project_kernel, before is None, last),
        in_specs=[pl.BlockSpec(memory_space=pltpu.SMEM)]
        + [pl.BlockSpec(memory_space=pltpu.VMEM)] * len(operands),
        out_specs=pl.BlockSpec(memory_space=pltpu.VMEM),
        out_shape=jax.ShapeDtypeStruct((feat, rows) if last else (rows, feat), jnp.float32),
        compiler_params=pltpu.CompilerParams(vmem_limit_bytes=32 * 1024 * 1024),
        cost_estimate=pl.CostEstimate(
            flops=4 * rows * feat * own.shape[0] * own.shape[1],
            bytes_accessed=2 * 1024 * 1024,
            transcendentals=0,
        ),
    )(order, *operands)


def weight_kernel(own_ref, other_ref, columns_ref, *refs):
    *before, total_ref = refs
    step = pl.program_id(0) * pl.num_programs(1) + pl.program_id(1)
    half = own_ref.shape[0]

    @pl.when(step == 0)
    def _():
        total_ref[...] = jnp.zeros_like(total_ref)

    quarters, devices, share, rows = columns_ref.shape
    pieces = [columns_ref[:, d].reshape(quarters * share, rows) for d in range(devices)]
    columns = jnp.concatenate(pieces, axis=0)
    grad = jnp.concatenate([own_ref[...], other_ref[...]], axis=0)
    total_ref[...] += jnp.dot(grad, columns, preferred_element_type=jnp.float32)

    if before:
        position_ref, *parts, out_ref, placed_ref = before

        @pl.when(step == pl.num_programs(0) * pl.num_programs(1) - 1)
        def _():
            for k, part in enumerate(parts + [total_ref]):
                placed_ref[2 * half * k : 2 * half * (k + 1)] = part[...]
            blocks = [
                placed_ref[pl.ds(pl.multiple_of(position_ref[block] * 8, 8), 8)] for block in range(DP)
            ]
            out_ref[...] = jnp.concatenate(blocks, axis=0).T


def weight_part(own, other, columns, position=None, parts=()):
    half, depth = own.shape
    slices, devices, share, rows = columns.shape
    quarters, group = slices // 2, 8
    features = 2 * half * (len(parts) + 1)
    grad_spec = pl.BlockSpec(
        (half, group * quarters * share), lambda v, d: (0, v * (devices // group) + d)
    )
    in_specs = [
        grad_spec,
        grad_spec,
        pl.BlockSpec((quarters, group, share, rows), lambda v, d: (v, d, 0, 0)),
    ]
    scratch = []
    if parts:
        in_specs.append(pl.BlockSpec(memory_space=pltpu.SMEM))
        in_specs += [pl.BlockSpec((2 * half, rows), lambda v, d: (0, 0))] * len(parts)
        scratch = [pltpu.VMEM((features, rows), jnp.float32), pltpu.VMEM((2 * half, rows), jnp.float32)]
    shape = (rows, features) if parts else (2 * half, rows)
    return pl.pallas_call(
        weight_kernel,
        grid=(2, devices // group),
        in_specs=in_specs,
        out_specs=pl.BlockSpec(shape, lambda v, d: (0, 0)),
        out_shape=jax.ShapeDtypeStruct(shape, jnp.float32),
        scratch_shapes=scratch,
        compiler_params=pltpu.CompilerParams(vmem_limit_bytes=32 * 1024 * 1024),
        cost_estimate=pl.CostEstimate(
            flops=4 * half * depth * rows, bytes_accessed=5 * 1024 * 1024, transcendentals=0
        ),
    )(own, other, columns, *((position, *parts) if parts else ()))


def per_device(inputs, weight):
    views, images, width = inputs.shape
    total = images * DP
    data_index = lax.axis_index("dp")
    model_index = lax.axis_index("mp")
    feat = weight.shape[1]
    block = feat // DP
    rows = width // DP
    flat = inputs.reshape(views * images, width)

    place = jnp.arange(DP, dtype=jnp.int32)
    order = data_index ^ ((place >> 3) << 3 | (place & 3) << 1 | ((place >> 2) & 1))
    relative = place ^ data_index
    position = (relative >> 3) << 3 | (relative & 1) << 2 | ((relative >> 1) & 3)

    share = views * images // Y
    mine = lax.dynamic_slice_in_dim(flat, lax.rem(model_index, Y) * share, share, axis=0)
    pieces = mine.reshape(share, DP, rows).transpose(1, 0, 2)
    along_z = gather(weight, ALONG_Z)
    parts = [along_z] + [swap(along_z, *mask) for mask in ALONG_X]
    projected = None
    for k in ARRIVAL:
        projected = project(
            order[8 * k : 8 * k + 8], flat, parts[k], swap(parts[k], 1), projected, k == ARRIVAL[-1]
        )

    own = lax.all_to_all(
        projected.reshape(DP, block, views * images), "dp", split_axis=0, concat_axis=0
    ).reshape(DP, block, views, images)
    average = jnp.sum(own, axis=(0, 3), keepdims=True) / total
    centered = own - average
    variance = jnp.sum(centered * centered, axis=(0, 3), keepdims=True) / total
    inverse = lax.rsqrt(variance + epsilon)
    normed = (centered * inverse).astype(jnp.bfloat16).transpose(2, 1, 0, 3).reshape(views, block, total)
    inverse = inverse.reshape(block, views).T[:, :, None]

    first, second, pieces = lax.optimization_barrier((normed[0], normed[1], pieces))
    pair = jnp.stack([second, partner(second)])
    first, pair = lax.optimization_barrier((first, pair))
    columns_b = lax.all_gather(pair, "mp", axis=0, axis_index_groups=GROUPS)
    columns_b = columns_b.reshape(MP * block, total)
    along_z, pieces = lax.optimization_barrier((gather(first, STRIDED_Z), pieces))
    slices = lax.all_to_all(pieces, "dp", split_axis=0, concat_axis=0)
    rows_own, columns_b, slices = lax.optimization_barrier(
        (gather(along_z, ALONG_X), columns_b, slices)
    )
    rows_other = swap(rows_own, 1).reshape(feat // 2, total)
    rows_own = rows_own.reshape(feat // 2, total)

    def gradient_of(rows_a, with_diagonal):
        correlation = (
            lax.dot_general(rows_a, columns_b, (((1,), (1,)), ((), ())), preferred_element_type=jnp.float32)
            / total
        )
        inner = 2.0 * redundancy_weight * correlation
        if with_diagonal:
            row = lax.broadcasted_iota(jnp.int32, correlation.shape, 0)
            column = lax.broadcasted_iota(jnp.int32, correlation.shape, 1)
            diagonal = (row < block) & (column == lax.rem(model_index, Y) * 2 * block + row)
            inner = inner + diagonal.astype(jnp.float32) * (2.0 * (correlation - 1.0) - inner)
        return (loss_scale * inner).astype(jnp.bfloat16)

    corr_own = gradient_of(rows_own, True)
    corr_other = gradient_of(rows_other, False)

    def times(lhs, rhs, dims):
        return lax.dot_general(lhs, rhs, (dims, ((), ())), preferred_element_type=jnp.float32) / total

    half = (feat // 2, Y, 2, block)
    sides = [
        corr.reshape(half).transpose(2, 0, 1, 3).reshape(2, feat // 2, Y * block)
        for corr in (corr_own, corr_other)
    ]
    terms_b = [
        times(sides[0][k], rows_own, ((0,), (0,))) + times(sides[1][k], rows_other, ((0,), (0,)))
        for k in (0, 1)
    ]
    away = terms_b[1].astype(jnp.bfloat16)
    corr_own, corr_other, away = lax.optimization_barrier((corr_own, corr_other, away))
    terms_b = (terms_b[0] + partner(away).astype(jnp.float32)).astype(jnp.bfloat16)
    terms_b = lax.all_to_all(
        terms_b.reshape(Y, block, total), "mp", split_axis=0, concat_axis=0, axis_index_groups=GROUPS
    )
    terms_b, slices = lax.optimization_barrier((terms_b, slices))
    columns = lax.all_gather(slices, "mp", axis=0, axis_index_groups=GROUPS)
    grad_b = jnp.sum(terms_b.astype(jnp.float32), axis=0)
    terms_other = times(corr_other, columns_b, ((1,), (0,))).astype(jnp.bfloat16)
    terms_own = times(corr_own, columns_b, ((1,), (0,)))
    shape = (4, 4, block, total)
    both = terms_own.reshape(shape) + swap(terms_other.reshape(shape), 1).astype(jnp.float32)
    along_x = add(both.astype(jnp.bfloat16), ALONG_X).astype(jnp.bfloat16)
    grads = jnp.stack([add(along_x, STRIDED_Z), grad_b])
    wide = normed.astype(jnp.float32)
    grad_mean = jnp.sum(grads, axis=2, keepdims=True) / total
    cross_mean = jnp.sum(grads * wide, axis=2, keepdims=True) / total
    grad_proj = ((grads - grad_mean - wide * cross_mean) * inverse).astype(jnp.bfloat16)
    grad_proj = grad_proj.transpose(1, 0, 2).reshape(block, views * total)
    along_z = gather(grad_proj, ALONG_Z)
    parts = [along_z] + [swap(along_z, *mask) for mask in ALONG_X]
    shape = (4 * block, views * total)
    pairs = [(part.reshape(shape), swap(part, 1).reshape(shape)) for part in parts]
    products = [weight_part(*pairs[k], columns) for k in ARRIVAL[:-1]]
    turn = sum(jnp.where(position // 8 == k, place, 0) for place, k in enumerate(ARRIVAL))
    position = turn * 8 + position % 8
    return weight_part(*pairs[ARRIVAL[-1]], columns, position, products)


def solution(mesh):
    placed = (P(None, "dp", None), P("dp", "mp"))
    return jax.shard_map(
        per_device, mesh=mesh, in_specs=placed, out_specs=P("dp", "mp"), check_vma=False
    )
```

```python
import functools

import jax
import jax.numpy as jnp
from jax import lax
from jax.experimental import pallas as pl
from jax.experimental.pallas import tpu as pltpu
from jax.sharding import PartitionSpec as P

epsilon = 1e-05
redundancy_weight = 0.0051
loss_scale = 512.0
DP = 32
MP = 16
Y = 8
GROUPS = [list(range(Y)), list(range(Y, MP))]
ALONG_X = [(8,), (16,), (24,)]
ALONG_Z = [(2,), (4,), (6,)]
STRIDED_Z = [(4,), (0, 8), (4, 8)]


def swap(array, data, model=0):
    mask = data * MP + model
    return lax.ppermute(array, ("dp", "mp"), [(i, i ^ mask) for i in range(DP * MP)])


def partner(array):
    return swap(array, 2)


def gather(block, masks, *later):
    parts = [block] + [swap(block, *mask) for mask in masks]
    if later:
        parts[1], *later = lax.optimization_barrier((parts[1], *later))
    return jnp.stack(parts), *later


def add(blocks, masks, *later):
    parts = [blocks[0]] + [swap(blocks[k + 1], *mask) for k, mask in enumerate(masks)]
    if later:
        parts[1], *later = lax.optimization_barrier((parts[1], *later))
    return sum(part.astype(jnp.float32) for part in parts), *later


def project_kernel(last, order_ref, inputs_ref, weight_ref, *refs):
    out_ref = refs[-1]
    blocks, depth, _ = weight_ref.shape
    result = refs[0][...] if last else None
    for k in range(blocks):
        columns = pl.ds(pl.multiple_of(order_ref[k] * depth, depth), depth)
        part = jnp.dot(inputs_ref[:, columns], weight_ref[k], preferred_element_type=jnp.float32)
        result = part if result is None else result + part
    out_ref[...] = result.T if last else result


def project(order, inputs, weight, before=None):
    rows, feat = inputs.shape[0], weight.shape[2]
    operands = (inputs, weight) if before is None else (inputs, weight, before)
    return pl.pallas_call(
        functools.partial(project_kernel, before is not None),
        in_specs=[pl.BlockSpec(memory_space=pltpu.SMEM)]
        + [pl.BlockSpec(memory_space=pltpu.VMEM)] * len(operands),
        out_specs=pl.BlockSpec(memory_space=pltpu.VMEM),
        out_shape=jax.ShapeDtypeStruct((rows, feat) if before is None else (feat, rows), jnp.float32),
        compiler_params=pltpu.CompilerParams(vmem_limit_bytes=32 * 1024 * 1024),
        cost_estimate=pl.CostEstimate(
            flops=2 * rows * feat * weight.shape[0] * weight.shape[1],
            bytes_accessed=6 * 1024 * 1024,
            transcendentals=0,
        ),
    )(order, *operands)


def weight_kernel(last, grad_ref, columns_ref, *refs):
    total_ref = refs[-1]
    step = pl.program_id(0) * pl.num_programs(1) + pl.program_id(1)

    @pl.when(step == 0)
    def _():
        total_ref[...] = jnp.zeros_like(total_ref)

    quarters, devices, share, rows = columns_ref.shape
    pieces = [columns_ref[:, d].reshape(quarters * share, rows) for d in range(devices)]
    columns = jnp.concatenate(pieces, axis=0)
    total_ref[...] += jnp.dot(grad_ref[...], columns, preferred_element_type=jnp.float32)

    if last:
        position_ref, own_ref, out_ref, placed_ref = refs[:4]
        half = own_ref.shape[0]

        @pl.when(step == pl.num_programs(0) * pl.num_programs(1) - 1)
        def _():
            placed_ref[:half] = own_ref[...]
            placed_ref[half:] = total_ref[...]
            blocks = [
                placed_ref[pl.ds(pl.multiple_of(position_ref[block] * 8, 8), 8)] for block in range(DP)
            ]
            out_ref[...] = jnp.concatenate(blocks, axis=0).T


def weight_half(grad, columns, position=None, own=None):
    half, depth = grad.shape
    slices, devices, share, rows = columns.shape
    quarters, group = slices // 2, 8
    last = own is not None
    in_specs = [
        pl.BlockSpec((half, group * quarters * share), lambda v, d: (0, v * (devices // group) + d)),
        pl.BlockSpec((quarters, group, share, rows), lambda v, d: (v, d, 0, 0)),
    ]
    scratch = [pltpu.VMEM((half, rows), jnp.float32)]
    if last:
        in_specs += [
            pl.BlockSpec(memory_space=pltpu.SMEM),
            pl.BlockSpec((half, rows), lambda v, d: (0, 0)),
        ]
        scratch = [pltpu.VMEM((2 * half, rows), jnp.float32)] + scratch
    return pl.pallas_call(
        functools.partial(weight_kernel, last),
        grid=(2, devices // group),
        in_specs=in_specs,
        out_specs=pl.BlockSpec((rows, 2 * half) if last else (half, rows), lambda v, d: (0, 0)),
        out_shape=jax.ShapeDtypeStruct((rows, 2 * half) if last else (half, rows), jnp.float32),
        scratch_shapes=scratch if last else [],
        compiler_params=pltpu.CompilerParams(vmem_limit_bytes=32 * 1024 * 1024),
        cost_estimate=pl.CostEstimate(
            flops=2 * half * depth * rows, bytes_accessed=6 * 1024 * 1024, transcendentals=0
        ),
    )(grad, columns, *((position, own) if last else ()))


def per_device(inputs, weight):
    views, images, width = inputs.shape
    total = images * DP
    data_index = lax.axis_index("dp")
    model_index = lax.axis_index("mp")
    feat = weight.shape[1]
    block = feat // DP
    rows = width // DP
    flat = inputs.reshape(views * images, width)

    place = jnp.arange(DP, dtype=jnp.int32)
    distance = (place >> 4) | ((place >> 2) & 3) << 3 | (place & 3) << 1
    order = data_index ^ distance
    relative = place ^ data_index
    position = (relative & 1) << 4 | (relative >> 3) << 2 | ((relative >> 1) & 3)

    share = views * images // Y
    mine = lax.dynamic_slice_in_dim(flat, lax.rem(model_index, Y) * share, share, axis=0)
    pieces = mine.reshape(share, DP, rows).transpose(1, 0, 2)
    weight_own = gather(gather(weight, ALONG_Z)[0], ALONG_X)[0]
    weight_other = swap(weight_own, 1)
    half = (DP // 2, rows, feat)
    projected = project(order[: DP // 2], flat, weight_own.reshape(half))
    projected = project(order[DP // 2 :], flat, weight_other.reshape(half), projected)

    own = lax.all_to_all(
        projected.reshape(DP, block, views * images), "dp", split_axis=0, concat_axis=0
    ).reshape(DP, block, views, images)
    average = jnp.sum(own, axis=(0, 3), keepdims=True) / total
    centered = own - average
    variance = jnp.sum(centered * centered, axis=(0, 3), keepdims=True) / total
    inverse = lax.rsqrt(variance + epsilon)
    normed = (centered * inverse).astype(jnp.bfloat16).transpose(2, 1, 0, 3).reshape(views, block, total)
    inverse = inverse.reshape(block, views).T[:, :, None]

    first, second, pieces = lax.optimization_barrier((normed[0], normed[1], pieces))
    pair = jnp.stack([second, partner(second)])
    first, pair = lax.optimization_barrier((first, pair))
    columns_b = lax.all_gather(pair, "mp", axis=0, axis_index_groups=GROUPS)
    columns_b = columns_b.reshape(MP * block, total)
    rows_own, pieces = gather(gather(first, STRIDED_Z)[0], ALONG_X, pieces)
    slices = lax.all_to_all(pieces, "dp", split_axis=0, concat_axis=0)
    rows_own, columns_b = lax.optimization_barrier((rows_own, columns_b))
    rows_other = swap(rows_own, 1).reshape(feat // 2, total)
    rows_own = rows_own.reshape(feat // 2, total)

    def gradient_of(rows_a, with_diagonal):
        correlation = (
            lax.dot_general(rows_a, columns_b, (((1,), (1,)), ((), ())), preferred_element_type=jnp.float32)
            / total
        )
        inner = 2.0 * redundancy_weight * correlation
        if with_diagonal:
            row = lax.broadcasted_iota(jnp.int32, correlation.shape, 0)
            column = lax.broadcasted_iota(jnp.int32, correlation.shape, 1)
            diagonal = (row < block) & (column == lax.rem(model_index, Y) * 2 * block + row)
            inner = inner + diagonal.astype(jnp.float32) * (2.0 * (correlation - 1.0) - inner)
        return (loss_scale * inner).astype(jnp.bfloat16)

    corr_own = gradient_of(rows_own, True)
    corr_other = gradient_of(rows_other, False)

    def times(lhs, rhs, dims):
        return lax.dot_general(lhs, rhs, (dims, ((), ())), preferred_element_type=jnp.float32) / total

    half = (feat // 2, Y, 2, block)
    sides = [
        corr.reshape(half).transpose(2, 0, 1, 3).reshape(2, feat // 2, Y * block)
        for corr in (corr_own, corr_other)
    ]
    terms_b = [
        times(sides[0][k], rows_own, ((0,), (0,))) + times(sides[1][k], rows_other, ((0,), (0,)))
        for k in (0, 1)
    ]
    away = terms_b[1].astype(jnp.bfloat16)
    corr_own, corr_other, away = lax.optimization_barrier((corr_own, corr_other, away))
    terms_b = (terms_b[0] + partner(away).astype(jnp.float32)).astype(jnp.bfloat16)
    terms_b, slices = lax.optimization_barrier((terms_b, slices))
    terms_b = lax.all_to_all(
        terms_b.reshape(Y, block, total), "mp", split_axis=0, concat_axis=0, axis_index_groups=GROUPS
    )
    terms_other = times(corr_other, columns_b, ((1,), (0,))).astype(jnp.bfloat16)
    terms_own = times(corr_own, columns_b, ((1,), (0,)))
    shape = (4, 4, block, total)
    both = terms_own.reshape(shape) + swap(terms_other.reshape(shape), 1).astype(jnp.float32)
    along_x = add(both.astype(jnp.bfloat16), ALONG_X)[0].astype(jnp.bfloat16)
    grad_a, terms_b, slices = add(along_x, STRIDED_Z, terms_b, slices)
    columns = lax.all_gather(slices, "mp", axis=0, axis_index_groups=GROUPS)
    grads = jnp.stack([grad_a, jnp.sum(terms_b.astype(jnp.float32), axis=0)])
    wide = normed.astype(jnp.float32)
    grad_mean = jnp.sum(grads, axis=2, keepdims=True) / total
    cross_mean = jnp.sum(grads * wide, axis=2, keepdims=True) / total
    grad_proj = ((grads - grad_mean - wide * cross_mean) * inverse).astype(jnp.bfloat16)
    grad_proj = grad_proj.transpose(1, 0, 2).reshape(block, views * total)
    grad_own, columns = gather(gather(grad_proj, ALONG_Z)[0], ALONG_X, columns)
    grad_other = swap(grad_own, 1)
    part = weight_half(grad_own.reshape(feat // 2, views * total), columns)
    return weight_half(grad_other.reshape(feat // 2, views * total), columns, position, part)


def solution(mesh):
    placed = (P(None, "dp", None), P("dp", "mp"))
    return jax.shard_map(
        per_device, mesh=mesh, in_specs=placed, out_specs=P("dp", "mp"), check_vma=False
    )
```

```python
import functools

import jax
import jax.numpy as jnp
from jax import lax
from jax.experimental import pallas as pl
from jax.experimental.pallas import tpu as pltpu
from jax.sharding import PartitionSpec as P

epsilon = 1e-05
redundancy_weight = 0.0051
loss_scale = 512.0
DP = 32
MP = 16
Y = 8
GROUPS = [list(range(Y)), list(range(Y, MP))]
ALONG_X = [(8,), (16,), (24,)]
ALONG_Z = [(2,), (4,), (6,)]
STRIDED_Z = [(4,), (0, 8), (4, 8)]


def swap(array, data, model=0):
    mask = data * MP + model
    return lax.ppermute(array, ("dp", "mp"), [(i, i ^ mask) for i in range(DP * MP)])


def partner(array):
    return swap(array, 2)


def gather(block, masks, *later):
    parts = [block] + [swap(block, *mask) for mask in masks]
    if later:
        parts[1], *later = lax.optimization_barrier((parts[1], *later))
    return jnp.stack(parts), *later


def add(blocks, masks, *later):
    parts = [blocks[0]] + [swap(blocks[k + 1], *mask) for k, mask in enumerate(masks)]
    *parts, later = lax.optimization_barrier((*parts, later))
    return sum(part.astype(jnp.float32) for part in parts), *later


def project_kernel(last, order_ref, inputs_ref, weight_ref, *refs):
    out_ref = refs[-1]
    blocks, depth, _ = weight_ref.shape
    result = refs[0][...] if last else None
    for k in range(blocks):
        columns = pl.ds(pl.multiple_of(order_ref[k] * depth, depth), depth)
        part = jnp.dot(inputs_ref[:, columns], weight_ref[k], preferred_element_type=jnp.float32)
        result = part if result is None else result + part
    out_ref[...] = result.T if last else result


def project(order, inputs, weight, before=None):
    rows, feat = inputs.shape[0], weight.shape[2]
    operands = (inputs, weight) if before is None else (inputs, weight, before)
    return pl.pallas_call(
        functools.partial(project_kernel, before is not None),
        in_specs=[pl.BlockSpec(memory_space=pltpu.SMEM)]
        + [pl.BlockSpec(memory_space=pltpu.VMEM)] * len(operands),
        out_specs=pl.BlockSpec(memory_space=pltpu.VMEM),
        out_shape=jax.ShapeDtypeStruct((rows, feat) if before is None else (feat, rows), jnp.float32),
        compiler_params=pltpu.CompilerParams(vmem_limit_bytes=32 * 1024 * 1024),
        cost_estimate=pl.CostEstimate(
            flops=2 * rows * feat * weight.shape[0] * weight.shape[1],
            bytes_accessed=6 * 1024 * 1024,
            transcendentals=0,
        ),
    )(order, *operands)


def weight_kernel(last, grad_ref, columns_ref, *refs):
    total_ref = refs[-1]
    step = pl.program_id(0) * pl.num_programs(1) + pl.program_id(1)

    @pl.when(step == 0)
    def _():
        total_ref[...] = jnp.zeros_like(total_ref)

    quarters, devices, share, rows = columns_ref.shape
    pieces = [columns_ref[:, d].reshape(quarters * share, rows) for d in range(devices)]
    columns = jnp.concatenate(pieces, axis=0)
    total_ref[...] += jnp.dot(grad_ref[...], columns, preferred_element_type=jnp.float32)

    if last:
        position_ref, own_ref, out_ref, placed_ref = refs[:4]
        half = own_ref.shape[0]

        @pl.when(step == pl.num_programs(0) * pl.num_programs(1) - 1)
        def _():
            placed_ref[:half] = own_ref[...]
            placed_ref[half:] = total_ref[...]
            blocks = [
                placed_ref[pl.ds(pl.multiple_of(position_ref[block] * 8, 8), 8)] for block in range(DP)
            ]
            out_ref[...] = jnp.concatenate(blocks, axis=0).T


def weight_half(grad, columns, position=None, own=None):
    half, depth = grad.shape
    slices, devices, share, rows = columns.shape
    quarters, group = slices // 2, 8
    last = own is not None
    in_specs = [
        pl.BlockSpec((half, group * quarters * share), lambda v, d: (0, v * (devices // group) + d)),
        pl.BlockSpec((quarters, group, share, rows), lambda v, d: (v, d, 0, 0)),
    ]
    scratch = [pltpu.VMEM((half, rows), jnp.float32)]
    if last:
        in_specs += [
            pl.BlockSpec(memory_space=pltpu.SMEM),
            pl.BlockSpec((half, rows), lambda v, d: (0, 0)),
        ]
        scratch = [pltpu.VMEM((2 * half, rows), jnp.float32)] + scratch
    return pl.pallas_call(
        functools.partial(weight_kernel, last),
        grid=(2, devices // group),
        in_specs=in_specs,
        out_specs=pl.BlockSpec((rows, 2 * half) if last else (half, rows), lambda v, d: (0, 0)),
        out_shape=jax.ShapeDtypeStruct((rows, 2 * half) if last else (half, rows), jnp.float32),
        scratch_shapes=scratch if last else [],
        compiler_params=pltpu.CompilerParams(vmem_limit_bytes=32 * 1024 * 1024),
        cost_estimate=pl.CostEstimate(
            flops=2 * half * depth * rows, bytes_accessed=6 * 1024 * 1024, transcendentals=0
        ),
    )(grad, columns, *((position, own) if last else ()))


def per_device(inputs, weight):
    views, images, width = inputs.shape
    total = images * DP
    data_index = lax.axis_index("dp")
    model_index = lax.axis_index("mp")
    feat = weight.shape[1]
    block = feat // DP
    rows = width // DP
    flat = inputs.reshape(views * images, width)

    place = jnp.arange(DP, dtype=jnp.int32)
    distance = (place >> 4) | ((place >> 2) & 3) << 3 | (place & 3) << 1
    order = data_index ^ distance
    relative = place ^ data_index
    position = (relative & 1) << 4 | (relative >> 3) << 2 | ((relative >> 1) & 3)

    share = views * images // Y
    mine = lax.dynamic_slice_in_dim(flat, lax.rem(model_index, Y) * share, share, axis=0)
    pieces = mine.reshape(share, DP, rows).transpose(1, 0, 2)
    weight_own = gather(gather(weight, ALONG_Z)[0], ALONG_X)[0]
    weight_other = swap(weight_own, 1)
    half = (DP // 2, rows, feat)
    projected = project(order[: DP // 2], flat, weight_own.reshape(half))
    projected = project(order[DP // 2 :], flat, weight_other.reshape(half), projected)

    own = lax.all_to_all(
        projected.reshape(DP, block, views * images), "dp", split_axis=0, concat_axis=0
    ).reshape(DP, block, views, images)
    average = jnp.sum(own, axis=(0, 3), keepdims=True) / total
    centered = own - average
    variance = jnp.sum(centered * centered, axis=(0, 3), keepdims=True) / total
    inverse = lax.rsqrt(variance + epsilon)
    normed = (centered * inverse).astype(jnp.bfloat16).transpose(2, 1, 0, 3).reshape(views, block, total)
    inverse = inverse.reshape(block, views).T[:, :, None]

    first, second, pieces = lax.optimization_barrier((normed[0], normed[1], pieces))
    pair = jnp.stack([second, partner(second)])
    first, pair = lax.optimization_barrier((first, pair))
    columns_b = lax.all_gather(pair, "mp", axis=0, axis_index_groups=GROUPS)
    columns_b = columns_b.reshape(MP * block, total)
    along_z, pieces = lax.optimization_barrier((gather(first, STRIDED_Z)[0], pieces))
    slices = lax.all_to_all(pieces, "dp", split_axis=0, concat_axis=0)
    rows_own, columns_b, slices = lax.optimization_barrier(
        (gather(along_z, ALONG_X)[0], columns_b, slices)
    )
    rows_other = swap(rows_own, 1).reshape(feat // 2, total)
    rows_own = rows_own.reshape(feat // 2, total)

    def gradient_of(rows_a, with_diagonal):
        correlation = (
            lax.dot_general(rows_a, columns_b, (((1,), (1,)), ((), ())), preferred_element_type=jnp.float32)
            / total
        )
        inner = 2.0 * redundancy_weight * correlation
        if with_diagonal:
            row = lax.broadcasted_iota(jnp.int32, correlation.shape, 0)
            column = lax.broadcasted_iota(jnp.int32, correlation.shape, 1)
            diagonal = (row < block) & (column == lax.rem(model_index, Y) * 2 * block + row)
            inner = inner + diagonal.astype(jnp.float32) * (2.0 * (correlation - 1.0) - inner)
        return (loss_scale * inner).astype(jnp.bfloat16)

    corr_own = gradient_of(rows_own, True)
    corr_other = gradient_of(rows_other, False)

    def times(lhs, rhs, dims):
        return lax.dot_general(lhs, rhs, (dims, ((), ())), preferred_element_type=jnp.float32) / total

    half = (feat // 2, Y, 2, block)
    sides = [
        corr.reshape(half).transpose(2, 0, 1, 3).reshape(2, feat // 2, Y * block)
        for corr in (corr_own, corr_other)
    ]
    terms_b = [
        times(sides[0][k], rows_own, ((0,), (0,))) + times(sides[1][k], rows_other, ((0,), (0,)))
        for k in (0, 1)
    ]
    away = terms_b[1].astype(jnp.bfloat16)
    corr_own, corr_other, away = lax.optimization_barrier((corr_own, corr_other, away))
    terms_b = (terms_b[0] + partner(away).astype(jnp.float32)).astype(jnp.bfloat16)
    terms_b = lax.all_to_all(
        terms_b.reshape(Y, block, total), "mp", split_axis=0, concat_axis=0, axis_index_groups=GROUPS
    )
    terms_other = times(corr_other, columns_b, ((1,), (0,))).astype(jnp.bfloat16)
    terms_own = times(corr_own, columns_b, ((1,), (0,)))
    shape = (4, 4, block, total)
    both = terms_own.reshape(shape) + swap(terms_other.reshape(shape), 1).astype(jnp.float32)
    along_x = add(both.astype(jnp.bfloat16), ALONG_X)[0].astype(jnp.bfloat16)
    grad_a, terms_b, slices = add(along_x, STRIDED_Z, terms_b, slices)
    columns = lax.all_gather(slices, "mp", axis=0, axis_index_groups=GROUPS)
    grads = jnp.stack([grad_a, jnp.sum(terms_b.astype(jnp.float32), axis=0)])
    wide = normed.astype(jnp.float32)
    grad_mean = jnp.sum(grads, axis=2, keepdims=True) / total
    cross_mean = jnp.sum(grads * wide, axis=2, keepdims=True) / total
    grad_proj = ((grads - grad_mean - wide * cross_mean) * inverse).astype(jnp.bfloat16)
    grad_proj = grad_proj.transpose(1, 0, 2).reshape(block, views * total)
    grad_own, columns = gather(gather(grad_proj, ALONG_Z)[0], ALONG_X, columns)
    grad_other = swap(grad_own, 1)
    part = weight_half(grad_own.reshape(feat // 2, views * total), columns)
    return weight_half(grad_other.reshape(feat // 2, views * total), columns, position, part)


def solution(mesh):
    placed = (P(None, "dp", None), P("dp", "mp"))
    return jax.shard_map(
        per_device, mesh=mesh, in_specs=placed, out_specs=P("dp", "mp"), check_vma=False
    )
```

```python
import functools

import jax
import jax.numpy as jnp
from jax import lax
from jax.experimental import pallas as pl
from jax.experimental.pallas import tpu as pltpu
from jax.sharding import PartitionSpec as P

epsilon = 1e-05
redundancy_weight = 0.0051
loss_scale = 512.0
DP = 32
MP = 16
Y = 8
GROUPS = [list(range(Y)), list(range(Y, MP))]
ALONG_X = [(8,), (16,), (24,)]
ALONG_Z = [(2,), (4,), (6,)]
STRIDED_Z = [(4,), (0, 8), (4, 8)]


def swap(array, data, model=0):
    mask = data * MP + model
    return lax.ppermute(array, ("dp", "mp"), [(i, i ^ mask) for i in range(DP * MP)])


def partner(array):
    return swap(array, 2)


def gather(block, masks, *later):
    parts = [block] + [swap(block, *mask) for mask in masks]
    if later:
        parts[1], *later = lax.optimization_barrier((parts[1], *later))
    return jnp.stack(parts), *later


def add(blocks, masks, *later):
    parts = [blocks[0]] + [swap(blocks[k + 1], *mask) for k, mask in enumerate(masks)]
    parts, later = lax.optimization_barrier((parts, later))
    return sum(part.astype(jnp.float32) for part in parts), *later


def project_kernel(last, order_ref, inputs_ref, weight_ref, *refs):
    out_ref = refs[-1]
    blocks, depth, _ = weight_ref.shape
    result = refs[0][...] if last else None
    for k in range(blocks):
        columns = pl.ds(pl.multiple_of(order_ref[k] * depth, depth), depth)
        part = jnp.dot(inputs_ref[:, columns], weight_ref[k], preferred_element_type=jnp.float32)
        result = part if result is None else result + part
    out_ref[...] = result.T if last else result


def project(order, inputs, weight, before=None):
    rows, feat = inputs.shape[0], weight.shape[2]
    operands = (inputs, weight) if before is None else (inputs, weight, before)
    return pl.pallas_call(
        functools.partial(project_kernel, before is not None),
        in_specs=[pl.BlockSpec(memory_space=pltpu.SMEM)]
        + [pl.BlockSpec(memory_space=pltpu.VMEM)] * len(operands),
        out_specs=pl.BlockSpec(memory_space=pltpu.VMEM),
        out_shape=jax.ShapeDtypeStruct((rows, feat) if before is None else (feat, rows), jnp.float32),
        compiler_params=pltpu.CompilerParams(vmem_limit_bytes=32 * 1024 * 1024),
        cost_estimate=pl.CostEstimate(
            flops=2 * rows * feat * weight.shape[0] * weight.shape[1],
            bytes_accessed=6 * 1024 * 1024,
            transcendentals=0,
        ),
    )(order, *operands)


def weight_kernel(last, grad_ref, columns_ref, *refs):
    total_ref = refs[-1]
    step = pl.program_id(0) * pl.num_programs(1) + pl.program_id(1)

    @pl.when(step == 0)
    def _():
        total_ref[...] = jnp.zeros_like(total_ref)

    quarters, devices, share, rows = columns_ref.shape
    pieces = [columns_ref[:, d].reshape(quarters * share, rows) for d in range(devices)]
    columns = jnp.concatenate(pieces, axis=0)
    total_ref[...] += jnp.dot(grad_ref[...], columns, preferred_element_type=jnp.float32)

    if last:
        position_ref, own_ref, out_ref, placed_ref = refs[:4]
        half = own_ref.shape[0]

        @pl.when(step == pl.num_programs(0) * pl.num_programs(1) - 1)
        def _():
            placed_ref[:half] = own_ref[...]
            placed_ref[half:] = total_ref[...]
            blocks = [
                placed_ref[pl.ds(pl.multiple_of(position_ref[block] * 8, 8), 8)] for block in range(DP)
            ]
            out_ref[...] = jnp.concatenate(blocks, axis=0).T


def weight_half(grad, columns, position=None, own=None):
    half, depth = grad.shape
    slices, devices, share, rows = columns.shape
    quarters, group = slices // 2, 8
    last = own is not None
    in_specs = [
        pl.BlockSpec((half, group * quarters * share), lambda v, d: (0, v * (devices // group) + d)),
        pl.BlockSpec((quarters, group, share, rows), lambda v, d: (v, d, 0, 0)),
    ]
    scratch = [pltpu.VMEM((half, rows), jnp.float32)]
    if last:
        in_specs += [
            pl.BlockSpec(memory_space=pltpu.SMEM),
            pl.BlockSpec((half, rows), lambda v, d: (0, 0)),
        ]
        scratch = [pltpu.VMEM((2 * half, rows), jnp.float32)] + scratch
    return pl.pallas_call(
        functools.partial(weight_kernel, last),
        grid=(2, devices // group),
        in_specs=in_specs,
        out_specs=pl.BlockSpec((rows, 2 * half) if last else (half, rows), lambda v, d: (0, 0)),
        out_shape=jax.ShapeDtypeStruct((rows, 2 * half) if last else (half, rows), jnp.float32),
        scratch_shapes=scratch if last else [],
        compiler_params=pltpu.CompilerParams(vmem_limit_bytes=32 * 1024 * 1024),
        cost_estimate=pl.CostEstimate(
            flops=2 * half * depth * rows, bytes_accessed=6 * 1024 * 1024, transcendentals=0
        ),
    )(grad, columns, *((position, own) if last else ()))


def per_device(inputs, weight):
    views, images, width = inputs.shape
    total = images * DP
    data_index = lax.axis_index("dp")
    model_index = lax.axis_index("mp")
    feat = weight.shape[1]
    block = feat // DP
    rows = width // DP
    flat = inputs.reshape(views * images, width)

    place = jnp.arange(DP, dtype=jnp.int32)
    distance = (place >> 4) | ((place >> 2) & 3) << 3 | (place & 3) << 1
    order = data_index ^ distance
    relative = place ^ data_index
    position = (relative & 1) << 4 | (relative >> 3) << 2 | ((relative >> 1) & 3)

    share = views * images // Y
    mine = lax.dynamic_slice_in_dim(flat, lax.rem(model_index, Y) * share, share, axis=0)
    pieces = mine.reshape(share, DP, rows).transpose(1, 0, 2)
    weight_own, pieces = gather(gather(weight, ALONG_Z)[0], ALONG_X, pieces)
    slices = lax.all_to_all(pieces, "dp", split_axis=0, concat_axis=0)
    weight_other = swap(weight_own, 1)
    half = (DP // 2, rows, feat)
    projected = project(order[: DP // 2], flat, weight_own.reshape(half))
    projected, slices = lax.optimization_barrier((projected, slices))
    projected = project(order[DP // 2 :], flat, weight_other.reshape(half), projected)

    own = lax.all_to_all(
        projected.reshape(DP, block, views * images), "dp", split_axis=0, concat_axis=0
    ).reshape(DP, block, views, images)
    average = jnp.sum(own, axis=(0, 3), keepdims=True) / total
    centered = own - average
    variance = jnp.sum(centered * centered, axis=(0, 3), keepdims=True) / total
    inverse = lax.rsqrt(variance + epsilon)
    normed = (centered * inverse).astype(jnp.bfloat16).transpose(2, 1, 0, 3).reshape(views, block, total)
    inverse = inverse.reshape(block, views).T[:, :, None]

    second = normed[1]
    pair = jnp.stack([second, partner(second)])
    first, pair = lax.optimization_barrier((normed[0], pair))
    columns_b = lax.all_gather(pair, "mp", axis=0, axis_index_groups=GROUPS)
    columns_b = columns_b.reshape(MP * block, total)
    rows_own = gather(gather(first, STRIDED_Z)[0], ALONG_X)[0]
    rows_own, columns_b, slices = lax.optimization_barrier((rows_own, columns_b, slices))
    columns = lax.all_gather(slices, "mp", axis=0, axis_index_groups=GROUPS)
    rows_other = swap(rows_own, 1).reshape(feat // 2, total)
    rows_own = rows_own.reshape(feat // 2, total)

    def gradient_of(rows_a, with_diagonal):
        correlation = (
            lax.dot_general(rows_a, columns_b, (((1,), (1,)), ((), ())), preferred_element_type=jnp.float32)
            / total
        )
        inner = 2.0 * redundancy_weight * correlation
        if with_diagonal:
            row = lax.broadcasted_iota(jnp.int32, correlation.shape, 0)
            column = lax.broadcasted_iota(jnp.int32, correlation.shape, 1)
            diagonal = (row < block) & (column == lax.rem(model_index, Y) * 2 * block + row)
            inner = inner + diagonal.astype(jnp.float32) * (2.0 * (correlation - 1.0) - inner)
        return (loss_scale * inner).astype(jnp.bfloat16)

    corr_own = gradient_of(rows_own, True)
    corr_other = gradient_of(rows_other, False)

    def times(lhs, rhs, dims):
        return lax.dot_general(lhs, rhs, (dims, ((), ())), preferred_element_type=jnp.float32) / total

    half = (feat // 2, Y, 2, block)
    sides = [
        corr.reshape(half).transpose(2, 0, 1, 3).reshape(2, feat // 2, Y * block)
        for corr in (corr_own, corr_other)
    ]
    terms_b = [
        times(sides[0][k], rows_own, ((0,), (0,))) + times(sides[1][k], rows_other, ((0,), (0,)))
        for k in (0, 1)
    ]
    away = terms_b[1].astype(jnp.bfloat16)
    corr_own, corr_other, away = lax.optimization_barrier((corr_own, corr_other, away))
    terms_b = (terms_b[0] + partner(away).astype(jnp.float32)).astype(jnp.bfloat16)
    terms_b = lax.all_to_all(
        terms_b.reshape(Y, block, total), "mp", split_axis=0, concat_axis=0, axis_index_groups=GROUPS
    )
    terms_other = times(corr_other, columns_b, ((1,), (0,))).astype(jnp.bfloat16)
    terms_own = times(corr_own, columns_b, ((1,), (0,)))
    shape = (4, 4, block, total)
    both = terms_own.reshape(shape) + swap(terms_other.reshape(shape), 1).astype(jnp.float32)
    along_x = add(both.astype(jnp.bfloat16), ALONG_X)[0].astype(jnp.bfloat16)
    grad_a, terms_b = add(along_x, STRIDED_Z, terms_b)
    grads = jnp.stack([grad_a, jnp.sum(terms_b.astype(jnp.float32), axis=0)])
    wide = normed.astype(jnp.float32)
    grad_mean = jnp.sum(grads, axis=2, keepdims=True) / total
    cross_mean = jnp.sum(grads * wide, axis=2, keepdims=True) / total
    grad_proj = ((grads - grad_mean - wide * cross_mean) * inverse).astype(jnp.bfloat16)
    grad_proj = grad_proj.transpose(1, 0, 2).reshape(block, views * total)
    along_z, columns = gather(grad_proj, ALONG_Z, columns)
    grad_own = gather(along_z, ALONG_X)[0]
    grad_other = swap(grad_own, 1)
    part = weight_half(grad_own.reshape(feat // 2, views * total), columns)
    return weight_half(grad_other.reshape(feat // 2, views * total), columns, position, part)


def solution(mesh):
    placed = (P(None, "dp", None), P("dp", "mp"))
    return jax.shard_map(
        per_device, mesh=mesh, in_specs=placed, out_specs=P("dp", "mp"), check_vma=False
    )
```

```python
import functools

import jax
import jax.numpy as jnp
from jax import lax
from jax.experimental import pallas as pl
from jax.experimental.pallas import tpu as pltpu
from jax.sharding import PartitionSpec as P

epsilon = 1e-05
redundancy_weight = 0.0051
loss_scale = 512.0
DP = 32
MP = 16
Y = 8
GROUPS = [list(range(Y)), list(range(Y, MP))]
ALONG_X = [(8,), (16,), (24,)]
ALONG_Z = [(2,), (4,), (6,)]
STRIDED_Z = [(4,), (0, 8), (4, 8)]


def swap(array, data, model=0):
    mask = data * MP + model
    return lax.ppermute(array, ("dp", "mp"), [(i, i ^ mask) for i in range(DP * MP)])


def partner(array):
    return swap(array, 2)


def gather(block, masks, *later):
    parts = [block] + [swap(block, *mask) for mask in masks]
    if later:
        parts[1], *later = lax.optimization_barrier((parts[1], *later))
    return jnp.stack(parts), *later


def add(blocks, masks, *later):
    parts = [blocks[0]] + [swap(blocks[k + 1], *mask) for k, mask in enumerate(masks)]
    parts, later = lax.optimization_barrier((parts, later))
    return sum(part.astype(jnp.float32) for part in parts), *later


def project_kernel(last, order_ref, inputs_ref, weight_ref, *refs):
    out_ref = refs[-1]
    blocks, depth, _ = weight_ref.shape
    result = refs[0][...] if last else None
    for k in range(blocks):
        columns = pl.ds(pl.multiple_of(order_ref[k] * depth, depth), depth)
        part = jnp.dot(inputs_ref[:, columns], weight_ref[k], preferred_element_type=jnp.float32)
        result = part if result is None else result + part
    out_ref[...] = result.T if last else result


def project(order, inputs, weight, before=None):
    rows, feat = inputs.shape[0], weight.shape[2]
    operands = (inputs, weight) if before is None else (inputs, weight, before)
    return pl.pallas_call(
        functools.partial(project_kernel, before is not None),
        in_specs=[pl.BlockSpec(memory_space=pltpu.SMEM)]
        + [pl.BlockSpec(memory_space=pltpu.VMEM)] * len(operands),
        out_specs=pl.BlockSpec(memory_space=pltpu.VMEM),
        out_shape=jax.ShapeDtypeStruct((rows, feat) if before is None else (feat, rows), jnp.float32),
        compiler_params=pltpu.CompilerParams(vmem_limit_bytes=32 * 1024 * 1024),
        cost_estimate=pl.CostEstimate(
            flops=2 * rows * feat * weight.shape[0] * weight.shape[1],
            bytes_accessed=6 * 1024 * 1024,
            transcendentals=0,
        ),
    )(order, *operands)


def weight_kernel(last, grad_ref, columns_ref, *refs):
    total_ref = refs[-1]
    step = pl.program_id(0) * pl.num_programs(1) + pl.program_id(1)

    @pl.when(step == 0)
    def _():
        total_ref[...] = jnp.zeros_like(total_ref)

    quarters, devices, share, rows = columns_ref.shape
    pieces = [columns_ref[:, d].reshape(quarters * share, rows) for d in range(devices)]
    columns = jnp.concatenate(pieces, axis=0)
    total_ref[...] += jnp.dot(grad_ref[...], columns, preferred_element_type=jnp.float32)

    if last:
        position_ref, own_ref, out_ref, placed_ref = refs[:4]
        half = own_ref.shape[0]

        @pl.when(step == pl.num_programs(0) * pl.num_programs(1) - 1)
        def _():
            placed_ref[:half] = own_ref[...]
            placed_ref[half:] = total_ref[...]
            blocks = [
                placed_ref[pl.ds(pl.multiple_of(position_ref[block] * 8, 8), 8)] for block in range(DP)
            ]
            out_ref[...] = jnp.concatenate(blocks, axis=0).T


def weight_half(grad, columns, position=None, own=None):
    half, depth = grad.shape
    slices, devices, share, rows = columns.shape
    quarters, group = slices // 2, 8
    last = own is not None
    in_specs = [
        pl.BlockSpec((half, group * quarters * share), lambda v, d: (0, v * (devices // group) + d)),
        pl.BlockSpec((quarters, group, share, rows), lambda v, d: (v, d, 0, 0)),
    ]
    scratch = [pltpu.VMEM((half, rows), jnp.float32)]
    if last:
        in_specs += [
            pl.BlockSpec(memory_space=pltpu.SMEM),
            pl.BlockSpec((half, rows), lambda v, d: (0, 0)),
        ]
        scratch = [pltpu.VMEM((2 * half, rows), jnp.float32)] + scratch
    return pl.pallas_call(
        functools.partial(weight_kernel, last),
        grid=(2, devices // group),
        in_specs=in_specs,
        out_specs=pl.BlockSpec((rows, 2 * half) if last else (half, rows), lambda v, d: (0, 0)),
        out_shape=jax.ShapeDtypeStruct((rows, 2 * half) if last else (half, rows), jnp.float32),
        scratch_shapes=scratch if last else [],
        compiler_params=pltpu.CompilerParams(vmem_limit_bytes=32 * 1024 * 1024),
        cost_estimate=pl.CostEstimate(
            flops=2 * half * depth * rows, bytes_accessed=6 * 1024 * 1024, transcendentals=0
        ),
    )(grad, columns, *((position, own) if last else ()))


def per_device(inputs, weight):
    views, images, width = inputs.shape
    total = images * DP
    data_index = lax.axis_index("dp")
    model_index = lax.axis_index("mp")
    feat = weight.shape[1]
    block = feat // DP
    rows = width // DP
    flat = inputs.reshape(views * images, width)

    place = jnp.arange(DP, dtype=jnp.int32)
    distance = (place >> 4) | ((place >> 2) & 3) << 3 | (place & 3) << 1
    order = data_index ^ distance
    relative = place ^ data_index
    position = (relative & 1) << 4 | (relative >> 3) << 2 | ((relative >> 1) & 3)

    share = views * images // Y
    mine = lax.dynamic_slice_in_dim(flat, lax.rem(model_index, Y) * share, share, axis=0)
    pieces = mine.reshape(share, DP, rows).transpose(1, 0, 2)
    weight_own = gather(gather(weight, ALONG_Z)[0], ALONG_X)[0]
    weight_other = swap(weight_own, 1)
    half = (DP // 2, rows, feat)
    projected = project(order[: DP // 2], flat, weight_own.reshape(half))
    projected = project(order[DP // 2 :], flat, weight_other.reshape(half), projected)

    own = lax.all_to_all(
        projected.reshape(DP, block, views * images), "dp", split_axis=0, concat_axis=0
    ).reshape(DP, block, views, images)
    average = jnp.sum(own, axis=(0, 3), keepdims=True) / total
    centered = own - average
    variance = jnp.sum(centered * centered, axis=(0, 3), keepdims=True) / total
    inverse = lax.rsqrt(variance + epsilon)
    normed = (centered * inverse).astype(jnp.bfloat16).transpose(2, 1, 0, 3).reshape(views, block, total)
    inverse = inverse.reshape(block, views).T[:, :, None]

    second = normed[1]
    pair = jnp.stack([second, partner(second)])
    first, pair = lax.optimization_barrier((normed[0], pair))
    columns_b = lax.all_gather(pair, "mp", axis=0, axis_index_groups=GROUPS)
    columns_b = columns_b.reshape(MP * block, total)
    along_z, pieces = gather(first, STRIDED_Z, pieces)
    slices = lax.all_to_all(pieces, "dp", split_axis=0, concat_axis=0)
    rows_own = gather(along_z, ALONG_X)[0]
    rows_own, columns_b, slices = lax.optimization_barrier((rows_own, columns_b, slices))
    columns = lax.all_gather(slices, "mp", axis=0, axis_index_groups=GROUPS)
    rows_other = swap(rows_own, 1).reshape(feat // 2, total)
    rows_own = rows_own.reshape(feat // 2, total)

    def gradient_of(rows_a, with_diagonal):
        correlation = (
            lax.dot_general(rows_a, columns_b, (((1,), (1,)), ((), ())), preferred_element_type=jnp.float32)
            / total
        )
        inner = 2.0 * redundancy_weight * correlation
        if with_diagonal:
            row = lax.broadcasted_iota(jnp.int32, correlation.shape, 0)
            column = lax.broadcasted_iota(jnp.int32, correlation.shape, 1)
            diagonal = (row < block) & (column == lax.rem(model_index, Y) * 2 * block + row)
            inner = inner + diagonal.astype(jnp.float32) * (2.0 * (correlation - 1.0) - inner)
        return (loss_scale * inner).astype(jnp.bfloat16)

    corr_own = gradient_of(rows_own, True)
    corr_other = gradient_of(rows_other, False)

    def times(lhs, rhs, dims):
        return lax.dot_general(lhs, rhs, (dims, ((), ())), preferred_element_type=jnp.float32) / total

    half = (feat // 2, Y, 2, block)
    sides = [
        corr.reshape(half).transpose(2, 0, 1, 3).reshape(2, feat // 2, Y * block)
        for corr in (corr_own, corr_other)
    ]
    terms_b = [
        times(sides[0][k], rows_own, ((0,), (0,))) + times(sides[1][k], rows_other, ((0,), (0,)))
        for k in (0, 1)
    ]
    away = terms_b[1].astype(jnp.bfloat16)
    corr_own, corr_other, away = lax.optimization_barrier((corr_own, corr_other, away))
    terms_b = (terms_b[0] + partner(away).astype(jnp.float32)).astype(jnp.bfloat16)
    terms_b = lax.all_to_all(
        terms_b.reshape(Y, block, total), "mp", split_axis=0, concat_axis=0, axis_index_groups=GROUPS
    )
    terms_other = times(corr_other, columns_b, ((1,), (0,))).astype(jnp.bfloat16)
    terms_own = times(corr_own, columns_b, ((1,), (0,)))
    shape = (4, 4, block, total)
    both = terms_own.reshape(shape) + swap(terms_other.reshape(shape), 1).astype(jnp.float32)
    along_x = add(both.astype(jnp.bfloat16), ALONG_X)[0].astype(jnp.bfloat16)
    grad_a, terms_b = add(along_x, STRIDED_Z, terms_b)
    grads = jnp.stack([grad_a, jnp.sum(terms_b.astype(jnp.float32), axis=0)])
    wide = normed.astype(jnp.float32)
    grad_mean = jnp.sum(grads, axis=2, keepdims=True) / total
    cross_mean = jnp.sum(grads * wide, axis=2, keepdims=True) / total
    grad_proj = ((grads - grad_mean - wide * cross_mean) * inverse).astype(jnp.bfloat16)
    grad_proj = grad_proj.transpose(1, 0, 2).reshape(block, views * total)
    along_z, columns = gather(grad_proj, ALONG_Z, columns)
    grad_own = gather(along_z, ALONG_X)[0]
    grad_other = swap(grad_own, 1)
    part = weight_half(grad_own.reshape(feat // 2, views * total), columns)
    return weight_half(grad_other.reshape(feat // 2, views * total), columns, position, part)


def solution(mesh):
    placed = (P(None, "dp", None), P("dp", "mp"))
    return jax.shard_map(
        per_device, mesh=mesh, in_specs=placed, out_specs=P("dp", "mp"), check_vma=False
    )
```

```python
import functools

import jax
import jax.numpy as jnp
from jax import lax
from jax.experimental import pallas as pl
from jax.experimental.pallas import tpu as pltpu
from jax.sharding import PartitionSpec as P

epsilon = 1e-05
redundancy_weight = 0.0051
loss_scale = 512.0
DP = 32
MP = 16
Y = 8
GROUPS = [list(range(Y)), list(range(Y, MP))]
ALONG_X = [(8,), (16,), (24,)]
ALONG_Z = [(2,), (4,), (6,)]
STRIDED_Z = [(4,), (0, 8), (4, 8)]


def swap(array, data, model=0):
    mask = data * MP + model
    return lax.ppermute(array, ("dp", "mp"), [(i, i ^ mask) for i in range(DP * MP)])


def partner(array):
    return swap(array, 2)


def gather(block, masks, *later):
    parts = [block] + [swap(block, *mask) for mask in masks]
    if later:
        parts[1], *later = lax.optimization_barrier((parts[1], *later))
    return jnp.stack(parts), *later


def add(blocks, masks, *later):
    parts = [blocks[0]] + [swap(blocks[k + 1], *mask) for k, mask in enumerate(masks)]
    parts, later = lax.optimization_barrier((parts, later))
    return sum(part.astype(jnp.float32) for part in parts), *later


def project_kernel(last, order_ref, inputs_ref, weight_ref, *refs):
    out_ref = refs[-1]
    blocks, depth, _ = weight_ref.shape
    result = refs[0][...] if last else None
    for k in range(blocks):
        columns = pl.ds(pl.multiple_of(order_ref[k] * depth, depth), depth)
        part = jnp.dot(inputs_ref[:, columns], weight_ref[k], preferred_element_type=jnp.float32)
        result = part if result is None else result + part
    out_ref[...] = result.T if last else result


def project(order, inputs, weight, before=None):
    rows, feat = inputs.shape[0], weight.shape[2]
    operands = (inputs, weight) if before is None else (inputs, weight, before)
    return pl.pallas_call(
        functools.partial(project_kernel, before is not None),
        in_specs=[pl.BlockSpec(memory_space=pltpu.SMEM)]
        + [pl.BlockSpec(memory_space=pltpu.VMEM)] * len(operands),
        out_specs=pl.BlockSpec(memory_space=pltpu.VMEM),
        out_shape=jax.ShapeDtypeStruct((rows, feat) if before is None else (feat, rows), jnp.float32),
        compiler_params=pltpu.CompilerParams(vmem_limit_bytes=32 * 1024 * 1024),
        cost_estimate=pl.CostEstimate(
            flops=2 * rows * feat * weight.shape[0] * weight.shape[1],
            bytes_accessed=6 * 1024 * 1024,
            transcendentals=0,
        ),
    )(order, *operands)


def weight_kernel(last, grad_ref, columns_ref, *refs):
    total_ref = refs[-1]
    step = pl.program_id(0) * pl.num_programs(1) + pl.program_id(1)

    @pl.when(step == 0)
    def _():
        total_ref[...] = jnp.zeros_like(total_ref)

    quarters, devices, share, rows = columns_ref.shape
    pieces = [columns_ref[:, d].reshape(quarters * share, rows) for d in range(devices)]
    columns = jnp.concatenate(pieces, axis=0)
    total_ref[...] += jnp.dot(grad_ref[...], columns, preferred_element_type=jnp.float32)

    if last:
        position_ref, own_ref, out_ref, placed_ref = refs[:4]
        half = own_ref.shape[0]

        @pl.when(step == pl.num_programs(0) * pl.num_programs(1) - 1)
        def _():
            placed_ref[:half] = own_ref[...]
            placed_ref[half:] = total_ref[...]
            blocks = [
                placed_ref[pl.ds(pl.multiple_of(position_ref[block] * 8, 8), 8)] for block in range(DP)
            ]
            out_ref[...] = jnp.concatenate(blocks, axis=0).T


def weight_half(grad, columns, position=None, own=None):
    half, depth = grad.shape
    slices, devices, share, rows = columns.shape
    quarters, group = slices // 2, 8
    last = own is not None
    in_specs = [
        pl.BlockSpec((half, group * quarters * share), lambda v, d: (0, v * (devices // group) + d)),
        pl.BlockSpec((quarters, group, share, rows), lambda v, d: (v, d, 0, 0)),
    ]
    scratch = [pltpu.VMEM((half, rows), jnp.float32)]
    if last:
        in_specs += [
            pl.BlockSpec(memory_space=pltpu.SMEM),
            pl.BlockSpec((half, rows), lambda v, d: (0, 0)),
        ]
        scratch = [pltpu.VMEM((2 * half, rows), jnp.float32)] + scratch
    return pl.pallas_call(
        functools.partial(weight_kernel, last),
        grid=(2, devices // group),
        in_specs=in_specs,
        out_specs=pl.BlockSpec((rows, 2 * half) if last else (half, rows), lambda v, d: (0, 0)),
        out_shape=jax.ShapeDtypeStruct((rows, 2 * half) if last else (half, rows), jnp.float32),
        scratch_shapes=scratch if last else [],
        compiler_params=pltpu.CompilerParams(vmem_limit_bytes=32 * 1024 * 1024),
        cost_estimate=pl.CostEstimate(
            flops=2 * half * depth * rows, bytes_accessed=6 * 1024 * 1024, transcendentals=0
        ),
    )(grad, columns, *((position, own) if last else ()))


def per_device(inputs, weight):
    views, images, width = inputs.shape
    total = images * DP
    data_index = lax.axis_index("dp")
    model_index = lax.axis_index("mp")
    feat = weight.shape[1]
    block = feat // DP
    rows = width // DP
    flat = inputs.reshape(views * images, width)

    place = jnp.arange(DP, dtype=jnp.int32)
    distance = (place >> 4) | ((place >> 2) & 3) << 3 | (place & 3) << 1
    order = data_index ^ distance
    relative = place ^ data_index
    position = (relative & 1) << 4 | (relative >> 3) << 2 | ((relative >> 1) & 3)

    share = views * images // Y
    mine = lax.dynamic_slice_in_dim(flat, lax.rem(model_index, Y) * share, share, axis=0)
    pieces = mine.reshape(share, DP, rows).transpose(1, 0, 2)
    weight_own = gather(gather(weight, ALONG_Z)[0], ALONG_X)[0]
    weight_other = swap(weight_own, 1)
    half = (DP // 2, rows, feat)
    projected = project(order[: DP // 2], flat, weight_own.reshape(half))
    projected = project(order[DP // 2 :], flat, weight_other.reshape(half), projected)

    own = lax.all_to_all(
        projected.reshape(DP, block, views * images), "dp", split_axis=0, concat_axis=0
    ).reshape(DP, block, views, images)
    average = jnp.sum(own, axis=(0, 3), keepdims=True) / total
    centered = own - average
    variance = jnp.sum(centered * centered, axis=(0, 3), keepdims=True) / total
    inverse = lax.rsqrt(variance + epsilon)
    normed = (centered * inverse).astype(jnp.bfloat16).transpose(2, 1, 0, 3).reshape(views, block, total)
    inverse = inverse.reshape(block, views).T[:, :, None]

    second = normed[1]
    pair = jnp.stack([second, partner(second)])
    first, pair, pieces = lax.optimization_barrier((normed[0], pair, pieces))
    slices = lax.all_to_all(pieces, "dp", split_axis=0, concat_axis=0)
    columns_b = lax.all_gather(pair, "mp", axis=0, axis_index_groups=GROUPS)
    columns_b = columns_b.reshape(MP * block, total)
    rows_own = gather(gather(first, STRIDED_Z)[0], ALONG_X)[0]
    rows_own, columns_b, slices = lax.optimization_barrier((rows_own, columns_b, slices))
    columns = lax.all_gather(slices, "mp", axis=0, axis_index_groups=GROUPS)
    rows_other = swap(rows_own, 1).reshape(feat // 2, total)
    rows_own = rows_own.reshape(feat // 2, total)

    def gradient_of(rows_a, with_diagonal):
        correlation = (
            lax.dot_general(rows_a, columns_b, (((1,), (1,)), ((), ())), preferred_element_type=jnp.float32)
            / total
        )
        inner = 2.0 * redundancy_weight * correlation
        if with_diagonal:
            row = lax.broadcasted_iota(jnp.int32, correlation.shape, 0)
            column = lax.broadcasted_iota(jnp.int32, correlation.shape, 1)
            diagonal = (row < block) & (column == lax.rem(model_index, Y) * 2 * block + row)
            inner = inner + diagonal.astype(jnp.float32) * (2.0 * (correlation - 1.0) - inner)
        return (loss_scale * inner).astype(jnp.bfloat16)

    corr_own = gradient_of(rows_own, True)
    corr_other = gradient_of(rows_other, False)

    def times(lhs, rhs, dims):
        return lax.dot_general(lhs, rhs, (dims, ((), ())), preferred_element_type=jnp.float32) / total

    half = (feat // 2, Y, 2, block)
    sides = [
        corr.reshape(half).transpose(2, 0, 1, 3).reshape(2, feat // 2, Y * block)
        for corr in (corr_own, corr_other)
    ]
    terms_b = [
        times(sides[0][k], rows_own, ((0,), (0,))) + times(sides[1][k], rows_other, ((0,), (0,)))
        for k in (0, 1)
    ]
    away = terms_b[1].astype(jnp.bfloat16)
    corr_own, corr_other, away = lax.optimization_barrier((corr_own, corr_other, away))
    terms_b = (terms_b[0] + partner(away).astype(jnp.float32)).astype(jnp.bfloat16)
    terms_b = lax.all_to_all(
        terms_b.reshape(Y, block, total), "mp", split_axis=0, concat_axis=0, axis_index_groups=GROUPS
    )
    terms_other = times(corr_other, columns_b, ((1,), (0,))).astype(jnp.bfloat16)
    terms_own = times(corr_own, columns_b, ((1,), (0,)))
    shape = (4, 4, block, total)
    both = terms_own.reshape(shape) + swap(terms_other.reshape(shape), 1).astype(jnp.float32)
    along_x = add(both.astype(jnp.bfloat16), ALONG_X)[0].astype(jnp.bfloat16)
    grad_a, terms_b = add(along_x, STRIDED_Z, terms_b)
    grads = jnp.stack([grad_a, jnp.sum(terms_b.astype(jnp.float32), axis=0)])
    wide = normed.astype(jnp.float32)
    grad_mean = jnp.sum(grads, axis=2, keepdims=True) / total
    cross_mean = jnp.sum(grads * wide, axis=2, keepdims=True) / total
    grad_proj = ((grads - grad_mean - wide * cross_mean) * inverse).astype(jnp.bfloat16)
    grad_proj = grad_proj.transpose(1, 0, 2).reshape(block, views * total)
    along_z, columns = gather(grad_proj, ALONG_Z, columns)
    grad_own = gather(along_z, ALONG_X)[0]
    grad_other = swap(grad_own, 1)
    part = weight_half(grad_own.reshape(feat // 2, views * total), columns)
    return weight_half(grad_other.reshape(feat // 2, views * total), columns, position, part)


def solution(mesh):
    placed = (P(None, "dp", None), P("dp", "mp"))
    return jax.shard_map(
        per_device, mesh=mesh, in_specs=placed, out_specs=P("dp", "mp"), check_vma=False
    )
```

```python
import functools

import jax
import jax.numpy as jnp
from jax import lax
from jax.experimental import pallas as pl
from jax.experimental.pallas import tpu as pltpu
from jax.sharding import PartitionSpec as P

epsilon = 1e-05
redundancy_weight = 0.0051
loss_scale = 512.0
DP = 32
MP = 16
Y = 8
X = 4
GROUPS = [list(range(Y)), list(range(Y, MP))]
SAME_REST = [list(range(g, DP, DP // X)) for g in range(DP // X)]
SAME_X = [list(range(x * DP // X, (x + 1) * DP // X)) for x in range(X)]
ALONG_X = [(8,), (16,), (24,)]
ALONG_Z = [(2,), (4,), (6,)]
STRIDED_Z = [(4,), (0, 8), (4, 8)]


def swap(array, data, model=0):
    mask = data * MP + model
    return lax.ppermute(array, ("dp", "mp"), [(i, i ^ mask) for i in range(DP * MP)])


def partner(array):
    return swap(array, 2)


def gather(block, masks, *later):
    parts = [block] + [swap(block, *mask) for mask in masks]
    if later:
        parts[1], *later = lax.optimization_barrier((parts[1], *later))
    return jnp.stack(parts), *later


def add(blocks, masks, *later):
    parts = [blocks[0]] + [swap(blocks[k + 1], *mask) for k, mask in enumerate(masks)]
    parts, later = lax.optimization_barrier((parts, later))
    return sum(part.astype(jnp.float32) for part in parts), *later


def project_kernel(last, order_ref, inputs_ref, weight_ref, *refs):
    out_ref = refs[-1]
    blocks, depth, _ = weight_ref.shape
    result = refs[0][...] if last else None
    for k in range(blocks):
        columns = pl.ds(pl.multiple_of(order_ref[k] * depth, depth), depth)
        part = jnp.dot(inputs_ref[:, columns], weight_ref[k], preferred_element_type=jnp.float32)
        result = part if result is None else result + part
    out_ref[...] = result.T if last else result


def project(order, inputs, weight, before=None):
    rows, feat = inputs.shape[0], weight.shape[2]
    operands = (inputs, weight) if before is None else (inputs, weight, before)
    return pl.pallas_call(
        functools.partial(project_kernel, before is not None),
        in_specs=[pl.BlockSpec(memory_space=pltpu.SMEM)]
        + [pl.BlockSpec(memory_space=pltpu.VMEM)] * len(operands),
        out_specs=pl.BlockSpec(memory_space=pltpu.VMEM),
        out_shape=jax.ShapeDtypeStruct((rows, feat) if before is None else (feat, rows), jnp.float32),
        compiler_params=pltpu.CompilerParams(vmem_limit_bytes=32 * 1024 * 1024),
        cost_estimate=pl.CostEstimate(
            flops=2 * rows * feat * weight.shape[0] * weight.shape[1],
            bytes_accessed=6 * 1024 * 1024,
            transcendentals=0,
        ),
    )(order, *operands)


def weight_kernel(grad_ref, columns_ref, *refs):
    *before, out_ref = refs
    slices, devices, share, rows = columns_ref.shape
    half = slices // 2
    pieces = [
        columns_ref[half * view : half * (view + 1), d].reshape(half * share, rows)
        for view in range(2)
        for d in range(devices)
    ]
    columns = jnp.concatenate(pieces, axis=0)
    result = jnp.dot(grad_ref[...], columns, preferred_element_type=jnp.float32)
    if before:
        features = result.shape[0]
        out_ref[0, :features] = before[0][0]
        out_ref[0, features:] = result
    else:
        out_ref[0] = result


def weight_half(grad, columns, before=()):
    half, depth = grad.shape
    slices, devices, share, wide = columns.shape
    rows = wide // X
    features = half * (len(before) + 1)
    return pl.pallas_call(
        weight_kernel,
        grid=(X,),
        in_specs=[
            pl.BlockSpec((half, depth), lambda x: (0, 0)),
            pl.BlockSpec((slices, devices, share, rows), lambda x: (0, 0, 0, x)),
        ]
        + [pl.BlockSpec((1, half, rows), lambda x: (x, 0, 0))] * len(before),
        out_specs=pl.BlockSpec((1, features, rows), lambda x: (x, 0, 0)),
        out_shape=jax.ShapeDtypeStruct((X, features, rows), jnp.float32),
        compiler_params=pltpu.CompilerParams(vmem_limit_bytes=32 * 1024 * 1024),
        cost_estimate=pl.CostEstimate(
            flops=2 * half * depth * wide, bytes_accessed=5 * 1024 * 1024, transcendentals=0
        ),
    )(grad, columns, *before)


def finish_kernel(position_ref, terms_ref, out_ref, total_ref):
    total_ref[...] = (terms_ref[0] + terms_ref[1]) + (terms_ref[2] + terms_ref[3])
    blocks = [total_ref[pl.ds(pl.multiple_of(position_ref[j] * 8, 8), 8)] for j in range(DP)]
    out_ref[...] = jnp.concatenate(blocks, axis=0).T


def finish(position, terms):
    _, features, rows = terms.shape
    return pl.pallas_call(
        finish_kernel,
        in_specs=[pl.BlockSpec(memory_space=pltpu.SMEM), pl.BlockSpec(memory_space=pltpu.VMEM)],
        out_specs=pl.BlockSpec(memory_space=pltpu.VMEM),
        out_shape=jax.ShapeDtypeStruct((rows, features), jnp.float32),
        scratch_shapes=[pltpu.VMEM((features, rows), jnp.float32)],
        compiler_params=pltpu.CompilerParams(vmem_limit_bytes=32 * 1024 * 1024),
    )(position, terms)


def per_device(inputs, weight):
    views, images, width = inputs.shape
    total = images * DP
    data_index = lax.axis_index("dp")
    model_index = lax.axis_index("mp")
    feat = weight.shape[1]
    block = feat // DP
    rows = width // DP
    flat = inputs.reshape(views * images, width)

    place = jnp.arange(DP, dtype=jnp.int32)
    distance = (place >> 4) | ((place >> 2) & 3) << 3 | (place & 3) << 1
    order = data_index ^ distance
    relative = place ^ data_index
    position = (relative & 1) << 4 | ((relative >> 1) & 3) << 2 | (place >> 3)

    share = views * images // Y
    mine = lax.dynamic_slice_in_dim(flat, lax.rem(model_index, Y) * share, share, axis=0)
    pieces = mine.reshape(share, X, DP // X, rows).transpose(2, 0, 1, 3).reshape(DP // X, share, X * rows)
    weight_own = gather(gather(weight, ALONG_Z)[0], ALONG_X)[0]
    weight_other = swap(weight_own, 1)
    half = (DP // 2, rows, feat)
    projected = project(order[: DP // 2], flat, weight_own.reshape(half))
    projected = project(order[DP // 2 :], flat, weight_other.reshape(half), projected)

    own = lax.all_to_all(
        projected.reshape(DP, block, views * images), "dp", split_axis=0, concat_axis=0
    ).reshape(DP, block, views, images)
    average = jnp.sum(own, axis=(0, 3), keepdims=True) / total
    centered = own - average
    variance = jnp.sum(centered * centered, axis=(0, 3), keepdims=True) / total
    inverse = lax.rsqrt(variance + epsilon)
    normed = (centered * inverse).astype(jnp.bfloat16).transpose(2, 1, 0, 3).reshape(views, block, total)
    inverse = inverse.reshape(block, views).T[:, :, None]

    second = normed[1]
    pair = jnp.stack([second, partner(second)])
    first, pair, pieces = lax.optimization_barrier((normed[0], pair, pieces))
    slices = lax.all_to_all(
        pieces, "dp", split_axis=0, concat_axis=0, axis_index_groups=SAME_X
    )
    columns_b = lax.all_gather(pair, "mp", axis=0, axis_index_groups=GROUPS)
    columns_b = columns_b.reshape(MP * block, total)
    rows_own = gather(gather(first, STRIDED_Z)[0], ALONG_X)[0]
    rows_own, columns_b, slices = lax.optimization_barrier((rows_own, columns_b, slices))
    columns = lax.all_gather(slices, "mp", axis=0, axis_index_groups=GROUPS)
    rows_other = swap(rows_own, 1).reshape(feat // 2, total)
    rows_own = rows_own.reshape(feat // 2, total)

    def gradient_of(rows_a, with_diagonal):
        correlation = (
            lax.dot_general(rows_a, columns_b, (((1,), (1,)), ((), ())), preferred_element_type=jnp.float32)
            / total
        )
        inner = 2.0 * redundancy_weight * correlation
        if with_diagonal:
            row = lax.broadcasted_iota(jnp.int32, correlation.shape, 0)
            column = lax.broadcasted_iota(jnp.int32, correlation.shape, 1)
            diagonal = (row < block) & (column == lax.rem(model_index, Y) * 2 * block + row)
            inner = inner + diagonal.astype(jnp.float32) * (2.0 * (correlation - 1.0) - inner)
        return (loss_scale * inner).astype(jnp.bfloat16)

    corr_own = gradient_of(rows_own, True)
    corr_other = gradient_of(rows_other, False)

    def times(lhs, rhs, dims):
        return lax.dot_general(lhs, rhs, (dims, ((), ())), preferred_element_type=jnp.float32) / total

    half = (feat // 2, Y, 2, block)
    sides = [
        corr.reshape(half).transpose(2, 0, 1, 3).reshape(2, feat // 2, Y * block)
        for corr in (corr_own, corr_other)
    ]
    terms_b = [
        times(sides[0][k], rows_own, ((0,), (0,))) + times(sides[1][k], rows_other, ((0,), (0,)))
        for k in (0, 1)
    ]
    away = terms_b[1].astype(jnp.bfloat16)
    corr_own, corr_other, away = lax.optimization_barrier((corr_own, corr_other, away))
    terms_b = (terms_b[0] + partner(away).astype(jnp.float32)).astype(jnp.bfloat16)
    terms_b = lax.all_to_all(
        terms_b.reshape(Y, block, total), "mp", split_axis=0, concat_axis=0, axis_index_groups=GROUPS
    )
    terms_other = times(corr_other, columns_b, ((1,), (0,))).astype(jnp.bfloat16)
    terms_own = times(corr_own, columns_b, ((1,), (0,)))
    shape = (4, 4, block, total)
    both = terms_own.reshape(shape) + swap(terms_other.reshape(shape), 1).astype(jnp.float32)
    along_x = add(both.astype(jnp.bfloat16), ALONG_X)[0].astype(jnp.bfloat16)
    grad_a, terms_b = add(along_x, STRIDED_Z, terms_b)
    grads = jnp.stack([grad_a, jnp.sum(terms_b.astype(jnp.float32), axis=0)])
    wide = normed.astype(jnp.float32)
    grad_mean = jnp.sum(grads, axis=2, keepdims=True) / total
    cross_mean = jnp.sum(grads * wide, axis=2, keepdims=True) / total
    grad_proj = ((grads - grad_mean - wide * cross_mean) * inverse).astype(jnp.bfloat16)
    images_x = total // X
    depth = views * images_x
    grad_proj = jnp.stack(
        [
            jnp.concatenate(
                [grad_proj[v, :, x * images_x : (x + 1) * images_x] for v in range(views)], axis=1
            )
            for x in range(X)
        ]
    )
    grad_proj = lax.all_to_all(
        grad_proj, "dp", split_axis=0, concat_axis=0, axis_index_groups=SAME_REST
    )
    grad_own, columns = gather(grad_proj, ALONG_Z, columns)
    grad_other = swap(grad_own, 1)
    terms = weight_half(grad_own.reshape(feat // 2, depth), columns)
    terms = weight_half(grad_other.reshape(feat // 2, depth), columns, (terms,))
    terms = lax.all_to_all(
        terms, "dp", split_axis=0, concat_axis=0, axis_index_groups=SAME_REST
    )
    return finish(position, terms)


def solution(mesh):
    placed = (P(None, "dp", None), P("dp", "mp"))
    return jax.shard_map(
        per_device, mesh=mesh, in_specs=placed, out_specs=P("dp", "mp"), check_vma=False
    )
```

```python
import functools

import jax
import jax.numpy as jnp
import numpy as np
from jax import lax
from jax.experimental import pallas as pl
from jax.experimental.pallas import tpu as pltpu
from jax.sharding import PartitionSpec as P

epsilon = 1e-05
redundancy_weight = 0.0051
loss_scale = 512.0
DP = 32
MP = 16
Y = 8
X = 4
GROUPS = [list(range(Y)), list(range(Y, MP))]
SAME_REST = [list(range(g, DP, DP // X)) for g in range(DP // X)]
SAME_X = [list(range(x * DP // X, (x + 1) * DP // X)) for x in range(X)]
X_SLOTS = np.array([0, 2, 1, 3])
Z_SLOTS = np.array([0, 3, 2, 1])
ALONG_X = [(8 * int(k),) for k in X_SLOTS[1:]]
ALONG_Z = [(2 * int(k),) for k in Z_SLOTS[1:]]
STRIDED_Z = [(4,), (0, 8), (4, 8)]


def swap(array, data, model=0):
    mask = data * MP + model
    return lax.ppermute(array, ("dp", "mp"), [(i, i ^ mask) for i in range(DP * MP)])


def partner(array):
    return swap(array, 2)


def gather(block, masks, *later):
    parts = [block] + [swap(block, *mask) for mask in masks]
    if later:
        parts[1], *later = lax.optimization_barrier((parts[1], *later))
    return jnp.stack(parts), *later


def add(blocks, masks, *later):
    parts = [blocks[0]] + [swap(blocks[k + 1], *mask) for k, mask in enumerate(masks)]
    parts, later = lax.optimization_barrier((parts, later))
    return sum(part.astype(jnp.float32) for part in parts), *later


def project_kernel(last, order_ref, inputs_ref, weight_ref, *refs):
    out_ref = refs[-1]
    blocks, depth, _ = weight_ref.shape
    result = refs[0][...] if last else None
    for k in range(blocks):
        columns = pl.ds(pl.multiple_of(order_ref[k] * depth, depth), depth)
        part = jnp.dot(inputs_ref[:, columns], weight_ref[k], preferred_element_type=jnp.float32)
        result = part if result is None else result + part
    out_ref[...] = result.T if last else result


def project(order, inputs, weight, before=None):
    rows, feat = inputs.shape[0], weight.shape[2]
    operands = (inputs, weight) if before is None else (inputs, weight, before)
    return pl.pallas_call(
        functools.partial(project_kernel, before is not None),
        in_specs=[pl.BlockSpec(memory_space=pltpu.SMEM)]
        + [pl.BlockSpec(memory_space=pltpu.VMEM)] * len(operands),
        out_specs=pl.BlockSpec(memory_space=pltpu.VMEM),
        out_shape=jax.ShapeDtypeStruct((rows, feat) if before is None else (feat, rows), jnp.float32),
        compiler_params=pltpu.CompilerParams(vmem_limit_bytes=16 * 1024 * 1024),
        cost_estimate=pl.CostEstimate(
            flops=2 * rows * feat * weight.shape[0] * weight.shape[1],
            bytes_accessed=6 * 1024 * 1024,
            transcendentals=0,
        ),
    )(order, *operands)


def weight_kernel(grad_ref, columns_ref, *refs):
    *before, out_ref = refs
    slices, devices, share, rows = columns_ref.shape
    half = slices // 2
    pieces = [
        columns_ref[half * view : half * (view + 1), d].reshape(half * share, rows)
        for view in range(2)
        for d in range(devices)
    ]
    columns = jnp.concatenate(pieces, axis=0)
    result = jnp.dot(grad_ref[...], columns, preferred_element_type=jnp.float32)
    if before:
        features = result.shape[0]
        out_ref[0, :features] = before[0][0]
        out_ref[0, features:] = result
    else:
        out_ref[0] = result


def weight_half(grad, columns, before=()):
    half, depth = grad.shape
    slices, devices, share, wide = columns.shape
    rows = wide // X
    features = half * (len(before) + 1)
    return pl.pallas_call(
        weight_kernel,
        grid=(X,),
        in_specs=[
            pl.BlockSpec((half, depth), lambda x: (0, 0)),
            pl.BlockSpec((slices, devices, share, rows), lambda x: (0, 0, 0, x)),
        ]
        + [pl.BlockSpec((1, half, rows), lambda x: (x, 0, 0))] * len(before),
        out_specs=pl.BlockSpec((1, features, rows), lambda x: (x, 0, 0)),
        out_shape=jax.ShapeDtypeStruct((X, features, rows), jnp.float32),
        compiler_params=pltpu.CompilerParams(vmem_limit_bytes=16 * 1024 * 1024),
        cost_estimate=pl.CostEstimate(
            flops=2 * half * depth * wide, bytes_accessed=5 * 1024 * 1024, transcendentals=0
        ),
    )(grad, columns, *before)


def finish_kernel(position_ref, terms_ref, out_ref, total_ref):
    total_ref[...] = (terms_ref[0] + terms_ref[1]) + (terms_ref[2] + terms_ref[3])
    blocks = [total_ref[pl.ds(pl.multiple_of(position_ref[j] * 8, 8), 8)] for j in range(DP)]
    out_ref[...] = jnp.concatenate(blocks, axis=0).T


def finish(position, terms):
    _, features, rows = terms.shape
    return pl.pallas_call(
        finish_kernel,
        in_specs=[pl.BlockSpec(memory_space=pltpu.SMEM), pl.BlockSpec(memory_space=pltpu.VMEM)],
        out_specs=pl.BlockSpec(memory_space=pltpu.VMEM),
        out_shape=jax.ShapeDtypeStruct((rows, features), jnp.float32),
        scratch_shapes=[pltpu.VMEM((features, rows), jnp.float32)],
        compiler_params=pltpu.CompilerParams(vmem_limit_bytes=16 * 1024 * 1024),
    )(position, terms)


def per_device(inputs, weight):
    views, images, width = inputs.shape
    total = images * DP
    data_index = lax.axis_index("dp")
    model_index = lax.axis_index("mp")
    feat = weight.shape[1]
    block = feat // DP
    rows = width // DP
    flat = inputs.reshape(views * images, width)

    place = np.arange(DP)
    distance = place >> 4 | X_SLOTS[place >> 2 & 3] << 3 | Z_SLOTS[place & 3] << 1
    order = data_index ^ jnp.asarray(distance, jnp.int32)
    relative = data_index ^ jnp.asarray(place, jnp.int32)
    slot = (4 - (relative >> 1 & 3)) & 3
    position = (relative & 1) << 4 | slot << 2 | jnp.asarray(place >> 3, jnp.int32)

    share = views * images // Y
    mine = lax.dynamic_slice_in_dim(flat, lax.rem(model_index, Y) * share, share, axis=0)
    pieces = mine.reshape(share, X, DP // X, rows).transpose(2, 0, 1, 3).reshape(DP // X, share, X * rows)
    weight_own = gather(gather(weight, ALONG_Z)[0], ALONG_X)[0]
    weight_other = swap(weight_own, 1)
    half = (DP // 2, rows, feat)
    projected = project(order[: DP // 2], flat, weight_own.reshape(half))
    projected = project(order[DP // 2 :], flat, weight_other.reshape(half), projected)

    own = lax.all_to_all(
        projected.reshape(DP, block, views * images), "dp", split_axis=0, concat_axis=0
    ).reshape(DP, block, views, images)
    average = jnp.sum(own, axis=(0, 3), keepdims=True) / total
    centered = own - average
    variance = jnp.sum(centered * centered, axis=(0, 3), keepdims=True) / total
    inverse = lax.rsqrt(variance + epsilon)
    normed = (centered * inverse).astype(jnp.bfloat16).transpose(2, 1, 0, 3).reshape(views, block, total)
    inverse = inverse.reshape(block, views).T[:, :, None]

    second = normed[1]
    pair = jnp.stack([second, partner(second)])
    first, pair, pieces = lax.optimization_barrier((normed[0], pair, pieces))
    slices = lax.all_to_all(
        pieces, "dp", split_axis=0, concat_axis=0, axis_index_groups=SAME_X
    )
    columns_b = lax.all_gather(pair, "mp", axis=0, axis_index_groups=GROUPS)
    columns_b = columns_b.reshape(MP * block, total)
    rows_own = gather(gather(first, STRIDED_Z)[0], ALONG_X)[0]
    rows_own, columns_b, slices = lax.optimization_barrier((rows_own, columns_b, slices))
    columns = lax.all_gather(slices, "mp", axis=0, axis_index_groups=GROUPS)
    rows_other = swap(rows_own, 1).reshape(feat // 2, total)
    rows_own = rows_own.reshape(feat // 2, total)

    def gradient_of(rows_a, with_diagonal):
        correlation = (
            lax.dot_general(rows_a, columns_b, (((1,), (1,)), ((), ())), preferred_element_type=jnp.float32)
            / total
        )
        inner = 2.0 * redundancy_weight * correlation
        if with_diagonal:
            row = lax.broadcasted_iota(jnp.int32, correlation.shape, 0)
            column = lax.broadcasted_iota(jnp.int32, correlation.shape, 1)
            diagonal = (row < block) & (column == lax.rem(model_index, Y) * 2 * block + row)
            inner = inner + diagonal.astype(jnp.float32) * (2.0 * (correlation - 1.0) - inner)
        return (loss_scale * inner).astype(jnp.bfloat16)

    corr_own = gradient_of(rows_own, True)
    corr_other = gradient_of(rows_other, False)

    def times(lhs, rhs, dims):
        return lax.dot_general(lhs, rhs, (dims, ((), ())), preferred_element_type=jnp.float32) / total

    half = (feat // 2, Y, 2, block)
    sides = [
        corr.reshape(half).transpose(2, 0, 1, 3).reshape(2, feat // 2, Y * block)
        for corr in (corr_own, corr_other)
    ]
    terms_b = [
        times(sides[0][k], rows_own, ((0,), (0,))) + times(sides[1][k], rows_other, ((0,), (0,)))
        for k in (0, 1)
    ]
    away = terms_b[1].astype(jnp.bfloat16)
    corr_own, corr_other, away = lax.optimization_barrier((corr_own, corr_other, away))
    terms_b = (terms_b[0] + partner(away).astype(jnp.float32)).astype(jnp.bfloat16)
    terms_b = lax.all_to_all(
        terms_b.reshape(Y, block, total), "mp", split_axis=0, concat_axis=0, axis_index_groups=GROUPS
    )
    terms_other = times(corr_other, columns_b, ((1,), (0,))).astype(jnp.bfloat16)
    terms_own = times(corr_own, columns_b, ((1,), (0,)))
    shape = (4, 4, block, total)
    both = terms_own.reshape(shape) + swap(terms_other.reshape(shape), 1).astype(jnp.float32)
    along_x = add(both.astype(jnp.bfloat16), ALONG_X)[0].astype(jnp.bfloat16)
    grad_a, terms_b = add(along_x, STRIDED_Z, terms_b)
    grads = jnp.stack([grad_a, jnp.sum(terms_b.astype(jnp.float32), axis=0)])
    wide = normed.astype(jnp.float32)
    grad_mean = jnp.sum(grads, axis=2, keepdims=True) / total
    cross_mean = jnp.sum(grads * wide, axis=2, keepdims=True) / total
    grad_proj = ((grads - grad_mean - wide * cross_mean) * inverse).astype(jnp.bfloat16)
    images_x = total // X
    depth = views * images_x
    grad_proj = jnp.stack(
        [
            jnp.concatenate(
                [grad_proj[v, :, x * images_x : (x + 1) * images_x] for v in range(views)], axis=1
            )
            for x in range(X)
        ]
    )
    grad_proj = lax.all_to_all(
        grad_proj, "dp", split_axis=0, concat_axis=0, axis_index_groups=SAME_REST
    )
    grad_own, columns = gather(grad_proj, ALONG_Z, columns)
    grad_other = swap(grad_own, 1)
    terms = weight_half(grad_own.reshape(feat // 2, depth), columns)
    terms = weight_half(grad_other.reshape(feat // 2, depth), columns, (terms,))
    terms = lax.all_to_all(
        terms, "dp", split_axis=0, concat_axis=0, axis_index_groups=SAME_REST
    )
    return finish(position, terms)


def solution(mesh):
    placed = (P(None, "dp", None), P("dp", "mp"))
    return jax.shard_map(
        per_device, mesh=mesh, in_specs=placed, out_specs=P("dp", "mp"), check_vma=False
    )
```

```python
import functools

import jax
import jax.numpy as jnp
import numpy as np
from jax import lax
from jax.experimental import pallas as pl
from jax.experimental.pallas import tpu as pltpu
from jax.sharding import PartitionSpec as P

epsilon = 1e-05
redundancy_weight = 0.0051
loss_scale = 512.0
DP = 32
MP = 16
Y = 8
X = 4
GROUPS = [list(range(Y)), list(range(Y, MP))]
SAME_REST = [list(range(g, DP, DP // X)) for g in range(DP // X)]
SAME_X = [list(range(x * DP // X, (x + 1) * DP // X)) for x in range(X)]
X_SLOTS = np.array([0, 2, 1, 3])
Z_SLOTS = np.array([0, 3, 2, 1])
ALONG_X = [(8 * int(k),) for k in X_SLOTS[1:]]
ALONG_Z = [(2 * int(k),) for k in Z_SLOTS[1:]]
STRIDED_Z = [(0, 8), (4,), (4, 8)]


def swap(array, data, model=0):
    mask = data * MP + model
    return lax.ppermute(array, ("dp", "mp"), [(i, i ^ mask) for i in range(DP * MP)])


def partner(array):
    return swap(array, 2)


def gather(block, masks, *later):
    parts = [block] + [swap(block, *mask) for mask in masks]
    if later:
        parts[1], *later = lax.optimization_barrier((parts[1], *later))
    return jnp.stack(parts), *later


def add(blocks, masks, *later):
    parts = [blocks[0]] + [swap(blocks[k + 1], *mask) for k, mask in enumerate(masks)]
    parts, later = lax.optimization_barrier((parts, later))
    return sum(part.astype(jnp.float32) for part in parts), *later


def project_kernel(last, order_ref, inputs_ref, weight_ref, *refs):
    out_ref = refs[-1]
    blocks, depth, _ = weight_ref.shape
    result = refs[0][...] if last else None
    for k in range(blocks):
        columns = pl.ds(pl.multiple_of(order_ref[k] * depth, depth), depth)
        part = jnp.dot(inputs_ref[:, columns], weight_ref[k], preferred_element_type=jnp.float32)
        result = part if result is None else result + part
    out_ref[...] = result.T if last else result


def project(order, inputs, weight, before=None):
    rows, feat = inputs.shape[0], weight.shape[2]
    operands = (inputs, weight) if before is None else (inputs, weight, before)
    return pl.pallas_call(
        functools.partial(project_kernel, before is not None),
        in_specs=[pl.BlockSpec(memory_space=pltpu.SMEM)]
        + [pl.BlockSpec(memory_space=pltpu.VMEM)] * len(operands),
        out_specs=pl.BlockSpec(memory_space=pltpu.VMEM),
        out_shape=jax.ShapeDtypeStruct((rows, feat) if before is None else (feat, rows), jnp.float32),
        compiler_params=pltpu.CompilerParams(vmem_limit_bytes=16 * 1024 * 1024),
        cost_estimate=pl.CostEstimate(
            flops=2 * rows * feat * weight.shape[0] * weight.shape[1],
            bytes_accessed=6 * 1024 * 1024,
            transcendentals=0,
        ),
    )(order, *operands)


def weight_kernel(targets_ref, grad_ref, columns_ref, *refs):
    before, outs = refs[:-X], refs[-X:]
    slices, devices, share, wide = columns_ref.shape
    rows = wide // X
    half = slices // 2
    features = grad_ref.shape[0]
    for k in range(X):
        target = pl.ds(pl.multiple_of(targets_ref[k] * rows, rows), rows)
        pieces = [
            columns_ref[half * view : half * (view + 1), d, :, target].reshape(half * share, rows)
            for view in range(2)
            for d in range(devices)
        ]
        columns = jnp.concatenate(pieces, axis=0)
        result = jnp.dot(grad_ref[...], columns, preferred_element_type=jnp.float32)
        if before:
            outs[k][:features] = before[k][...]
            outs[k][features:] = result
        else:
            outs[k][...] = result


def weight_half(targets, grad, columns, *before):
    half, depth = grad.shape
    wide = columns.shape[3]
    features = 2 * half if before else half
    vmem = pl.BlockSpec(memory_space=pltpu.VMEM)
    return pl.pallas_call(
        weight_kernel,
        in_specs=[pl.BlockSpec(memory_space=pltpu.SMEM)] + [vmem] * (2 + len(before)),
        out_specs=[vmem] * X,
        out_shape=[jax.ShapeDtypeStruct((features, wide // X), jnp.float32)] * X,
        compiler_params=pltpu.CompilerParams(vmem_limit_bytes=16 * 1024 * 1024),
        cost_estimate=pl.CostEstimate(
            flops=2 * half * depth * wide, bytes_accessed=5 * 1024 * 1024, transcendentals=0
        ),
    )(targets, grad, columns, *before)


def finish_kernel(position_ref, *refs):
    *terms, out_ref, total_ref = refs
    total_ref[...] = (terms[0][...] + terms[1][...]) + (terms[2][...] + terms[3][...])
    blocks = [total_ref[pl.ds(pl.multiple_of(position_ref[j] * 8, 8), 8)] for j in range(DP)]
    out_ref[...] = jnp.concatenate(blocks, axis=0).T


def finish(position, terms):
    features, rows = terms[0].shape
    vmem = pl.BlockSpec(memory_space=pltpu.VMEM)
    return pl.pallas_call(
        finish_kernel,
        in_specs=[pl.BlockSpec(memory_space=pltpu.SMEM)] + [vmem] * len(terms),
        out_specs=vmem,
        out_shape=jax.ShapeDtypeStruct((rows, features), jnp.float32),
        scratch_shapes=[pltpu.VMEM((features, rows), jnp.float32)],
        compiler_params=pltpu.CompilerParams(vmem_limit_bytes=16 * 1024 * 1024),
    )(position, *terms)


def per_device(inputs, weight):
    views, images, width = inputs.shape
    total = images * DP
    data_index = lax.axis_index("dp")
    model_index = lax.axis_index("mp")
    feat = weight.shape[1]
    block = feat // DP
    rows = width // DP
    flat = inputs.reshape(views * images, width)

    place = np.arange(DP)
    distance = place >> 4 | X_SLOTS[place >> 2 & 3] << 3 | Z_SLOTS[place & 3] << 1
    order = data_index ^ jnp.asarray(distance, jnp.int32)
    relative = data_index ^ jnp.asarray(place, jnp.int32)
    slot = (4 - (relative >> 1 & 3)) & 3
    position = (relative & 1) << 4 | slot << 2 | jnp.asarray(place >> 3, jnp.int32)

    share = views * images // Y
    mine = lax.dynamic_slice_in_dim(flat, lax.rem(model_index, Y) * share, share, axis=0)
    pieces = mine.reshape(share, X, DP // X, rows).transpose(2, 0, 1, 3).reshape(DP // X, share, X * rows)
    weight_own = gather(gather(weight, ALONG_Z)[0], ALONG_X)[0]
    weight_other = swap(weight_own, 1)
    half = (DP // 2, rows, feat)
    projected = project(order[: DP // 2], flat, weight_own.reshape(half))
    projected = project(order[DP // 2 :], flat, weight_other.reshape(half), projected)

    own = lax.all_to_all(
        projected.reshape(DP, block, views * images), "dp", split_axis=0, concat_axis=0
    ).reshape(DP, block, views, images)
    average = jnp.sum(own, axis=(0, 3), keepdims=True) / total
    centered = own - average
    variance = jnp.sum(centered * centered, axis=(0, 3), keepdims=True) / total
    inverse = lax.rsqrt(variance + epsilon)
    normed = (centered * inverse).astype(jnp.bfloat16).transpose(2, 1, 0, 3).reshape(views, block, total)
    inverse = inverse.reshape(block, views).T[:, :, None]

    second = normed[1]
    pair = jnp.stack([second, partner(second)])
    first, pair, pieces = lax.optimization_barrier((normed[0], pair, pieces))
    slices = lax.all_to_all(
        pieces, "dp", split_axis=0, concat_axis=0, axis_index_groups=SAME_X
    )
    columns_b = lax.all_gather(pair, "mp", axis=0, axis_index_groups=GROUPS)
    columns_b = columns_b.reshape(MP * block, total)
    rows_own = gather(gather(first, STRIDED_Z)[0], ALONG_X)[0]
    rows_own, columns_b, slices = lax.optimization_barrier((rows_own, columns_b, slices))
    columns = lax.all_gather(slices, "mp", axis=0, axis_index_groups=GROUPS)
    rows_other = swap(rows_own, 1).reshape(feat // 2, total)
    rows_own = rows_own.reshape(feat // 2, total)

    def gradient_of(rows_a, with_diagonal):
        correlation = (
            lax.dot_general(rows_a, columns_b, (((1,), (1,)), ((), ())), preferred_element_type=jnp.float32)
            / total
        )
        inner = 2.0 * redundancy_weight * correlation
        if with_diagonal:
            row = lax.broadcasted_iota(jnp.int32, correlation.shape, 0)
            column = lax.broadcasted_iota(jnp.int32, correlation.shape, 1)
            diagonal = (row < block) & (column == lax.rem(model_index, Y) * 2 * block + row)
            inner = inner + diagonal.astype(jnp.float32) * (2.0 * (correlation - 1.0) - inner)
        return (loss_scale * inner).astype(jnp.bfloat16)

    corr_own = gradient_of(rows_own, True)
    corr_other = gradient_of(rows_other, False)

    def times(lhs, rhs, dims):
        return lax.dot_general(lhs, rhs, (dims, ((), ())), preferred_element_type=jnp.float32) / total

    half = (feat // 2, Y, 2, block)
    sides = [
        corr.reshape(half).transpose(2, 0, 1, 3).reshape(2, feat // 2, Y * block)
        for corr in (corr_own, corr_other)
    ]
    terms_b = [
        times(sides[0][k], rows_own, ((0,), (0,))) + times(sides[1][k], rows_other, ((0,), (0,)))
        for k in (0, 1)
    ]
    away = terms_b[1].astype(jnp.bfloat16)
    corr_own, corr_other, away = lax.optimization_barrier((corr_own, corr_other, away))
    terms_b = (terms_b[0] + partner(away).astype(jnp.float32)).astype(jnp.bfloat16)
    terms_b = lax.all_to_all(
        terms_b.reshape(Y, block, total), "mp", split_axis=0, concat_axis=0, axis_index_groups=GROUPS
    )
    terms_other = times(corr_other, columns_b, ((1,), (0,))).astype(jnp.bfloat16)
    terms_own = times(corr_own, columns_b, ((1,), (0,)))
    shape = (4, 4, block, total)
    both = terms_own.reshape(shape) + swap(terms_other.reshape(shape), 1).astype(jnp.float32)
    along_x = add(both.astype(jnp.bfloat16), ALONG_X)[0].astype(jnp.bfloat16)
    grad_a, terms_b = add(along_x, STRIDED_Z, terms_b)
    grads = jnp.stack([grad_a, jnp.sum(terms_b.astype(jnp.float32), axis=0)])
    wide = normed.astype(jnp.float32)
    grad_mean = jnp.sum(grads, axis=2, keepdims=True) / total
    cross_mean = jnp.sum(grads * wide, axis=2, keepdims=True) / total
    grad_proj = ((grads - grad_mean - wide * cross_mean) * inverse).astype(jnp.bfloat16)
    images_x = total // X
    depth = views * images_x
    grad_proj = jnp.stack(
        [
            jnp.concatenate(
                [grad_proj[v, :, x * images_x : (x + 1) * images_x] for v in range(views)], axis=1
            )
            for x in range(X)
        ]
    )
    grad_proj = lax.all_to_all(
        grad_proj, "dp", split_axis=0, concat_axis=0, axis_index_groups=SAME_REST
    )
    grad_own, columns = gather(grad_proj, ALONG_Z, columns)
    grad_other = swap(grad_own, 1)
    targets = data_index >> 3 ^ jnp.asarray(X_SLOTS, jnp.int32)
    terms = weight_half(targets, grad_own.reshape(feat // 2, depth), columns)
    terms = weight_half(targets, grad_other.reshape(feat // 2, depth), columns, *terms)
    return finish(position, [terms[0]] + [swap(terms[k + 1], *mask) for k, mask in enumerate(ALONG_X)])


def solution(mesh):
    placed = (P(None, "dp", None), P("dp", "mp"))
    return jax.shard_map(
        per_device, mesh=mesh, in_specs=placed, out_specs=P("dp", "mp"), check_vma=False
    )
```

```python
import functools

import jax
import jax.numpy as jnp
import numpy as np
from jax import lax
from jax.experimental import pallas as pl
from jax.experimental.pallas import tpu as pltpu
from jax.sharding import PartitionSpec as P

epsilon = 1e-05
redundancy_weight = 0.0051
loss_scale = 512.0
DP = 32
MP = 16
Y = 8
X = 4
GROUPS = [list(range(Y)), list(range(Y, MP))]
SAME_CORE = [list(range(core, DP, 2)) for core in range(2)]
SAME_X = [list(range(x * DP // X, (x + 1) * DP // X)) for x in range(X)]
X_SLOTS = np.array([0, 2, 1, 3])
Z_SLOTS = np.array([0, 3, 2, 1])
ALONG_X = [(8 * int(k),) for k in X_SLOTS[1:]]
ALONG_Z = [(2 * int(k),) for k in Z_SLOTS[1:]]
STRIDED_Z = [(0, 8), (4,), (4, 8)]


def swap(array, data, model=0):
    mask = data * MP + model
    return lax.ppermute(array, ("dp", "mp"), [(i, i ^ mask) for i in range(DP * MP)])


def partner(array):
    return swap(array, 2)


def gather(block, masks, *later):
    parts = [block] + [swap(block, *mask) for mask in masks]
    if later:
        parts[1], *later = lax.optimization_barrier((parts[1], *later))
    return jnp.stack(parts), *later


def add(blocks, masks, *later):
    parts = [blocks[0]] + [swap(blocks[k + 1], *mask) for k, mask in enumerate(masks)]
    parts, later = lax.optimization_barrier((parts, later))
    return sum(part.astype(jnp.float32) for part in parts), *later


def project_kernel(last, order_ref, inputs_ref, weight_ref, *refs):
    out_ref = refs[-1]
    blocks, depth, _ = weight_ref.shape
    result = refs[0][...] if last else None
    for k in range(blocks):
        columns = pl.ds(pl.multiple_of(order_ref[k] * depth, depth), depth)
        part = jnp.dot(inputs_ref[:, columns], weight_ref[k], preferred_element_type=jnp.float32)
        result = part if result is None else result + part
    out_ref[...] = result.T if last else result


def project(order, inputs, weight, before=None):
    rows, feat = inputs.shape[0], weight.shape[2]
    operands = (inputs, weight) if before is None else (inputs, weight, before)
    return pl.pallas_call(
        functools.partial(project_kernel, before is not None),
        in_specs=[pl.BlockSpec(memory_space=pltpu.SMEM)]
        + [pl.BlockSpec(memory_space=pltpu.VMEM)] * len(operands),
        out_specs=pl.BlockSpec(memory_space=pltpu.VMEM),
        out_shape=jax.ShapeDtypeStruct((rows, feat) if before is None else (feat, rows), jnp.float32),
        compiler_params=pltpu.CompilerParams(vmem_limit_bytes=16 * 1024 * 1024),
        cost_estimate=pl.CostEstimate(
            flops=2 * rows * feat * weight.shape[0] * weight.shape[1],
            bytes_accessed=6 * 1024 * 1024,
            transcendentals=0,
        ),
    )(order, *operands)


def weight_kernel(targets_ref, grad_ref, columns_ref, *refs):
    before, outs = refs[:-X], refs[-X:]
    slices, devices, share, wide = columns_ref.shape
    rows = wide // X
    half = slices // 2
    features = grad_ref.shape[0]
    for k in range(X):
        target = pl.ds(pl.multiple_of(targets_ref[k] * rows, rows), rows)
        pieces = [
            columns_ref[half * view : half * (view + 1), d, :, target].reshape(half * share, rows)
            for view in range(2)
            for d in range(devices)
        ]
        columns = jnp.concatenate(pieces, axis=0)
        result = jnp.dot(grad_ref[...], columns, preferred_element_type=jnp.float32)
        if before:
            outs[k][:features] = before[k][...]
            outs[k][features:] = result
        else:
            outs[k][...] = result


def weight_half(targets, grad, columns, *before):
    half, depth = grad.shape
    wide = columns.shape[3]
    features = 2 * half if before else half
    vmem = pl.BlockSpec(memory_space=pltpu.VMEM)
    return pl.pallas_call(
        weight_kernel,
        in_specs=[pl.BlockSpec(memory_space=pltpu.SMEM)] + [vmem] * (2 + len(before)),
        out_specs=[vmem] * X,
        out_shape=[jax.ShapeDtypeStruct((features, wide // X), jnp.float32)] * X,
        compiler_params=pltpu.CompilerParams(vmem_limit_bytes=16 * 1024 * 1024),
        cost_estimate=pl.CostEstimate(
            flops=2 * half * depth * wide, bytes_accessed=5 * 1024 * 1024, transcendentals=0
        ),
    )(targets, grad, columns, *before)


def finish_kernel(position_ref, *refs):
    *terms, out_ref, total_ref = refs
    total_ref[...] = (terms[0][...] + terms[1][...]) + (terms[2][...] + terms[3][...])
    blocks = [total_ref[pl.ds(pl.multiple_of(position_ref[j] * 8, 8), 8)] for j in range(DP)]
    out_ref[...] = jnp.concatenate(blocks, axis=0).T


def finish(position, terms):
    features, rows = terms[0].shape
    vmem = pl.BlockSpec(memory_space=pltpu.VMEM)
    return pl.pallas_call(
        finish_kernel,
        in_specs=[pl.BlockSpec(memory_space=pltpu.SMEM)] + [vmem] * len(terms),
        out_specs=vmem,
        out_shape=jax.ShapeDtypeStruct((rows, features), jnp.float32),
        scratch_shapes=[pltpu.VMEM((features, rows), jnp.float32)],
        compiler_params=pltpu.CompilerParams(vmem_limit_bytes=16 * 1024 * 1024),
    )(position, *terms)


def per_device(inputs, weight):
    views, images, width = inputs.shape
    total = images * DP
    data_index = lax.axis_index("dp")
    model_index = lax.axis_index("mp")
    feat = weight.shape[1]
    block = feat // DP
    rows = width // DP
    flat = inputs.reshape(views * images, width)

    place = np.arange(DP)
    distance = place >> 4 | X_SLOTS[place >> 2 & 3] << 3 | Z_SLOTS[place & 3] << 1
    order = data_index ^ jnp.asarray(distance, jnp.int32)
    position = (data_index & 1 ^ jnp.asarray(place & 1, jnp.int32)) << 4 | jnp.asarray(place >> 1, jnp.int32)

    share = views * images // Y
    mine = lax.dynamic_slice_in_dim(flat, lax.rem(model_index, Y) * share, share, axis=0)
    pieces = mine.reshape(share, X, DP // X, rows).transpose(2, 0, 1, 3).reshape(DP // X, share, X * rows)
    weight_own = gather(gather(weight, ALONG_Z)[0], ALONG_X)[0]
    weight_other = swap(weight_own, 1)
    half = (DP // 2, rows, feat)
    projected = project(order[: DP // 2], flat, weight_own.reshape(half))
    projected = project(order[DP // 2 :], flat, weight_other.reshape(half), projected)

    own = lax.all_to_all(
        projected.reshape(DP, block, views * images), "dp", split_axis=0, concat_axis=0
    ).reshape(DP, block, views, images)
    average = jnp.sum(own, axis=(0, 3), keepdims=True) / total
    centered = own - average
    variance = jnp.sum(centered * centered, axis=(0, 3), keepdims=True) / total
    inverse = lax.rsqrt(variance + epsilon)
    normed = (centered * inverse).astype(jnp.bfloat16).transpose(2, 1, 0, 3).reshape(views, block, total)
    inverse = inverse.reshape(block, views).T[:, :, None]

    second = normed[1]
    pair = jnp.stack([second, partner(second)])
    first, pair, pieces = lax.optimization_barrier((normed[0], pair, pieces))
    slices = lax.all_to_all(
        pieces, "dp", split_axis=0, concat_axis=0, axis_index_groups=SAME_X
    )
    columns_b = lax.all_gather(pair, "mp", axis=0, axis_index_groups=GROUPS)
    columns_b = columns_b.reshape(MP * block, total)
    rows_own = gather(gather(first, STRIDED_Z)[0], ALONG_X)[0]
    rows_own, columns_b, slices = lax.optimization_barrier((rows_own, columns_b, slices))
    columns = lax.all_gather(slices, "mp", axis=0, axis_index_groups=GROUPS)
    rows_other = swap(rows_own, 1).reshape(feat // 2, total)
    rows_own = rows_own.reshape(feat // 2, total)

    def gradient_of(rows_a, with_diagonal):
        correlation = (
            lax.dot_general(rows_a, columns_b, (((1,), (1,)), ((), ())), preferred_element_type=jnp.float32)
            / total
        )
        inner = 2.0 * redundancy_weight * correlation
        if with_diagonal:
            row = lax.broadcasted_iota(jnp.int32, correlation.shape, 0)
            column = lax.broadcasted_iota(jnp.int32, correlation.shape, 1)
            diagonal = (row < block) & (column == lax.rem(model_index, Y) * 2 * block + row)
            inner = inner + diagonal.astype(jnp.float32) * (2.0 * (correlation - 1.0) - inner)
        return (loss_scale * inner).astype(jnp.bfloat16)

    corr_own = gradient_of(rows_own, True)
    corr_other = gradient_of(rows_other, False)

    def times(lhs, rhs, dims):
        return lax.dot_general(lhs, rhs, (dims, ((), ())), preferred_element_type=jnp.float32) / total

    half = (feat // 2, Y, 2, block)
    sides = [
        corr.reshape(half).transpose(2, 0, 1, 3).reshape(2, feat // 2, Y * block)
        for corr in (corr_own, corr_other)
    ]
    terms_b = [
        times(sides[0][k], rows_own, ((0,), (0,))) + times(sides[1][k], rows_other, ((0,), (0,)))
        for k in (0, 1)
    ]
    away = terms_b[1].astype(jnp.bfloat16)
    corr_own, corr_other, away = lax.optimization_barrier((corr_own, corr_other, away))
    terms_b = (terms_b[0] + partner(away).astype(jnp.float32)).astype(jnp.bfloat16)
    terms_b = lax.all_to_all(
        terms_b.reshape(Y, block, total), "mp", split_axis=0, concat_axis=0, axis_index_groups=GROUPS
    )
    terms_other = times(corr_other, columns_b, ((1,), (0,))).astype(jnp.bfloat16)
    terms_own = times(corr_own, columns_b, ((1,), (0,)))
    shape = (4, 4, block, total)
    terms_own, terms_other = terms_own.reshape(shape), swap(terms_other.reshape(shape), 1)
    both = [(terms_own[k] + terms_other[k].astype(jnp.float32)).astype(jnp.bfloat16) for k in range(X)]
    along_x = add(both, ALONG_X)[0].astype(jnp.bfloat16)
    grad_a, terms_b = add(along_x, STRIDED_Z, terms_b)
    grads = jnp.stack([grad_a, jnp.sum(terms_b.astype(jnp.float32), axis=0)])
    wide = normed.astype(jnp.float32)
    grad_mean = jnp.sum(grads, axis=2, keepdims=True) / total
    cross_mean = jnp.sum(grads * wide, axis=2, keepdims=True) / total
    grad_proj = ((grads - grad_mean - wide * cross_mean) * inverse).astype(jnp.bfloat16)
    images_x = total // X
    depth = views * images_x
    blocks = [
        jnp.concatenate([grad_proj[v, :, x * images_x : (x + 1) * images_x] for v in range(views)], axis=1)
        for x in range(X)
    ]
    grad_own = lax.all_to_all(
        jnp.stack([part for part in blocks for _ in range(DP // X // 2)]),
        "dp",
        split_axis=0,
        concat_axis=0,
        axis_index_groups=SAME_CORE,
    )
    grad_own, columns = lax.optimization_barrier((grad_own, columns))
    grad_other = swap(grad_own, 1)
    targets = data_index >> 3 ^ jnp.asarray(X_SLOTS, jnp.int32)
    terms = weight_half(targets, grad_own.reshape(feat // 2, depth), columns)
    terms = weight_half(targets, grad_other.reshape(feat // 2, depth), columns, *terms)
    return finish(position, [terms[0]] + [swap(terms[k + 1], *mask) for k, mask in enumerate(ALONG_X)])


def solution(mesh):
    placed = (P(None, "dp", None), P("dp", "mp"))
    return jax.shard_map(
        per_device, mesh=mesh, in_specs=placed, out_specs=P("dp", "mp"), check_vma=False
    )
```

```python
import functools

import jax
import jax.numpy as jnp
import numpy as np
from jax import lax
from jax.experimental import pallas as pl
from jax.experimental.pallas import tpu as pltpu
from jax.sharding import PartitionSpec as P

epsilon = 1e-05
redundancy_weight = 0.0051
loss_scale = 512.0
DP = 32
MP = 16
Y = 8
X = 4
GROUPS = [list(range(Y)), list(range(Y, MP))]
SAME_CORE = [list(range(core, DP, 2)) for core in range(2)]
SAME_X = [list(range(x * DP // X, (x + 1) * DP // X)) for x in range(X)]
X_SLOTS = np.array([0, 2, 1, 3])
Z_SLOTS = np.array([0, 3, 2, 1])
ALONG_X = [(8 * int(k),) for k in X_SLOTS[1:]]
ALONG_Z = [(2 * int(k),) for k in Z_SLOTS[1:]]
STRIDED_Z = [(0, 8), (4,), (4, 8)]


def swap(array, data, model=0):
    mask = data * MP + model
    return lax.ppermute(array, ("dp", "mp"), [(i, i ^ mask) for i in range(DP * MP)])


def partner(array):
    return swap(array, 2)


def gather(block, masks, *later):
    parts = [block] + [swap(block, *mask) for mask in masks]
    if later:
        parts[1], *later = lax.optimization_barrier((parts[1], *later))
    return jnp.stack(parts), *later


def add(blocks, masks, *later):
    parts = [blocks[0]] + [swap(blocks[k + 1], *mask) for k, mask in enumerate(masks)]
    parts, later = lax.optimization_barrier((parts, later))
    return sum(part.astype(jnp.float32) for part in parts), *later


def project_kernel(last, order_ref, inputs_ref, weight_ref, *refs):
    out_ref = refs[-1]
    blocks, depth, _ = weight_ref.shape
    result = refs[0][...] if last else None
    for k in range(blocks):
        columns = pl.ds(pl.multiple_of(order_ref[k] * depth, depth), depth)
        part = jnp.dot(inputs_ref[:, columns], weight_ref[k], preferred_element_type=jnp.float32)
        result = part if result is None else result + part
    out_ref[...] = result.T if last else result


def project(order, inputs, weight, before=None):
    rows, feat = inputs.shape[0], weight.shape[2]
    operands = (inputs, weight) if before is None else (inputs, weight, before)
    return pl.pallas_call(
        functools.partial(project_kernel, before is not None),
        in_specs=[pl.BlockSpec(memory_space=pltpu.SMEM)]
        + [pl.BlockSpec(memory_space=pltpu.VMEM)] * len(operands),
        out_specs=pl.BlockSpec(memory_space=pltpu.VMEM),
        out_shape=jax.ShapeDtypeStruct((rows, feat) if before is None else (feat, rows), jnp.float32),
        compiler_params=pltpu.CompilerParams(vmem_limit_bytes=16 * 1024 * 1024),
        cost_estimate=pl.CostEstimate(
            flops=2 * rows * feat * weight.shape[0] * weight.shape[1],
            bytes_accessed=6 * 1024 * 1024,
            transcendentals=0,
        ),
    )(order, *operands)


def weight_kernel(targets_ref, grad_ref, columns_ref, *refs):
    before, outs = refs[:-X], refs[-X:]
    slices, devices, share, wide = columns_ref.shape
    rows = wide // X
    half = slices // 2
    features = grad_ref.shape[0]
    for k in range(X):
        target = pl.ds(pl.multiple_of(targets_ref[k] * rows, rows), rows)
        pieces = [
            columns_ref[half * view : half * (view + 1), d, :, target].reshape(half * share, rows)
            for view in range(2)
            for d in range(devices)
        ]
        columns = jnp.concatenate(pieces, axis=0)
        result = jnp.dot(grad_ref[...], columns, preferred_element_type=jnp.float32)
        if before:
            outs[k][:features] = before[k][...]
            outs[k][features:] = result
        else:
            outs[k][...] = result


def weight_half(targets, grad, columns, *before):
    half, depth = grad.shape
    wide = columns.shape[3]
    features = 2 * half if before else half
    vmem = pl.BlockSpec(memory_space=pltpu.VMEM)
    return pl.pallas_call(
        weight_kernel,
        in_specs=[pl.BlockSpec(memory_space=pltpu.SMEM)] + [vmem] * (2 + len(before)),
        out_specs=[vmem] * X,
        out_shape=[jax.ShapeDtypeStruct((features, wide // X), jnp.float32)] * X,
        compiler_params=pltpu.CompilerParams(vmem_limit_bytes=16 * 1024 * 1024),
        cost_estimate=pl.CostEstimate(
            flops=2 * half * depth * wide, bytes_accessed=5 * 1024 * 1024, transcendentals=0
        ),
    )(targets, grad, columns, *before)


def finish_kernel(position_ref, *refs):
    *terms, out_ref, total_ref = refs
    total_ref[...] = (terms[0][...] + terms[1][...]) + (terms[2][...] + terms[3][...])
    blocks = [total_ref[pl.ds(pl.multiple_of(position_ref[j] * 8, 8), 8)] for j in range(DP)]
    out_ref[...] = jnp.concatenate(blocks, axis=0).T


def finish(position, terms):
    features, rows = terms[0].shape
    vmem = pl.BlockSpec(memory_space=pltpu.VMEM)
    return pl.pallas_call(
        finish_kernel,
        in_specs=[pl.BlockSpec(memory_space=pltpu.SMEM)] + [vmem] * len(terms),
        out_specs=vmem,
        out_shape=jax.ShapeDtypeStruct((rows, features), jnp.float32),
        scratch_shapes=[pltpu.VMEM((features, rows), jnp.float32)],
        compiler_params=pltpu.CompilerParams(vmem_limit_bytes=16 * 1024 * 1024),
    )(position, *terms)


def per_device(inputs, weight):
    views, images, width = inputs.shape
    total = images * DP
    data_index = lax.axis_index("dp")
    model_index = lax.axis_index("mp")
    feat = weight.shape[1]
    block = feat // DP
    rows = width // DP
    flat = inputs.reshape(views * images, width)

    place = np.arange(DP)
    distance = place >> 4 | X_SLOTS[place >> 2 & 3] << 3 | Z_SLOTS[place & 3] << 1
    order = data_index ^ jnp.asarray(distance, jnp.int32)
    position = (data_index & 1 ^ jnp.asarray(place & 1, jnp.int32)) << 4 | jnp.asarray(place >> 1, jnp.int32)

    share = views * images // Y
    mine = lax.dynamic_slice_in_dim(flat, lax.rem(model_index, Y) * share, share, axis=0)
    pieces = mine.reshape(share, X, DP // X, rows).transpose(2, 0, 1, 3).reshape(DP // X, share, X * rows)
    weight_own = gather(gather(weight, ALONG_Z)[0], ALONG_X)[0]
    weight_other = swap(weight_own, 1)
    half = (DP // 2, rows, feat)
    projected = project(order[: DP // 2], flat, weight_own.reshape(half))
    projected = project(order[DP // 2 :], flat, weight_other.reshape(half), projected)

    own = lax.all_to_all(
        projected.reshape(DP, block, views * images), "dp", split_axis=0, concat_axis=0
    ).reshape(DP, block, views, images)
    average = jnp.sum(own, axis=(0, 3), keepdims=True) / total
    centered = own - average
    variance = jnp.sum(centered * centered, axis=(0, 3), keepdims=True) / total
    inverse = lax.rsqrt(variance + epsilon)
    normed = (centered * inverse).astype(jnp.bfloat16).transpose(2, 1, 0, 3).reshape(views, block, total)
    inverse = inverse.reshape(block, views).T[:, :, None]

    second = normed[1]
    pair = jnp.stack([second, partner(second)])
    first, pair, pieces = lax.optimization_barrier((normed[0], pair, pieces))
    slices = lax.all_to_all(
        pieces, "dp", split_axis=0, concat_axis=0, axis_index_groups=SAME_X
    )
    columns_b = lax.all_gather(pair, "mp", axis=0, axis_index_groups=GROUPS)
    columns_b = columns_b.reshape(MP * block, total)
    rows_own, slices = gather(gather(first, STRIDED_Z)[0], ALONG_X, slices)
    rows_own, columns_b = lax.optimization_barrier((rows_own, columns_b))
    columns = lax.all_gather(slices, "mp", axis=0, axis_index_groups=GROUPS)
    rows_other = swap(rows_own, 1).reshape(feat // 2, total)
    rows_own = rows_own.reshape(feat // 2, total)

    def gradient_of(rows_a, with_diagonal):
        correlation = (
            lax.dot_general(rows_a, columns_b, (((1,), (1,)), ((), ())), preferred_element_type=jnp.float32)
            / total
        )
        inner = 2.0 * redundancy_weight * correlation
        if with_diagonal:
            row = lax.broadcasted_iota(jnp.int32, correlation.shape, 0)
            column = lax.broadcasted_iota(jnp.int32, correlation.shape, 1)
            diagonal = (row < block) & (column == lax.rem(model_index, Y) * 2 * block + row)
            inner = inner + diagonal.astype(jnp.float32) * (2.0 * (correlation - 1.0) - inner)
        return (loss_scale * inner).astype(jnp.bfloat16)

    corr_own = gradient_of(rows_own, True)
    corr_other = gradient_of(rows_other, False)

    def times(lhs, rhs, dims):
        return lax.dot_general(lhs, rhs, (dims, ((), ())), preferred_element_type=jnp.float32) / total

    half = (feat // 2, Y, 2, block)
    sides = [
        corr.reshape(half).transpose(2, 0, 1, 3).reshape(2, feat // 2, Y * block)
        for corr in (corr_own, corr_other)
    ]
    terms_b = [
        times(sides[0][k], rows_own, ((0,), (0,))) + times(sides[1][k], rows_other, ((0,), (0,)))
        for k in (0, 1)
    ]
    away = terms_b[1].astype(jnp.bfloat16)
    corr_own, corr_other, away = lax.optimization_barrier((corr_own, corr_other, away))
    terms_b = (terms_b[0] + partner(away).astype(jnp.float32)).astype(jnp.bfloat16)
    terms_b = lax.all_to_all(
        terms_b.reshape(Y, block, total), "mp", split_axis=0, concat_axis=0, axis_index_groups=GROUPS
    )
    terms_other = times(corr_other, columns_b, ((1,), (0,))).astype(jnp.bfloat16)
    terms_own = times(corr_own, columns_b, ((1,), (0,)))
    shape = (4, 4, block, total)
    terms_own, terms_other = terms_own.reshape(shape), swap(terms_other.reshape(shape), 1)
    both = [(terms_own[k] + terms_other[k].astype(jnp.float32)).astype(jnp.bfloat16) for k in range(X)]
    along_x = add(both, ALONG_X)[0].astype(jnp.bfloat16)
    grad_a, terms_b = add(along_x, STRIDED_Z, terms_b)
    grads = jnp.stack([grad_a, jnp.sum(terms_b.astype(jnp.float32), axis=0)])
    wide = normed.astype(jnp.float32)
    grad_mean = jnp.sum(grads, axis=2, keepdims=True) / total
    cross_mean = jnp.sum(grads * wide, axis=2, keepdims=True) / total
    grad_proj = ((grads - grad_mean - wide * cross_mean) * inverse).astype(jnp.bfloat16)
    images_x = total // X
    depth = views * images_x
    blocks = [
        jnp.concatenate([grad_proj[v, :, x * images_x : (x + 1) * images_x] for v in range(views)], axis=1)
        for x in range(X)
    ]
    grad_own = lax.all_to_all(
        jnp.stack([part for part in blocks for _ in range(DP // X // 2)]),
        "dp",
        split_axis=0,
        concat_axis=0,
        axis_index_groups=SAME_CORE,
    )
    grad_own, columns = lax.optimization_barrier((grad_own, columns))
    grad_other = swap(grad_own, 1)
    targets = data_index >> 3 ^ jnp.asarray(X_SLOTS, jnp.int32)
    terms = weight_half(targets, grad_own.reshape(feat // 2, depth), columns)
    terms = weight_half(targets, grad_other.reshape(feat // 2, depth), columns, *terms)
    return finish(position, [terms[0]] + [swap(terms[k + 1], *mask) for k, mask in enumerate(ALONG_X)])


def solution(mesh):
    placed = (P(None, "dp", None), P("dp", "mp"))
    return jax.shard_map(
        per_device, mesh=mesh, in_specs=placed, out_specs=P("dp", "mp"), check_vma=False
    )
```

```python
import functools

import jax
import jax.numpy as jnp
import numpy as np
from jax import lax
from jax.experimental import pallas as pl
from jax.experimental.pallas import tpu as pltpu
from jax.sharding import PartitionSpec as P

epsilon = 1e-05
redundancy_weight = 0.0051
loss_scale = 512.0
DP = 32
MP = 16
Y = 8
X = 4
GROUPS = [list(range(Y)), list(range(Y, MP))]
SAME_CORE = [list(range(core, DP, 2)) for core in range(2)]
SAME_X = [list(range(x * DP // X, (x + 1) * DP // X)) for x in range(X)]
X_SLOTS = np.array([0, 2, 1, 3])
Z_SLOTS = np.array([0, 3, 2, 1])
ALONG_X = [(8 * int(k),) for k in X_SLOTS[1:]]
ALONG_Z = [(2 * int(k),) for k in Z_SLOTS[1:]]
STRIDED_Z = [(0, 8), (4,), (4, 8)]


def swap(array, data, model=0):
    mask = data * MP + model
    return lax.ppermute(array, ("dp", "mp"), [(i, i ^ mask) for i in range(DP * MP)])


def partner(array):
    return swap(array, 2)


def gather(block, masks, *later):
    parts = [block] + [swap(block, *mask) for mask in masks]
    if later:
        parts[1], *later = lax.optimization_barrier((parts[1], *later))
    return jnp.stack(parts), *later


def add(blocks, masks, *later):
    parts = [blocks[0]] + [swap(blocks[k + 1], *mask) for k, mask in enumerate(masks)]
    parts, later = lax.optimization_barrier((parts, later))
    return sum(part.astype(jnp.float32) for part in parts), *later


def project_kernel(last, order_ref, inputs_ref, own_ref, other_ref, *refs):
    out_ref = refs[-1]
    blocks, depth, _ = own_ref.shape
    result = refs[0][...] if last else None
    for core, weight_ref in enumerate((own_ref, other_ref)):
        for k in range(blocks):
            start = pl.multiple_of(order_ref[core * blocks + k] * depth, depth)
            part = jnp.dot(
                inputs_ref[:, pl.ds(start, depth)], weight_ref[k], preferred_element_type=jnp.float32
            )
            result = part if result is None else result + part
    out_ref[...] = result.T if last else result


def project(order, inputs, own, other, *before):
    rows, feat = inputs.shape[0], own.shape[2]
    vmem = pl.BlockSpec(memory_space=pltpu.VMEM)
    return pl.pallas_call(
        functools.partial(project_kernel, bool(before)),
        in_specs=[pl.BlockSpec(memory_space=pltpu.SMEM)] + [vmem] * (3 + len(before)),
        out_specs=vmem,
        out_shape=jax.ShapeDtypeStruct((feat, rows) if before else (rows, feat), jnp.float32),
        compiler_params=pltpu.CompilerParams(vmem_limit_bytes=16 * 1024 * 1024),
        cost_estimate=pl.CostEstimate(
            flops=4 * rows * feat * own.shape[0] * own.shape[1],
            bytes_accessed=6 * 1024 * 1024,
            transcendentals=0,
        ),
    )(order, inputs, own, other, *before)


def weight_kernel(targets_ref, grad_ref, columns_ref, *refs):
    before, outs = refs[:-X], refs[-X:]
    slices, devices, share, wide = columns_ref.shape
    rows = wide // X
    half = slices // 2
    features = grad_ref.shape[0]
    for k in range(X):
        target = pl.ds(pl.multiple_of(targets_ref[k] * rows, rows), rows)
        pieces = [
            columns_ref[half * view : half * (view + 1), d, :, target].reshape(half * share, rows)
            for view in range(2)
            for d in range(devices)
        ]
        columns = jnp.concatenate(pieces, axis=0)
        result = jnp.dot(grad_ref[...], columns, preferred_element_type=jnp.float32)
        if before:
            outs[k][:features] = before[k][...]
            outs[k][features:] = result
        else:
            outs[k][...] = result


def weight_half(targets, grad, columns, *before):
    half, depth = grad.shape
    wide = columns.shape[3]
    features = 2 * half if before else half
    vmem = pl.BlockSpec(memory_space=pltpu.VMEM)
    return pl.pallas_call(
        weight_kernel,
        in_specs=[pl.BlockSpec(memory_space=pltpu.SMEM)] + [vmem] * (2 + len(before)),
        out_specs=[vmem] * X,
        out_shape=[jax.ShapeDtypeStruct((features, wide // X), jnp.float32)] * X,
        compiler_params=pltpu.CompilerParams(vmem_limit_bytes=16 * 1024 * 1024),
        cost_estimate=pl.CostEstimate(
            flops=2 * half * depth * wide, bytes_accessed=5 * 1024 * 1024, transcendentals=0
        ),
    )(targets, grad, columns, *before)


def finish_kernel(position_ref, *refs):
    *terms, out_ref, total_ref = refs
    total_ref[...] = (terms[0][...] + terms[1][...]) + (terms[2][...] + terms[3][...])
    blocks = [total_ref[pl.ds(pl.multiple_of(position_ref[j] * 8, 8), 8)] for j in range(DP)]
    out_ref[...] = jnp.concatenate(blocks, axis=0).T


def finish(position, terms):
    features, rows = terms[0].shape
    vmem = pl.BlockSpec(memory_space=pltpu.VMEM)
    return pl.pallas_call(
        finish_kernel,
        in_specs=[pl.BlockSpec(memory_space=pltpu.SMEM)] + [vmem] * len(terms),
        out_specs=vmem,
        out_shape=jax.ShapeDtypeStruct((rows, features), jnp.float32),
        scratch_shapes=[pltpu.VMEM((features, rows), jnp.float32)],
        compiler_params=pltpu.CompilerParams(vmem_limit_bytes=16 * 1024 * 1024),
    )(position, *terms)


def per_device(inputs, weight):
    views, images, width = inputs.shape
    total = images * DP
    data_index = lax.axis_index("dp")
    model_index = lax.axis_index("mp")
    feat = weight.shape[1]
    block = feat // DP
    rows = width // DP
    flat = inputs.reshape(views * images, width)

    place = np.arange(DP)
    distance = place >> 4 | X_SLOTS[place >> 2 & 3] << 3 | Z_SLOTS[place & 3] << 1
    position = (data_index & 1 ^ jnp.asarray(place & 1, jnp.int32)) << 4 | jnp.asarray(place >> 1, jnp.int32)

    share = views * images // Y
    mine = lax.dynamic_slice_in_dim(flat, lax.rem(model_index, Y) * share, share, axis=0)
    pieces = mine.reshape(share, X, DP // X, rows).transpose(2, 0, 1, 3).reshape(DP // X, share, X * rows)
    along_z = gather(weight, ALONG_Z)[0]
    parts = [along_z] + [swap(along_z, *mask) for mask in ALONG_X]
    projected = ()
    for k in (0, 2):
        weight_own = jnp.stack(parts[k : k + 2])
        weight_other = swap(weight_own, 1)
        blocks = np.concatenate([4 * k + np.arange(8), 16 + 4 * k + np.arange(8)])
        half = (DP // 4, rows, feat)
        order = data_index ^ jnp.asarray(distance[blocks], jnp.int32)
        halves = weight_own.reshape(half), weight_other.reshape(half)
        projected = (project(order, flat, *halves, *projected),)
    projected = projected[0]

    own = lax.all_to_all(
        projected.reshape(DP, block, views * images), "dp", split_axis=0, concat_axis=0
    ).reshape(DP, block, views, images)
    average = jnp.sum(own, axis=(0, 3), keepdims=True) / total
    centered = own - average
    variance = jnp.sum(centered * centered, axis=(0, 3), keepdims=True) / total
    inverse = lax.rsqrt(variance + epsilon)
    normed = (centered * inverse).astype(jnp.bfloat16).transpose(2, 1, 0, 3).reshape(views, block, total)
    inverse = inverse.reshape(block, views).T[:, :, None]

    second = normed[1]
    pair = jnp.stack([second, partner(second)])
    first, pair, pieces = lax.optimization_barrier((normed[0], pair, pieces))
    slices = lax.all_to_all(
        pieces, "dp", split_axis=0, concat_axis=0, axis_index_groups=SAME_X
    )
    columns_b = lax.all_gather(pair, "mp", axis=0, axis_index_groups=GROUPS)
    columns_b = columns_b.reshape(MP * block, total)
    rows_own, slices = gather(gather(first, STRIDED_Z)[0], ALONG_X, slices)
    rows_own, columns_b = lax.optimization_barrier((rows_own, columns_b))
    columns = lax.all_gather(slices, "mp", axis=0, axis_index_groups=GROUPS)
    rows_other = swap(rows_own, 1).reshape(feat // 2, total)
    rows_own = rows_own.reshape(feat // 2, total)

    def gradient_of(rows_a, with_diagonal):
        correlation = (
            lax.dot_general(rows_a, columns_b, (((1,), (1,)), ((), ())), preferred_element_type=jnp.float32)
            / total
        )
        inner = 2.0 * redundancy_weight * correlation
        if with_diagonal:
            row = lax.broadcasted_iota(jnp.int32, correlation.shape, 0)
            column = lax.broadcasted_iota(jnp.int32, correlation.shape, 1)
            diagonal = (row < block) & (column == lax.rem(model_index, Y) * 2 * block + row)
            inner = inner + diagonal.astype(jnp.float32) * (2.0 * (correlation - 1.0) - inner)
        return (loss_scale * inner).astype(jnp.bfloat16)

    corr_own = gradient_of(rows_own, True)
    corr_other = gradient_of(rows_other, False)

    def times(lhs, rhs, dims):
        return lax.dot_general(lhs, rhs, (dims, ((), ())), preferred_element_type=jnp.float32) / total

    half = (feat // 2, Y, 2, block)
    sides = [
        corr.reshape(half).transpose(2, 0, 1, 3).reshape(2, feat // 2, Y * block)
        for corr in (corr_own, corr_other)
    ]
    terms_b = [
        times(sides[0][k], rows_own, ((0,), (0,))) + times(sides[1][k], rows_other, ((0,), (0,)))
        for k in (0, 1)
    ]
    away = terms_b[1].astype(jnp.bfloat16)
    corr_own, corr_other, away = lax.optimization_barrier((corr_own, corr_other, away))
    terms_b = (terms_b[0] + partner(away).astype(jnp.float32)).astype(jnp.bfloat16)
    terms_b = lax.all_to_all(
        terms_b.reshape(Y, block, total), "mp", split_axis=0, concat_axis=0, axis_index_groups=GROUPS
    )
    terms_other = times(corr_other, columns_b, ((1,), (0,))).astype(jnp.bfloat16)
    terms_own = times(corr_own, columns_b, ((1,), (0,)))
    shape = (4, 4, block, total)
    terms_own, terms_other = terms_own.reshape(shape), swap(terms_other.reshape(shape), 1)
    both = [(terms_own[k] + terms_other[k].astype(jnp.float32)).astype(jnp.bfloat16) for k in range(X)]
    along_x = add(both, ALONG_X)[0].astype(jnp.bfloat16)
    grad_a, terms_b = add(along_x, STRIDED_Z, terms_b)
    grads = jnp.stack([grad_a, jnp.sum(terms_b.astype(jnp.float32), axis=0)])
    wide = normed.astype(jnp.float32)
    grad_mean = jnp.sum(grads, axis=2, keepdims=True) / total
    cross_mean = jnp.sum(grads * wide, axis=2, keepdims=True) / total
    grad_proj = ((grads - grad_mean - wide * cross_mean) * inverse).astype(jnp.bfloat16)
    images_x = total // X
    depth = views * images_x
    blocks = [
        jnp.concatenate([grad_proj[v, :, x * images_x : (x + 1) * images_x] for v in range(views)], axis=1)
        for x in range(X)
    ]
    grad_own = lax.all_to_all(
        jnp.stack([part for part in blocks for _ in range(DP // X // 2)]),
        "dp",
        split_axis=0,
        concat_axis=0,
        axis_index_groups=SAME_CORE,
    )
    grad_own, columns = lax.optimization_barrier((grad_own, columns))
    grad_other = swap(grad_own, 1)
    targets = data_index >> 3 ^ jnp.asarray(X_SLOTS, jnp.int32)
    terms = weight_half(targets, grad_own.reshape(feat // 2, depth), columns)
    terms = weight_half(targets, grad_other.reshape(feat // 2, depth), columns, *terms)
    return finish(position, [terms[0]] + [swap(terms[k + 1], *mask) for k, mask in enumerate(ALONG_X)])


def solution(mesh):
    placed = (P(None, "dp", None), P("dp", "mp"))
    return jax.shard_map(
        per_device, mesh=mesh, in_specs=placed, out_specs=P("dp", "mp"), check_vma=False
    )
```

```python
import functools

import jax
import jax.numpy as jnp
import numpy as np
from jax import lax
from jax.experimental import pallas as pl
from jax.experimental.pallas import tpu as pltpu
from jax.sharding import PartitionSpec as P

epsilon = 1e-05
redundancy_weight = 0.0051
loss_scale = 512.0
DP = 32
MP = 16
Y = 8
X = 4
GROUPS = [list(range(Y)), list(range(Y, MP))]
SAME_CORE = [list(range(core, DP, 2)) for core in range(2)]
SAME_X = [list(range(x * DP // X, (x + 1) * DP // X)) for x in range(X)]
X_SLOTS = np.array([0, 2, 1, 3])
Z_SLOTS = np.array([0, 3, 2, 1])
ALONG_X = [(8 * int(k),) for k in X_SLOTS[1:]]
ALONG_Z = [(2 * int(k),) for k in Z_SLOTS[1:]]
STRIDED_Z = [(0, 8), (4,), (4, 8)]


def swap(array, data, model=0):
    mask = data * MP + model
    return lax.ppermute(array, ("dp", "mp"), [(i, i ^ mask) for i in range(DP * MP)])


def partner(array):
    return swap(array, 2)


def gather(block, masks, *later):
    parts = [block] + [swap(block, *mask) for mask in masks]
    if later:
        parts[1], *later = lax.optimization_barrier((parts[1], *later))
    return jnp.stack(parts), *later


def add(blocks, masks, *later):
    parts = [blocks[0]] + [swap(blocks[k + 1], *mask) for k, mask in enumerate(masks)]
    parts, later = lax.optimization_barrier((parts, later))
    return sum(part.astype(jnp.float32) for part in parts), *later


def project_kernel(last, order_ref, inputs_ref, own_ref, other_ref, *refs):
    out_ref = refs[-1]
    blocks, depth, _ = own_ref.shape
    result = refs[0][...] if last else None
    for core, weight_ref in enumerate((own_ref, other_ref)):
        for k in range(blocks):
            start = pl.multiple_of(order_ref[core * blocks + k] * depth, depth)
            part = jnp.dot(
                inputs_ref[:, pl.ds(start, depth)], weight_ref[k], preferred_element_type=jnp.float32
            )
            result = part if result is None else result + part
    if not last:
        out_ref[...] = result
        return
    features = result.T
    rows = features.shape[1]
    out_ref[:, :rows] = features
    for j in range(DP):
        k = 8 * (j ^ 2)
        out_ref[8 * j : 8 * j + 8, rows:] = features[k : k + 8, rows // 2 :]


def project(order, inputs, own, other, *before):
    rows, feat = inputs.shape[0], own.shape[2]
    vmem = pl.BlockSpec(memory_space=pltpu.VMEM)
    return pl.pallas_call(
        functools.partial(project_kernel, bool(before)),
        in_specs=[pl.BlockSpec(memory_space=pltpu.SMEM)] + [vmem] * (3 + len(before)),
        out_specs=vmem,
        out_shape=jax.ShapeDtypeStruct((feat, rows // 2 * 3) if before else (rows, feat), jnp.float32),
        compiler_params=pltpu.CompilerParams(vmem_limit_bytes=16 * 1024 * 1024),
        cost_estimate=pl.CostEstimate(
            flops=4 * rows * feat * own.shape[0] * own.shape[1],
            bytes_accessed=6 * 1024 * 1024,
            transcendentals=0,
        ),
    )(order, inputs, own, other, *before)


def weight_kernel(targets_ref, grad_ref, columns_ref, *refs):
    before, outs = refs[:-X], refs[-X:]
    slices, devices, share, wide = columns_ref.shape
    rows = wide // X
    half = slices // 2
    features = grad_ref.shape[0]
    for k in range(X):
        target = pl.ds(pl.multiple_of(targets_ref[k] * rows, rows), rows)
        pieces = [
            columns_ref[half * view : half * (view + 1), d, :, target].reshape(half * share, rows)
            for view in range(2)
            for d in range(devices)
        ]
        columns = jnp.concatenate(pieces, axis=0)
        result = jnp.dot(grad_ref[...], columns, preferred_element_type=jnp.float32)
        if before:
            outs[k][:features] = before[k][...]
            outs[k][features:] = result
        else:
            outs[k][...] = result


def weight_half(targets, grad, columns, *before):
    half, depth = grad.shape
    wide = columns.shape[3]
    features = 2 * half if before else half
    vmem = pl.BlockSpec(memory_space=pltpu.VMEM)
    return pl.pallas_call(
        weight_kernel,
        in_specs=[pl.BlockSpec(memory_space=pltpu.SMEM)] + [vmem] * (2 + len(before)),
        out_specs=[vmem] * X,
        out_shape=[jax.ShapeDtypeStruct((features, wide // X), jnp.float32)] * X,
        compiler_params=pltpu.CompilerParams(vmem_limit_bytes=16 * 1024 * 1024),
        cost_estimate=pl.CostEstimate(
            flops=2 * half * depth * wide, bytes_accessed=5 * 1024 * 1024, transcendentals=0
        ),
    )(targets, grad, columns, *before)


def finish_kernel(position_ref, *refs):
    *terms, out_ref, total_ref = refs
    total_ref[...] = (terms[0][...] + terms[1][...]) + (terms[2][...] + terms[3][...])
    blocks = [total_ref[pl.ds(pl.multiple_of(position_ref[j] * 8, 8), 8)] for j in range(DP)]
    out_ref[...] = jnp.concatenate(blocks, axis=0).T


def finish(position, terms):
    features, rows = terms[0].shape
    vmem = pl.BlockSpec(memory_space=pltpu.VMEM)
    return pl.pallas_call(
        finish_kernel,
        in_specs=[pl.BlockSpec(memory_space=pltpu.SMEM)] + [vmem] * len(terms),
        out_specs=vmem,
        out_shape=jax.ShapeDtypeStruct((rows, features), jnp.float32),
        scratch_shapes=[pltpu.VMEM((features, rows), jnp.float32)],
        compiler_params=pltpu.CompilerParams(vmem_limit_bytes=16 * 1024 * 1024),
    )(position, *terms)


def per_device(inputs, weight):
    views, images, width = inputs.shape
    total = images * DP
    data_index = lax.axis_index("dp")
    model_index = lax.axis_index("mp")
    feat = weight.shape[1]
    block = feat // DP
    rows = width // DP
    flat = inputs.reshape(views * images, width)

    place = np.arange(DP)
    distance = place >> 4 | X_SLOTS[place >> 2 & 3] << 3 | Z_SLOTS[place & 3] << 1
    position = (data_index & 1 ^ jnp.asarray(place & 1, jnp.int32)) << 4 | jnp.asarray(place >> 1, jnp.int32)

    share = views * images // Y
    mine = lax.dynamic_slice_in_dim(flat, lax.rem(model_index, Y) * share, share, axis=0)
    pieces = mine.reshape(share, X, DP // X, rows).transpose(2, 0, 1, 3).reshape(DP // X, share, X * rows)
    along_z = gather(weight, ALONG_Z)[0]
    parts = [along_z] + [swap(along_z, *mask) for mask in ALONG_X]
    projected = ()
    for k in (0, 2):
        weight_own, pieces = lax.optimization_barrier((jnp.stack(parts[k : k + 2]), pieces))
        weight_other = swap(weight_own, 1)
        blocks = np.concatenate([4 * k + np.arange(8), 16 + 4 * k + np.arange(8)])
        half = (DP // 4, rows, feat)
        order = data_index ^ jnp.asarray(distance[blocks], jnp.int32)
        halves = weight_own.reshape(half), weight_other.reshape(half)
        projected = (project(order, flat, *halves, *projected),)
    projected = projected[0]

    own = lax.all_to_all(
        projected.reshape(DP, block, (views + 1) * images), "dp", split_axis=0, concat_axis=0
    ).reshape(DP, block, views + 1, images)
    average = jnp.sum(own, axis=(0, 3), keepdims=True) / total
    centered = own - average
    variance = jnp.sum(centered * centered, axis=(0, 3), keepdims=True) / total
    inverse = lax.rsqrt(variance + epsilon)
    normed = (centered * inverse).astype(jnp.bfloat16).transpose(2, 1, 0, 3).reshape(views + 1, block, total)
    inverse = inverse.reshape(block, views + 1).T[:views, :, None]

    first, pair, pieces = lax.optimization_barrier((normed[0], normed[1:], pieces))
    slices = lax.all_to_all(
        pieces, "dp", split_axis=0, concat_axis=0, axis_index_groups=SAME_X
    )
    columns_b = lax.all_gather(pair, "mp", axis=0, axis_index_groups=GROUPS)
    columns_b = columns_b.reshape(MP * block, total)
    rows_own, slices = gather(gather(first, STRIDED_Z)[0], ALONG_X, slices)
    rows_own, columns_b = lax.optimization_barrier((rows_own, columns_b))
    columns = lax.all_gather(slices, "mp", axis=0, axis_index_groups=GROUPS)
    rows_other = swap(rows_own, 1).reshape(feat // 2, total)
    rows_own = rows_own.reshape(feat // 2, total)

    def gradient_of(rows_a, with_diagonal):
        correlation = (
            lax.dot_general(rows_a, columns_b, (((1,), (1,)), ((), ())), preferred_element_type=jnp.float32)
            / total
        )
        inner = 2.0 * redundancy_weight * correlation
        if with_diagonal:
            row = lax.broadcasted_iota(jnp.int32, correlation.shape, 0)
            column = lax.broadcasted_iota(jnp.int32, correlation.shape, 1)
            diagonal = (row < block) & (column == lax.rem(model_index, Y) * 2 * block + row)
            inner = inner + diagonal.astype(jnp.float32) * (2.0 * (correlation - 1.0) - inner)
        return (loss_scale * inner).astype(jnp.bfloat16)

    corr_own = gradient_of(rows_own, True)
    corr_other = gradient_of(rows_other, False)

    def times(lhs, rhs, dims):
        return lax.dot_general(lhs, rhs, (dims, ((), ())), preferred_element_type=jnp.float32) / total

    half = (feat // 2, Y, 2, block)
    sides = [
        corr.reshape(half).transpose(2, 0, 1, 3).reshape(2, feat // 2, Y * block)
        for corr in (corr_own, corr_other)
    ]
    terms_b = [
        times(sides[0][k], rows_own, ((0,), (0,))) + times(sides[1][k], rows_other, ((0,), (0,)))
        for k in (0, 1)
    ]
    away = terms_b[1].astype(jnp.bfloat16)
    corr_own, corr_other, away = lax.optimization_barrier((corr_own, corr_other, away))
    terms_b = (terms_b[0] + partner(away).astype(jnp.float32)).astype(jnp.bfloat16)
    terms_b = lax.all_to_all(
        terms_b.reshape(Y, block, total), "mp", split_axis=0, concat_axis=0, axis_index_groups=GROUPS
    )
    terms_other = times(corr_other, columns_b, ((1,), (0,))).astype(jnp.bfloat16)
    terms_own = times(corr_own, columns_b, ((1,), (0,)))
    shape = (4, 4, block, total)
    terms_own, terms_other = terms_own.reshape(shape), swap(terms_other.reshape(shape), 1)
    both = [(terms_own[k] + terms_other[k].astype(jnp.float32)).astype(jnp.bfloat16) for k in range(X)]
    along_x = add(both, ALONG_X)[0].astype(jnp.bfloat16)
    grad_a, terms_b = add(along_x, STRIDED_Z, terms_b)
    grads = jnp.stack([grad_a, jnp.sum(terms_b.astype(jnp.float32), axis=0)])
    wide = normed[:views].astype(jnp.float32)
    grad_mean = jnp.sum(grads, axis=2, keepdims=True) / total
    cross_mean = jnp.sum(grads * wide, axis=2, keepdims=True) / total
    grad_proj = ((grads - grad_mean - wide * cross_mean) * inverse).astype(jnp.bfloat16)
    images_x = total // X
    depth = views * images_x
    blocks = [
        jnp.concatenate([grad_proj[v, :, x * images_x : (x + 1) * images_x] for v in range(views)], axis=1)
        for x in range(X)
    ]
    grad_own = lax.all_to_all(
        jnp.stack([part for part in blocks for _ in range(DP // X // 2)]),
        "dp",
        split_axis=0,
        concat_axis=0,
        axis_index_groups=SAME_CORE,
    )
    grad_own, columns = lax.optimization_barrier((grad_own, columns))
    grad_other = swap(grad_own, 1)
    targets = data_index >> 3 ^ jnp.asarray(X_SLOTS, jnp.int32)
    terms = weight_half(targets, grad_own.reshape(feat // 2, depth), columns)
    terms = weight_half(targets, grad_other.reshape(feat // 2, depth), columns, *terms)
    return finish(position, [terms[0]] + [swap(terms[k + 1], *mask) for k, mask in enumerate(ALONG_X)])


def solution(mesh):
    placed = (P(None, "dp", None), P("dp", "mp"))
    return jax.shard_map(
        per_device, mesh=mesh, in_specs=placed, out_specs=P("dp", "mp"), check_vma=False
    )
```

```python
import functools

import jax
import jax.numpy as jnp
import numpy as np
from jax import lax
from jax.experimental import pallas as pl
from jax.experimental.pallas import tpu as pltpu
from jax.sharding import PartitionSpec as P

epsilon = 1e-05
redundancy_weight = 0.0051
loss_scale = 512.0
DP = 32
MP = 16
Y = 8
X = 4
GROUPS = [list(range(Y)), list(range(Y, MP))]
SAME_CORE = [list(range(core, DP, 2)) for core in range(2)]
X_SLOTS = np.array([0, 2, 1, 3])
Z_SLOTS = np.array([0, 3, 2, 1])
ALONG_X = [(8 * int(k),) for k in X_SLOTS[1:]]
ALONG_Z = [(2 * int(k),) for k in Z_SLOTS[1:]]
STRIDED_Z = [(0, 8), (4,), (4, 8)]


def swap(array, data, model=0):
    mask = data * MP + model
    return lax.ppermute(array, ("dp", "mp"), [(i, i ^ mask) for i in range(DP * MP)])


def partner(array):
    return swap(array, 2)


def along_ring(array, step):
    pairs = []
    for i in range(DP * MP):
        data, model = divmod(i, MP)
        z = (model // Y * 4 + data // 2 % 4 + step) % 8
        target = (data // 8 * 8 + z % 4 * 2 + data % 2) * MP + z // 4 * Y + model % Y
        pairs.append((i, target))
    return lax.ppermute(array, ("dp", "mp"), pairs)


def gather(block, masks, *later):
    parts = [block] + [swap(block, *mask) for mask in masks]
    if later:
        parts[1], *later = lax.optimization_barrier((parts[1], *later))
    return jnp.stack(parts), *later


def add(blocks, masks, *later):
    parts = [blocks[0]] + [swap(blocks[k + 1], *mask) for k, mask in enumerate(masks)]
    parts, later = lax.optimization_barrier((parts, later))
    return sum(part.astype(jnp.float32) for part in parts), *later


def project_kernel(last, order_ref, inputs_ref, own_ref, other_ref, *refs):
    out_ref = refs[-1]
    blocks, depth, _ = own_ref.shape
    result = refs[0][...] if last else None
    for core, weight_ref in enumerate((own_ref, other_ref)):
        for k in range(blocks):
            start = pl.multiple_of(order_ref[core * blocks + k] * depth, depth)
            part = jnp.dot(
                inputs_ref[:, pl.ds(start, depth)], weight_ref[k], preferred_element_type=jnp.float32
            )
            result = part if result is None else result + part
    if not last:
        out_ref[...] = result
        return
    features = result.T
    rows = features.shape[1]
    out_ref[:, :rows] = features
    for j in range(DP):
        k = 8 * (j ^ 2)
        out_ref[8 * j : 8 * j + 8, rows:] = features[k : k + 8, rows // 2 :]


def project(order, inputs, own, other, *before):
    rows, feat = inputs.shape[0], own.shape[2]
    vmem = pl.BlockSpec(memory_space=pltpu.VMEM)
    return pl.pallas_call(
        functools.partial(project_kernel, bool(before)),
        in_specs=[pl.BlockSpec(memory_space=pltpu.SMEM)] + [vmem] * (3 + len(before)),
        out_specs=vmem,
        out_shape=jax.ShapeDtypeStruct((feat, rows // 2 * 3) if before else (rows, feat), jnp.float32),
        compiler_params=pltpu.CompilerParams(vmem_limit_bytes=16 * 1024 * 1024),
        cost_estimate=pl.CostEstimate(
            flops=4 * rows * feat * own.shape[0] * own.shape[1],
            bytes_accessed=6 * 1024 * 1024,
            transcendentals=0,
        ),
    )(order, inputs, own, other, *before)


def weight_kernel(targets_ref, sources_ref, grad_ref, own_ref, other_ref, *refs):
    before, outs = refs[:-X], refs[-X:]
    features, depth = grad_ref.shape
    places, share, wide = own_ref.shape
    rows, images = wide // X, share // 2
    pieces = []
    for view in range(2):
        for k in range(2 * places):
            start = view * (depth // 2) + sources_ref[k] * images
            pieces.append(grad_ref[:, pl.ds(pl.multiple_of(start, images), images)])
    grad = jnp.concatenate(pieces, axis=1)
    for k in range(X):
        target = pl.ds(pl.multiple_of(targets_ref[k] * rows, rows), rows)
        pieces = [
            ref[place, images * view : images * (view + 1), target]
            for view in range(2)
            for ref in (own_ref, other_ref)
            for place in range(places)
        ]
        columns = jnp.concatenate(pieces, axis=0)
        result = jnp.dot(grad, columns, preferred_element_type=jnp.float32)
        if before:
            outs[k][:features] = before[k][...]
            outs[k][features:] = result
        else:
            outs[k][...] = result


def weight_half(targets, grad, sources, own, other, *before):
    half, depth = grad.shape
    wide = own.shape[2]
    features = 2 * half if before else half
    smem, vmem = pl.BlockSpec(memory_space=pltpu.SMEM), pl.BlockSpec(memory_space=pltpu.VMEM)
    return pl.pallas_call(
        weight_kernel,
        in_specs=[smem, smem] + [vmem] * (3 + len(before)),
        out_specs=[vmem] * X,
        out_shape=[jax.ShapeDtypeStruct((features, wide // X), jnp.float32)] * X,
        compiler_params=pltpu.CompilerParams(vmem_limit_bytes=16 * 1024 * 1024),
        cost_estimate=pl.CostEstimate(
            flops=2 * half * depth * wide, bytes_accessed=5 * 1024 * 1024, transcendentals=0
        ),
    )(targets, sources, grad, own, other, *before)


def finish_kernel(position_ref, *refs):
    *terms, out_ref, total_ref = refs
    total_ref[...] = (terms[0][...] + terms[1][...]) + (terms[2][...] + terms[3][...])
    blocks = [total_ref[pl.ds(pl.multiple_of(position_ref[j] * 8, 8), 8)] for j in range(DP)]
    out_ref[...] = jnp.concatenate(blocks, axis=0).T


def finish(position, terms):
    features, rows = terms[0].shape
    vmem = pl.BlockSpec(memory_space=pltpu.VMEM)
    return pl.pallas_call(
        finish_kernel,
        in_specs=[pl.BlockSpec(memory_space=pltpu.SMEM)] + [vmem] * len(terms),
        out_specs=vmem,
        out_shape=jax.ShapeDtypeStruct((rows, features), jnp.float32),
        scratch_shapes=[pltpu.VMEM((features, rows), jnp.float32)],
        compiler_params=pltpu.CompilerParams(vmem_limit_bytes=16 * 1024 * 1024),
    )(position, *terms)


def per_device(inputs, weight):
    views, images, width = inputs.shape
    total = images * DP
    data_index = lax.axis_index("dp")
    model_index = lax.axis_index("mp")
    feat = weight.shape[1]
    block = feat // DP
    rows = width // DP
    flat = inputs.reshape(views * images, width)

    place = np.arange(DP)
    distance = place >> 4 | X_SLOTS[place >> 2 & 3] << 3 | Z_SLOTS[place & 3] << 1
    position = (data_index & 1 ^ jnp.asarray(place & 1, jnp.int32)) << 4 | jnp.asarray(place >> 1, jnp.int32)

    core, z = data_index & 1, data_index >> 1 & 3
    by_place = flat.reshape(views * images, X, 4, 2, rows)

    def piece(step, other):
        start = (0, 0, z + step & 3, core ^ other, 0)
        taken = lax.dynamic_slice(by_place, start, (views * images, X, 1, 1, rows))
        return taken.reshape(views * images, X * rows)

    steps = (0, 2, 1, -1)
    columns = [jnp.stack([piece(step, other) for other in (0, 1)]) for step in steps]
    sources = jnp.stack([(z - step & 3) * 2 + (core ^ other) for other in (0, 1) for step in steps])

    along_z = gather(weight, ALONG_Z)[0]
    parts = [along_z] + [swap(along_z, *mask) for mask in ALONG_X]
    projected = ()
    for k in (0, 2):
        weight_own = jnp.stack(parts[k : k + 2])
        if k == 0:
            weight_own, columns = lax.optimization_barrier((weight_own, columns))
            columns[1] = along_ring(columns[1], steps[1])
        weight_other = swap(weight_own, 1)
        blocks = np.concatenate([4 * k + np.arange(8), 16 + 4 * k + np.arange(8)])
        half = (DP // 4, rows, feat)
        order = data_index ^ jnp.asarray(distance[blocks], jnp.int32)
        halves = weight_own.reshape(half), weight_other.reshape(half)
        projected = (project(order, flat, *halves, *projected),)
    projected = projected[0]

    own = lax.all_to_all(
        projected.reshape(DP, block, (views + 1) * images), "dp", split_axis=0, concat_axis=0
    ).reshape(DP, block, views + 1, images)
    average = jnp.sum(own, axis=(0, 3), keepdims=True) / total
    centered = own - average
    variance = jnp.sum(centered * centered, axis=(0, 3), keepdims=True) / total
    inverse = lax.rsqrt(variance + epsilon)
    normed = (centered * inverse).astype(jnp.bfloat16).transpose(2, 1, 0, 3).reshape(views + 1, block, total)
    inverse = inverse.reshape(block, views + 1).T[:views, :, None]

    first, pair, columns = lax.optimization_barrier((normed[0], normed[1:], columns))
    columns[2:] = [along_ring(part, step) for part, step in zip(columns[2:], steps[2:])]
    copies = jnp.broadcast_to(pair[None], (Y,) + pair.shape)
    columns_b = lax.all_to_all(copies, "mp", split_axis=0, concat_axis=0, axis_index_groups=GROUPS)
    columns_b = columns_b.reshape(MP * block, total)
    rows_own = gather(gather(first, STRIDED_Z)[0], ALONG_X)[0]
    rows_own, columns_b = lax.optimization_barrier((rows_own, columns_b))
    rows_other = swap(rows_own, 1).reshape(feat // 2, total)
    rows_own = rows_own.reshape(feat // 2, total)

    def gradient_of(rows_a, with_diagonal):
        correlation = (
            lax.dot_general(rows_a, columns_b, (((1,), (1,)), ((), ())), preferred_element_type=jnp.float32)
            / total
        )
        inner = 2.0 * redundancy_weight * correlation
        if with_diagonal:
            row = lax.broadcasted_iota(jnp.int32, correlation.shape, 0)
            column = lax.broadcasted_iota(jnp.int32, correlation.shape, 1)
            diagonal = (row < block) & (column == lax.rem(model_index, Y) * 2 * block + row)
            inner = inner + diagonal.astype(jnp.float32) * (2.0 * (correlation - 1.0) - inner)
        return (loss_scale * inner).astype(jnp.bfloat16)

    corr_own = gradient_of(rows_own, True)
    corr_other = gradient_of(rows_other, False)

    def times(lhs, rhs, dims):
        return lax.dot_general(lhs, rhs, (dims, ((), ())), preferred_element_type=jnp.float32) / total

    half = (feat // 2, Y, 2, block)
    sides = [
        corr.reshape(half).transpose(2, 0, 1, 3).reshape(2, feat // 2, Y * block)
        for corr in (corr_own, corr_other)
    ]
    terms_b = [
        times(sides[0][k], rows_own, ((0,), (0,))) + times(sides[1][k], rows_other, ((0,), (0,)))
        for k in (0, 1)
    ]
    away = terms_b[1].astype(jnp.bfloat16)
    corr_own, corr_other, away = lax.optimization_barrier((corr_own, corr_other, away))
    terms_b = (terms_b[0] + partner(away).astype(jnp.float32)).astype(jnp.bfloat16)
    terms_b = lax.all_to_all(
        terms_b.reshape(Y, block, total), "mp", split_axis=0, concat_axis=0, axis_index_groups=GROUPS
    )
    terms_other = times(corr_other, columns_b, ((1,), (0,))).astype(jnp.bfloat16)
    terms_own = times(corr_own, columns_b, ((1,), (0,)))
    shape = (4, 4, block, total)
    terms_own, terms_other = terms_own.reshape(shape), swap(terms_other.reshape(shape), 1)
    both = [(terms_own[k] + terms_other[k].astype(jnp.float32)).astype(jnp.bfloat16) for k in range(X)]
    along_x = add(both, ALONG_X)[0].astype(jnp.bfloat16)
    along_x, columns = lax.optimization_barrier((along_x, columns))
    columns_own = jnp.stack([part[0] for part in columns])
    columns_other = swap(jnp.stack([part[1] for part in columns]), 1)
    grad_a, terms_b, columns_own, columns_other = add(
        along_x, STRIDED_Z, terms_b, columns_own, columns_other
    )
    grads = jnp.stack([grad_a, jnp.sum(terms_b.astype(jnp.float32), axis=0)])
    wide = normed[:views].astype(jnp.float32)
    grad_mean = jnp.sum(grads, axis=2, keepdims=True) / total
    cross_mean = jnp.sum(grads * wide, axis=2, keepdims=True) / total
    grad_proj = ((grads - grad_mean - wide * cross_mean) * inverse).astype(jnp.bfloat16)
    images_x = total // X
    depth = views * images_x
    blocks = [
        jnp.concatenate([grad_proj[v, :, x * images_x : (x + 1) * images_x] for v in range(views)], axis=1)
        for x in range(X)
    ]
    grad_own = lax.all_to_all(
        jnp.stack([part for part in blocks for _ in range(DP // X // 2)]),
        "dp",
        split_axis=0,
        concat_axis=0,
        axis_index_groups=SAME_CORE,
    )
    grad_other = swap(grad_own, 1)
    targets = data_index >> 3 ^ jnp.asarray(X_SLOTS, jnp.int32)
    columns = (sources, columns_own, columns_other)
    terms = weight_half(targets, grad_own.reshape(feat // 2, depth), *columns)
    terms = weight_half(targets, grad_other.reshape(feat // 2, depth), *columns, *terms)
    return finish(position, [terms[0]] + [swap(terms[k + 1], *mask) for k, mask in enumerate(ALONG_X)])


def solution(mesh):
    placed = (P(None, "dp", None), P("dp", "mp"))
    return jax.shard_map(
        per_device, mesh=mesh, in_specs=placed, out_specs=P("dp", "mp"), check_vma=False
    )
```

```python
import functools

import jax
import jax.numpy as jnp
import numpy as np
from jax import lax
from jax.experimental import pallas as pl
from jax.experimental.pallas import tpu as pltpu
from jax.sharding import PartitionSpec as P

epsilon = 1e-05
redundancy_weight = 0.0051
loss_scale = 512.0
DP = 32
MP = 16
Y = 8
X = 4
GROUPS = [list(range(Y)), list(range(Y, MP))]
SAME_CORE = [list(range(core, DP, 2)) for core in range(2)]
SAME_X = [list(range(x * DP // X, (x + 1) * DP // X)) for x in range(X)]
X_SLOTS = np.array([0, 2, 1, 3])
Z_SLOTS = np.array([0, 3, 2, 1])
ALONG_X = [(8 * int(k),) for k in X_SLOTS[1:]]
ALONG_Z = [(2 * int(k),) for k in Z_SLOTS[1:]]
STRIDED_Z = [(0, 8), (4,), (4, 8)]


def swap(array, data, model=0):
    mask = data * MP + model
    return lax.ppermute(array, ("dp", "mp"), [(i, i ^ mask) for i in range(DP * MP)])


def partner(array):
    return swap(array, 2)


def gather(block, masks, *later):
    parts = [block] + [swap(block, *mask) for mask in masks]
    if later:
        parts[1], *later = lax.optimization_barrier((parts[1], *later))
    return jnp.stack(parts), *later


def add(blocks, masks, *later):
    parts = [blocks[0]] + [swap(blocks[k + 1], *mask) for k, mask in enumerate(masks)]
    parts, later = lax.optimization_barrier((parts, later))
    return sum(part.astype(jnp.float32) for part in parts), *later


def project_kernel(last, order_ref, inputs_ref, own_ref, other_ref, *refs):
    out_ref = refs[-1]
    blocks, depth, _ = own_ref.shape
    result = refs[0][...] if last else None
    for core, weight_ref in enumerate((own_ref, other_ref)):
        for k in range(blocks):
            start = pl.multiple_of(order_ref[core * blocks + k] * depth, depth)
            part = jnp.dot(
                inputs_ref[:, pl.ds(start, depth)], weight_ref[k], preferred_element_type=jnp.float32
            )
            result = part if result is None else result + part
    if not last:
        out_ref[...] = result
        return
    features = result.T
    rows = features.shape[1]
    out_ref[:, :rows] = features
    for j in range(DP):
        k = 8 * (j ^ 2)
        out_ref[8 * j : 8 * j + 8, rows:] = features[k : k + 8, rows // 2 :]


def project(order, inputs, own, other, *before):
    rows, feat = inputs.shape[0], own.shape[2]
    vmem = pl.BlockSpec(memory_space=pltpu.VMEM)
    return pl.pallas_call(
        functools.partial(project_kernel, bool(before)),
        in_specs=[pl.BlockSpec(memory_space=pltpu.SMEM)] + [vmem] * (3 + len(before)),
        out_specs=vmem,
        out_shape=jax.ShapeDtypeStruct((feat, rows // 2 * 3) if before else (rows, feat), jnp.float32),
        compiler_params=pltpu.CompilerParams(vmem_limit_bytes=16 * 1024 * 1024),
        cost_estimate=pl.CostEstimate(
            flops=4 * rows * feat * own.shape[0] * own.shape[1],
            bytes_accessed=6 * 1024 * 1024,
            transcendentals=0,
        ),
    )(order, inputs, own, other, *before)


def weight_kernel(targets_ref, grad_ref, columns_ref, *refs):
    before, outs = refs[:-X], refs[-X:]
    slices, devices, share, wide = columns_ref.shape
    rows = wide // X
    half = slices // 2
    features = grad_ref.shape[0]
    for k in range(X):
        target = pl.ds(pl.multiple_of(targets_ref[k] * rows, rows), rows)
        pieces = [
            columns_ref[half * view : half * (view + 1), d, :, target].reshape(half * share, rows)
            for view in range(2)
            for d in range(devices)
        ]
        columns = jnp.concatenate(pieces, axis=0)
        result = jnp.dot(grad_ref[...], columns, preferred_element_type=jnp.float32)
        if before:
            outs[k][:features] = before[k][...]
            outs[k][features:] = result
        else:
            outs[k][...] = result


def weight_half(targets, grad, columns, *before):
    half, depth = grad.shape
    wide = columns.shape[3]
    features = 2 * half if before else half
    vmem = pl.BlockSpec(memory_space=pltpu.VMEM)
    return pl.pallas_call(
        weight_kernel,
        in_specs=[pl.BlockSpec(memory_space=pltpu.SMEM)] + [vmem] * (2 + len(before)),
        out_specs=[vmem] * X,
        out_shape=[jax.ShapeDtypeStruct((features, wide // X), jnp.float32)] * X,
        compiler_params=pltpu.CompilerParams(vmem_limit_bytes=16 * 1024 * 1024),
        cost_estimate=pl.CostEstimate(
            flops=2 * half * depth * wide, bytes_accessed=5 * 1024 * 1024, transcendentals=0
        ),
    )(targets, grad, columns, *before)


def finish_kernel(position_ref, *refs):
    *terms, out_ref, total_ref = refs
    total_ref[...] = (terms[0][...] + terms[1][...]) + (terms[2][...] + terms[3][...])
    blocks = [total_ref[pl.ds(pl.multiple_of(position_ref[j] * 8, 8), 8)] for j in range(DP)]
    out_ref[...] = jnp.concatenate(blocks, axis=0).T


def finish(position, terms):
    features, rows = terms[0].shape
    vmem = pl.BlockSpec(memory_space=pltpu.VMEM)
    return pl.pallas_call(
        finish_kernel,
        in_specs=[pl.BlockSpec(memory_space=pltpu.SMEM)] + [vmem] * len(terms),
        out_specs=vmem,
        out_shape=jax.ShapeDtypeStruct((rows, features), jnp.float32),
        scratch_shapes=[pltpu.VMEM((features, rows), jnp.float32)],
        compiler_params=pltpu.CompilerParams(vmem_limit_bytes=16 * 1024 * 1024),
    )(position, *terms)


def per_device(inputs, weight):
    views, images, width = inputs.shape
    total = images * DP
    data_index = lax.axis_index("dp")
    model_index = lax.axis_index("mp")
    feat = weight.shape[1]
    block = feat // DP
    rows = width // DP
    flat = inputs.reshape(views * images, width)

    place = np.arange(DP)
    distance = place >> 4 | X_SLOTS[place >> 2 & 3] << 3 | Z_SLOTS[place & 3] << 1
    position = (data_index & 1 ^ jnp.asarray(place & 1, jnp.int32)) << 4 | jnp.asarray(place >> 1, jnp.int32)

    share = views * images // Y
    mine = lax.dynamic_slice_in_dim(flat, lax.rem(model_index, Y) * share, share, axis=0)
    pieces = mine.reshape(share, X, DP // X, rows).transpose(2, 0, 1, 3).reshape(DP // X, share, X * rows)
    along_z, pieces = gather(weight, ALONG_Z, pieces)
    slices = lax.all_to_all(
        pieces, "dp", split_axis=0, concat_axis=0, axis_index_groups=SAME_X
    )
    parts = [along_z] + [swap(along_z, *mask) for mask in ALONG_X]
    projected = ()
    for k in (0, 2):
        weight_own = jnp.stack(parts[k : k + 2])
        if k == 0:
            weight_own, slices = lax.optimization_barrier((weight_own, slices))
        weight_other = swap(weight_own, 1)
        blocks = np.concatenate([4 * k + np.arange(8), 16 + 4 * k + np.arange(8)])
        half = (DP // 4, rows, feat)
        order = data_index ^ jnp.asarray(distance[blocks], jnp.int32)
        halves = weight_own.reshape(half), weight_other.reshape(half)
        projected = (project(order, flat, *halves, *projected),)
    projected = projected[0]

    own = lax.all_to_all(
        projected.reshape(DP, block, (views + 1) * images), "dp", split_axis=0, concat_axis=0
    ).reshape(DP, block, views + 1, images)
    average = jnp.sum(own, axis=(0, 3), keepdims=True) / total
    centered = own - average
    variance = jnp.sum(centered * centered, axis=(0, 3), keepdims=True) / total
    inverse = lax.rsqrt(variance + epsilon)
    normed = (centered * inverse).astype(jnp.bfloat16).transpose(2, 1, 0, 3).reshape(views + 1, block, total)
    inverse = inverse.reshape(block, views + 1).T[:views, :, None]

    first, pair = lax.optimization_barrier((normed[0], normed[1:]))
    copies = jnp.broadcast_to(pair[None], (Y,) + pair.shape)
    columns_b = lax.all_to_all(copies, "mp", split_axis=0, concat_axis=0, axis_index_groups=GROUPS)
    columns_b = columns_b.reshape(MP * block, total)
    rows_own, columns_b = gather(gather(first, STRIDED_Z)[0], ALONG_X, columns_b)
    columns = lax.all_gather(slices, "mp", axis=0, axis_index_groups=GROUPS)
    rows_other = swap(rows_own, 1).reshape(feat // 2, total)
    rows_own = rows_own.reshape(feat // 2, total)

    def gradient_of(rows_a, with_diagonal):
        correlation = (
            lax.dot_general(rows_a, columns_b, (((1,), (1,)), ((), ())), preferred_element_type=jnp.float32)
            / total
        )
        inner = 2.0 * redundancy_weight * correlation
        if with_diagonal:
            row = lax.broadcasted_iota(jnp.int32, correlation.shape, 0)
            column = lax.broadcasted_iota(jnp.int32, correlation.shape, 1)
            diagonal = (row < block) & (column == lax.rem(model_index, Y) * 2 * block + row)
            inner = inner + diagonal.astype(jnp.float32) * (2.0 * (correlation - 1.0) - inner)
        return (loss_scale * inner).astype(jnp.bfloat16)

    corr_own = gradient_of(rows_own, True)
    corr_other = gradient_of(rows_other, False)

    def times(lhs, rhs, dims):
        return lax.dot_general(lhs, rhs, (dims, ((), ())), preferred_element_type=jnp.float32) / total

    half = (feat // 2, Y, 2, block)
    sides = [
        corr.reshape(half).transpose(2, 0, 1, 3).reshape(2, feat // 2, Y * block)
        for corr in (corr_own, corr_other)
    ]
    terms_b = [
        times(sides[0][k], rows_own, ((0,), (0,))) + times(sides[1][k], rows_other, ((0,), (0,)))
        for k in (0, 1)
    ]
    away = terms_b[1].astype(jnp.bfloat16)
    corr_own, corr_other, away, columns = lax.optimization_barrier(
        (corr_own, corr_other, away, columns)
    )
    terms_b = (terms_b[0] + partner(away).astype(jnp.float32)).astype(jnp.bfloat16)
    terms_b = lax.all_to_all(
        terms_b.reshape(Y, block, total), "mp", split_axis=0, concat_axis=0, axis_index_groups=GROUPS
    )
    terms_other = times(corr_other, columns_b, ((1,), (0,))).astype(jnp.bfloat16)
    terms_own = times(corr_own, columns_b, ((1,), (0,)))
    shape = (4, 4, block, total)
    terms_own, terms_other = terms_own.reshape(shape), swap(terms_other.reshape(shape), 1)
    both = [(terms_own[k] + terms_other[k].astype(jnp.float32)).astype(jnp.bfloat16) for k in range(X)]
    along_x = add(both, ALONG_X)[0].astype(jnp.bfloat16)
    grad_a, terms_b = add(along_x, STRIDED_Z, terms_b)
    grads = jnp.stack([grad_a, jnp.sum(terms_b.astype(jnp.float32), axis=0)])
    wide = normed[:views].astype(jnp.float32)
    grad_mean = jnp.sum(grads, axis=2, keepdims=True) / total
    cross_mean = jnp.sum(grads * wide, axis=2, keepdims=True) / total
    grad_proj = ((grads - grad_mean - wide * cross_mean) * inverse).astype(jnp.bfloat16)
    images_x = total // X
    depth = views * images_x
    blocks = [
        jnp.concatenate([grad_proj[v, :, x * images_x : (x + 1) * images_x] for v in range(views)], axis=1)
        for x in range(X)
    ]
    grad_own = lax.all_to_all(
        jnp.broadcast_to(jnp.stack(blocks)[:, None], (X, DP // X // 2, block, depth)).reshape(
            DP // 2, block, depth
        ),
        "dp",
        split_axis=0,
        concat_axis=0,
        axis_index_groups=SAME_CORE,
    )
    grad_other = swap(grad_own, 1)
    targets = data_index >> 3 ^ jnp.asarray(X_SLOTS, jnp.int32)
    terms = weight_half(targets, grad_own.reshape(feat // 2, depth), columns)
    terms = weight_half(targets, grad_other.reshape(feat // 2, depth), columns, *terms)
    return finish(position, [terms[0]] + [swap(terms[k + 1], *mask) for k, mask in enumerate(ALONG_X)])


def solution(mesh):
    placed = (P(None, "dp", None), P("dp", "mp"))
    return jax.shard_map(
        per_device, mesh=mesh, in_specs=placed, out_specs=P("dp", "mp"), check_vma=False
    )
```

```python
import functools

import jax
import jax.numpy as jnp
import numpy as np
from jax import lax
from jax.experimental import pallas as pl
from jax.experimental.pallas import tpu as pltpu
from jax.sharding import PartitionSpec as P

epsilon = 1e-05
redundancy_weight = 0.0051
loss_scale = 512.0
DP = 32
MP = 16
Y = 8
X = 4
GROUPS = [list(range(Y)), list(range(Y, MP))]
SAME_CORE = [list(range(core, DP, 2)) for core in range(2)]
SAME_X = [list(range(x * DP // X, (x + 1) * DP // X)) for x in range(X)]
X_SLOTS = np.array([0, 2, 1, 3])
Z_SLOTS = np.array([0, 3, 2, 1])
ALONG_X = [(8 * int(k),) for k in X_SLOTS[1:]]
ALONG_Z = [(2 * int(k),) for k in Z_SLOTS[1:]]
STRIDED_Z = [(0, 8), (4,), (4, 8)]


def swap(array, data, model=0):
    mask = data * MP + model
    return lax.ppermute(array, ("dp", "mp"), [(i, i ^ mask) for i in range(DP * MP)])


def partner(array):
    return swap(array, 2)


def gather(block, masks, *later):
    parts = [block] + [swap(block, *mask) for mask in masks]
    if later:
        parts[1], *later = lax.optimization_barrier((parts[1], *later))
    return jnp.stack(parts), *later


def add(blocks, masks, *later):
    parts = [blocks[0]] + [swap(blocks[k + 1], *mask) for k, mask in enumerate(masks)]
    parts, later = lax.optimization_barrier((parts, later))
    return sum(part.astype(jnp.float32) for part in parts), *later


def project_kernel(last, order_ref, inputs_ref, *refs):
    *weight_refs, out_ref = refs
    result = weight_refs.pop()[...] if last else None
    place = 0
    for weight_ref in weight_refs:
        blocks, depth, _ = weight_ref.shape
        for k in range(blocks):
            start = pl.multiple_of(order_ref[place] * depth, depth)
            place += 1
            part = jnp.dot(
                inputs_ref[:, pl.ds(start, depth)], weight_ref[k], preferred_element_type=jnp.float32
            )
            result = part if result is None else result + part
    if not last:
        out_ref[...] = result
        return
    features = result.T
    rows = features.shape[1]
    out_ref[:, :rows] = features
    for j in range(DP):
        k = 8 * (j ^ 2)
        out_ref[8 * j : 8 * j + 8, rows:] = features[k : k + 8, rows // 2 :]


def project(order, inputs, weights, *before):
    rows, feat = inputs.shape[0], weights[0].shape[2]
    vmem = pl.BlockSpec(memory_space=pltpu.VMEM)
    return pl.pallas_call(
        functools.partial(project_kernel, bool(before)),
        in_specs=[pl.BlockSpec(memory_space=pltpu.SMEM)] + [vmem] * (1 + len(weights) + len(before)),
        out_specs=vmem,
        out_shape=jax.ShapeDtypeStruct((feat, rows // 2 * 3) if before else (rows, feat), jnp.float32),
        compiler_params=pltpu.CompilerParams(vmem_limit_bytes=16 * 1024 * 1024),
        cost_estimate=pl.CostEstimate(
            flops=2 * rows * feat * order.shape[0] * feat,
            bytes_accessed=6 * 1024 * 1024,
            transcendentals=0,
        ),
    )(order, inputs, *weights, *before)


def weight_kernel(targets_ref, grad_ref, columns_ref, *refs):
    before, outs = refs[:-X], refs[-X:]
    slices, devices, share, wide = columns_ref.shape
    rows = wide // X
    half = slices // 2
    features = grad_ref.shape[0]
    for k in range(X):
        target = pl.ds(pl.multiple_of(targets_ref[k] * rows, rows), rows)
        pieces = [
            columns_ref[half * view : half * (view + 1), d, :, target].reshape(half * share, rows)
            for view in range(2)
            for d in range(devices)
        ]
        columns = jnp.concatenate(pieces, axis=0)
        result = jnp.dot(grad_ref[...], columns, preferred_element_type=jnp.float32)
        if before:
            outs[k][:features] = before[k][...]
            outs[k][features:] = result
        else:
            outs[k][...] = result


def weight_half(targets, grad, columns, *before):
    half, depth = grad.shape
    wide = columns.shape[3]
    features = 2 * half if before else half
    vmem = pl.BlockSpec(memory_space=pltpu.VMEM)
    return pl.pallas_call(
        weight_kernel,
        in_specs=[pl.BlockSpec(memory_space=pltpu.SMEM)] + [vmem] * (2 + len(before)),
        out_specs=[vmem] * X,
        out_shape=[jax.ShapeDtypeStruct((features, wide // X), jnp.float32)] * X,
        compiler_params=pltpu.CompilerParams(vmem_limit_bytes=16 * 1024 * 1024),
        cost_estimate=pl.CostEstimate(
            flops=2 * half * depth * wide, bytes_accessed=5 * 1024 * 1024, transcendentals=0
        ),
    )(targets, grad, columns, *before)


def finish_kernel(position_ref, *refs):
    *terms, out_ref, total_ref = refs
    total_ref[...] = (terms[0][...] + terms[1][...]) + (terms[2][...] + terms[3][...])
    blocks = [total_ref[pl.ds(pl.multiple_of(position_ref[j] * 8, 8), 8)] for j in range(DP)]
    out_ref[...] = jnp.concatenate(blocks, axis=0).T


def finish(position, terms):
    features, rows = terms[0].shape
    vmem = pl.BlockSpec(memory_space=pltpu.VMEM)
    return pl.pallas_call(
        finish_kernel,
        in_specs=[pl.BlockSpec(memory_space=pltpu.SMEM)] + [vmem] * len(terms),
        out_specs=vmem,
        out_shape=jax.ShapeDtypeStruct((rows, features), jnp.float32),
        scratch_shapes=[pltpu.VMEM((features, rows), jnp.float32)],
        compiler_params=pltpu.CompilerParams(vmem_limit_bytes=16 * 1024 * 1024),
    )(position, *terms)


def per_device(inputs, weight):
    views, images, width = inputs.shape
    total = images * DP
    data_index = lax.axis_index("dp")
    model_index = lax.axis_index("mp")
    feat = weight.shape[1]
    block = feat // DP
    rows = width // DP
    flat = inputs.reshape(views * images, width)

    place = np.arange(DP)
    distance = place >> 4 | X_SLOTS[place >> 2 & 3] << 3 | Z_SLOTS[place & 3] << 1
    position = (data_index & 1 ^ jnp.asarray(place & 1, jnp.int32)) << 4 | jnp.asarray(place >> 1, jnp.int32)

    share = views * images // Y
    mine = lax.dynamic_slice_in_dim(flat, lax.rem(model_index, Y) * share, share, axis=0)
    pieces = mine.reshape(share, X, DP // X, rows).transpose(2, 0, 1, 3).reshape(DP // X, share, X * rows)
    along_z = gather(weight, ALONG_Z)[0]
    parts = [along_z] + [swap(along_z, *mask) for mask in ALONG_X]
    early, pieces = lax.optimization_barrier((parts[:2], pieces))
    late = jnp.stack(parts[2:]).reshape(DP // 4, rows, feat)

    def order(first):
        blocks = np.concatenate([first + np.arange(8), 16 + first + np.arange(8)])
        return data_index ^ jnp.asarray(distance[blocks], jnp.int32)

    projected = project(order(0), flat, early + [swap(part, 1) for part in early])
    projected = project(order(8), flat, [late, swap(late, 1)], projected)

    own = lax.all_to_all(
        projected.reshape(DP, block, (views + 1) * images), "dp", split_axis=0, concat_axis=0
    ).reshape(DP, block, views + 1, images)
    average = jnp.sum(own, axis=(0, 3), keepdims=True) / total
    centered = own - average
    variance = jnp.sum(centered * centered, axis=(0, 3), keepdims=True) / total
    inverse = lax.rsqrt(variance + epsilon)
    normed = (centered * inverse).astype(jnp.bfloat16).transpose(2, 1, 0, 3).reshape(views + 1, block, total)
    inverse = inverse.reshape(block, views + 1).T[:views, :, None]

    first, pair, pieces = lax.optimization_barrier((normed[0], normed[1:], pieces))
    slices = lax.all_to_all(
        pieces, "dp", split_axis=0, concat_axis=0, axis_index_groups=SAME_X
    )
    columns_b = lax.all_gather(pair, "mp", axis=0, axis_index_groups=GROUPS)
    columns_b = columns_b.reshape(MP * block, total)
    rows_own, slices = gather(gather(first, STRIDED_Z)[0], ALONG_X, slices)
    rows_own, columns_b = lax.optimization_barrier((rows_own, columns_b))
    columns = lax.all_gather(slices, "mp", axis=0, axis_index_groups=GROUPS)
    rows_other = swap(rows_own, 1).reshape(feat // 2, total)
    rows_own = rows_own.reshape(feat // 2, total)

    def gradient_of(rows_a, with_diagonal):
        correlation = (
            lax.dot_general(rows_a, columns_b, (((1,), (1,)), ((), ())), preferred_element_type=jnp.float32)
            / total
        )
        inner = 2.0 * redundancy_weight * correlation
        if with_diagonal:
            row = lax.broadcasted_iota(jnp.int32, correlation.shape, 0)
            column = lax.broadcasted_iota(jnp.int32, correlation.shape, 1)
            diagonal = (row < block) & (column == lax.rem(model_index, Y) * 2 * block + row)
            inner = inner + diagonal.astype(jnp.float32) * (2.0 * (correlation - 1.0) - inner)
        return (loss_scale * inner).astype(jnp.bfloat16)

    corr_own = gradient_of(rows_own, True)
    corr_other = gradient_of(rows_other, False)

    def times(lhs, rhs, dims):
        return lax.dot_general(lhs, rhs, (dims, ((), ())), preferred_element_type=jnp.float32) / total

    half = (feat // 2, Y, 2, block)
    sides = [
        corr.reshape(half).transpose(2, 0, 1, 3).reshape(2, feat // 2, Y * block)
        for corr in (corr_own, corr_other)
    ]
    terms_b = [
        times(sides[0][k], rows_own, ((0,), (0,))) + times(sides[1][k], rows_other, ((0,), (0,)))
        for k in (0, 1)
    ]
    away = terms_b[1].astype(jnp.bfloat16)
    corr_own, corr_other, away = lax.optimization_barrier((corr_own, corr_other, away))
    terms_b = (terms_b[0] + partner(away).astype(jnp.float32)).astype(jnp.bfloat16)
    terms_b = lax.all_to_all(
        terms_b.reshape(Y, block, total), "mp", split_axis=0, concat_axis=0, axis_index_groups=GROUPS
    )
    terms_other = times(corr_other, columns_b, ((1,), (0,))).astype(jnp.bfloat16)
    terms_own = times(corr_own, columns_b, ((1,), (0,)))
    shape = (4, 4, block, total)
    terms_own, terms_other = terms_own.reshape(shape), swap(terms_other.reshape(shape), 1)
    both = [(terms_own[k] + terms_other[k].astype(jnp.float32)).astype(jnp.bfloat16) for k in range(X)]
    along_x = add(both, ALONG_X)[0].astype(jnp.bfloat16)
    grad_a, terms_b = add(along_x, STRIDED_Z, terms_b)
    grads = jnp.stack([grad_a, jnp.sum(terms_b.astype(jnp.float32), axis=0)])
    wide = normed[:views].astype(jnp.float32)
    grad_mean = jnp.sum(grads, axis=2, keepdims=True) / total
    cross_mean = jnp.sum(grads * wide, axis=2, keepdims=True) / total
    grad_proj = ((grads - grad_mean - wide * cross_mean) * inverse).astype(jnp.bfloat16)
    images_x = total // X
    depth = views * images_x
    blocks = [
        jnp.concatenate([grad_proj[v, :, x * images_x : (x + 1) * images_x] for v in range(views)], axis=1)
        for x in range(X)
    ]
    grad_own = lax.all_to_all(
        jnp.stack([part for part in blocks for _ in range(DP // X // 2)]),
        "dp",
        split_axis=0,
        concat_axis=0,
        axis_index_groups=SAME_CORE,
    )
    grad_own, columns = lax.optimization_barrier((grad_own, columns))
    grad_other = swap(grad_own, 1)
    targets = data_index >> 3 ^ jnp.asarray(X_SLOTS, jnp.int32)
    terms = weight_half(targets, grad_own.reshape(feat // 2, depth), columns)
    terms = weight_half(targets, grad_other.reshape(feat // 2, depth), columns, *terms)
    return finish(position, [terms[0]] + [swap(terms[k + 1], *mask) for k, mask in enumerate(ALONG_X)])


def solution(mesh):
    placed = (P(None, "dp", None), P("dp", "mp"))
    return jax.shard_map(
        per_device, mesh=mesh, in_specs=placed, out_specs=P("dp", "mp"), check_vma=False
    )
```

```python
import functools

import jax
import jax.numpy as jnp
import numpy as np
from jax import lax
from jax.experimental import pallas as pl
from jax.experimental.pallas import tpu as pltpu
from jax.sharding import PartitionSpec as P

epsilon = 1e-05
redundancy_weight = 0.0051
loss_scale = 512.0
DP = 32
MP = 16
Y = 8
X = 4
GROUPS = [list(range(Y)), list(range(Y, MP))]
SAME_CORE = [list(range(core, DP, 2)) for core in range(2)]
SAME_X = [list(range(x * DP // X, (x + 1) * DP // X)) for x in range(X)]
X_SLOTS = np.array([0, 2, 3, 1])
Z_SLOTS = np.array([0, 3, 2, 1])
ALONG_X = [(8 * int(k),) for k in X_SLOTS[1:]]
ALONG_Z = [(2 * int(k),) for k in Z_SLOTS[1:]]
STRIDED_Z = [(0, 8), (4,), (4, 8)]


def swap(array, data, model=0):
    mask = data * MP + model
    return lax.ppermute(array, ("dp", "mp"), [(i, i ^ mask) for i in range(DP * MP)])


def partner(array):
    return swap(array, 2)


def gather(block, masks, *later):
    parts = [block] + [swap(block, *mask) for mask in masks]
    if later:
        parts[1], *later = lax.optimization_barrier((parts[1], *later))
    return jnp.stack(parts), *later


def add(blocks, masks, *later):
    parts = [blocks[0]] + [swap(blocks[k + 1], *mask) for k, mask in enumerate(masks)]
    parts, later = lax.optimization_barrier((parts, later))
    return sum(part.astype(jnp.float32) for part in parts), *later


def project_kernel(last, order_ref, inputs_ref, own_ref, other_ref, *refs):
    out_ref = refs[-1]
    blocks, depth, _ = own_ref.shape
    result = refs[0][...] if last else None
    for core, weight_ref in enumerate((own_ref, other_ref)):
        for k in range(blocks):
            start = pl.multiple_of(order_ref[core * blocks + k] * depth, depth)
            part = jnp.dot(
                inputs_ref[:, pl.ds(start, depth)], weight_ref[k], preferred_element_type=jnp.float32
            )
            result = part if result is None else result + part
    if not last:
        out_ref[...] = result
        return
    features = result.T
    rows = features.shape[1]
    out_ref[:, :rows] = features
    for j in range(DP):
        k = 8 * (j ^ 2)
        out_ref[8 * j : 8 * j + 8, rows:] = features[k : k + 8, rows // 2 :]


def project(order, inputs, own, other, *before):
    rows, feat = inputs.shape[0], own.shape[2]
    vmem = pl.BlockSpec(memory_space=pltpu.VMEM)
    return pl.pallas_call(
        functools.partial(project_kernel, bool(before)),
        in_specs=[pl.BlockSpec(memory_space=pltpu.SMEM)] + [vmem] * (3 + len(before)),
        out_specs=vmem,
        out_shape=jax.ShapeDtypeStruct((feat, rows // 2 * 3) if before else (rows, feat), jnp.float32),
        compiler_params=pltpu.CompilerParams(vmem_limit_bytes=16 * 1024 * 1024),
        cost_estimate=pl.CostEstimate(
            flops=4 * rows * feat * own.shape[0] * own.shape[1],
            bytes_accessed=6 * 1024 * 1024,
            transcendentals=0,
        ),
    )(order, inputs, own, other, *before)


def weight_kernel(targets_ref, grad_ref, columns_ref, *refs):
    before, outs = refs[:-X], refs[-X:]
    slices, devices, share, wide = columns_ref.shape
    rows = wide // X
    half = slices // 2
    features = grad_ref.shape[0]
    for k in range(X):
        target = pl.ds(pl.multiple_of(targets_ref[k] * rows, rows), rows)
        pieces = [
            columns_ref[half * view : half * (view + 1), d, :, target].reshape(half * share, rows)
            for view in range(2)
            for d in range(devices)
        ]
        columns = jnp.concatenate(pieces, axis=0)
        result = jnp.dot(grad_ref[...], columns, preferred_element_type=jnp.float32)
        if before:
            outs[k][:features] = before[k][...]
            outs[k][features:] = result
        else:
            outs[k][...] = result


def weight_half(targets, grad, columns, *before):
    half, depth = grad.shape
    wide = columns.shape[3]
    features = 2 * half if before else half
    vmem = pl.BlockSpec(memory_space=pltpu.VMEM)
    return pl.pallas_call(
        weight_kernel,
        in_specs=[pl.BlockSpec(memory_space=pltpu.SMEM)] + [vmem] * (2 + len(before)),
        out_specs=[vmem] * X,
        out_shape=[jax.ShapeDtypeStruct((features, wide // X), jnp.float32)] * X,
        compiler_params=pltpu.CompilerParams(vmem_limit_bytes=16 * 1024 * 1024),
        cost_estimate=pl.CostEstimate(
            flops=2 * half * depth * wide, bytes_accessed=5 * 1024 * 1024, transcendentals=0
        ),
    )(targets, grad, columns, *before)


def finish_kernel(position_ref, *refs):
    *terms, out_ref, total_ref = refs
    total_ref[...] = (terms[0][...] + terms[1][...]) + (terms[2][...] + terms[3][...])
    blocks = [total_ref[pl.ds(pl.multiple_of(position_ref[j] * 8, 8), 8)] for j in range(DP)]
    out_ref[...] = jnp.concatenate(blocks, axis=0).T


def finish(position, terms):
    features, rows = terms[0].shape
    vmem = pl.BlockSpec(memory_space=pltpu.VMEM)
    return pl.pallas_call(
        finish_kernel,
        in_specs=[pl.BlockSpec(memory_space=pltpu.SMEM)] + [vmem] * len(terms),
        out_specs=vmem,
        out_shape=jax.ShapeDtypeStruct((rows, features), jnp.float32),
        scratch_shapes=[pltpu.VMEM((features, rows), jnp.float32)],
        compiler_params=pltpu.CompilerParams(vmem_limit_bytes=16 * 1024 * 1024),
    )(position, *terms)


def per_device(inputs, weight):
    views, images, width = inputs.shape
    total = images * DP
    data_index = lax.axis_index("dp")
    model_index = lax.axis_index("mp")
    feat = weight.shape[1]
    block = feat // DP
    rows = width // DP
    flat = inputs.reshape(views * images, width)

    place = np.arange(DP)
    distance = place >> 4 | X_SLOTS[place >> 2 & 3] << 3 | Z_SLOTS[place & 3] << 1
    position = (data_index & 1 ^ jnp.asarray(place & 1, jnp.int32)) << 4 | jnp.asarray(place >> 1, jnp.int32)

    share = views * images // Y
    mine = lax.dynamic_slice_in_dim(flat, lax.rem(model_index, Y) * share, share, axis=0)
    pieces = mine.reshape(share, X, DP // X, rows).transpose(2, 0, 1, 3).reshape(DP // X, share, X * rows)
    along_z = gather(weight, ALONG_Z)[0]
    parts = [along_z] + [swap(along_z, *mask) for mask in ALONG_X]
    projected = ()
    for k in (0, 2):
        weight_own, pieces = lax.optimization_barrier((jnp.stack(parts[k : k + 2]), pieces))
        weight_other = swap(weight_own, 1)
        blocks = np.concatenate([4 * k + np.arange(8), 16 + 4 * k + np.arange(8)])
        half = (DP // 4, rows, feat)
        order = data_index ^ jnp.asarray(distance[blocks], jnp.int32)
        halves = weight_own.reshape(half), weight_other.reshape(half)
        projected = (project(order, flat, *halves, *projected),)
    projected = projected[0]

    own = lax.all_to_all(
        projected.reshape(DP, block, (views + 1) * images), "dp", split_axis=0, concat_axis=0
    ).reshape(DP, block, views + 1, images)
    average = jnp.sum(own, axis=(0, 3), keepdims=True) / total
    centered = own - average
    variance = jnp.sum(centered * centered, axis=(0, 3), keepdims=True) / total
    inverse = lax.rsqrt(variance + epsilon)
    normed = (centered * inverse).astype(jnp.bfloat16).transpose(2, 1, 0, 3).reshape(views + 1, block, total)
    inverse = inverse.reshape(block, views + 1).T[:views, :, None]

    first, pair, pieces = lax.optimization_barrier((normed[0], normed[1:], pieces))
    slices = lax.all_to_all(
        pieces, "dp", split_axis=0, concat_axis=0, axis_index_groups=SAME_X
    )
    columns_b = lax.all_gather(pair, "mp", axis=0, axis_index_groups=GROUPS)
    columns_b = columns_b.reshape(MP * block, total)
    rows_own, slices = gather(gather(first, STRIDED_Z)[0], ALONG_X, slices)
    rows_own, columns_b = lax.optimization_barrier((rows_own, columns_b))
    columns = lax.all_gather(slices, "mp", axis=0, axis_index_groups=GROUPS)
    rows_other = swap(rows_own, 1).reshape(feat // 2, total)
    rows_own = rows_own.reshape(feat // 2, total)

    def gradient_of(rows_a, with_diagonal):
        correlation = (
            lax.dot_general(rows_a, columns_b, (((1,), (1,)), ((), ())), preferred_element_type=jnp.float32)
            / total
        )
        inner = 2.0 * redundancy_weight * correlation
        if with_diagonal:
            row = lax.broadcasted_iota(jnp.int32, correlation.shape, 0)
            column = lax.broadcasted_iota(jnp.int32, correlation.shape, 1)
            diagonal = (row < block) & (column == lax.rem(model_index, Y) * 2 * block + row)
            inner = inner + diagonal.astype(jnp.float32) * (2.0 * (correlation - 1.0) - inner)
        return (loss_scale * inner).astype(jnp.bfloat16)

    corr_own = gradient_of(rows_own, True)
    corr_other = gradient_of(rows_other, False)

    def times(lhs, rhs, dims):
        return lax.dot_general(lhs, rhs, (dims, ((), ())), preferred_element_type=jnp.float32) / total

    half = (feat // 2, Y, 2, block)
    sides = [
        corr.reshape(half).transpose(2, 0, 1, 3).reshape(2, feat // 2, Y * block)
        for corr in (corr_own, corr_other)
    ]
    terms_b = [
        times(sides[0][k], rows_own, ((0,), (0,))) + times(sides[1][k], rows_other, ((0,), (0,)))
        for k in (0, 1)
    ]
    away = terms_b[1].astype(jnp.bfloat16)
    corr_own, corr_other, away = lax.optimization_barrier((corr_own, corr_other, away))
    terms_b = (terms_b[0] + partner(away).astype(jnp.float32)).astype(jnp.bfloat16)
    terms_b = lax.all_to_all(
        terms_b.reshape(Y, block, total), "mp", split_axis=0, concat_axis=0, axis_index_groups=GROUPS
    )
    terms_other = times(corr_other, columns_b, ((1,), (0,))).astype(jnp.bfloat16)
    terms_own = times(corr_own, columns_b, ((1,), (0,)))
    shape = (4, 4, block, total)
    terms_own, terms_other = terms_own.reshape(shape), swap(terms_other.reshape(shape), 1)
    both = [(terms_own[k] + terms_other[k].astype(jnp.float32)).astype(jnp.bfloat16) for k in range(X)]
    along_x = add(both, ALONG_X)[0].astype(jnp.bfloat16)
    grad_a, terms_b = add(along_x, STRIDED_Z, terms_b)
    grads = jnp.stack([grad_a, jnp.sum(terms_b.astype(jnp.float32), axis=0)])
    wide = normed[:views].astype(jnp.float32)
    grad_mean = jnp.sum(grads, axis=2, keepdims=True) / total
    cross_mean = jnp.sum(grads * wide, axis=2, keepdims=True) / total
    grad_proj = ((grads - grad_mean - wide * cross_mean) * inverse).astype(jnp.bfloat16)
    images_x = total // X
    depth = views * images_x
    blocks = [
        jnp.concatenate([grad_proj[v, :, x * images_x : (x + 1) * images_x] for v in range(views)], axis=1)
        for x in range(X)
    ]
    grad_own = lax.all_to_all(
        jnp.stack([part for part in blocks for _ in range(DP // X // 2)]),
        "dp",
        split_axis=0,
        concat_axis=0,
        axis_index_groups=SAME_CORE,
    )
    grad_own, columns = lax.optimization_barrier((grad_own, columns))
    grad_other = swap(grad_own, 1)
    targets = data_index >> 3 ^ jnp.asarray(X_SLOTS, jnp.int32)
    terms = weight_half(targets, grad_own.reshape(feat // 2, depth), columns)
    terms = weight_half(targets, grad_other.reshape(feat // 2, depth), columns, *terms)
    return finish(position, [terms[0]] + [swap(terms[k + 1], *mask) for k, mask in enumerate(ALONG_X)])


def solution(mesh):
    placed = (P(None, "dp", None), P("dp", "mp"))
    return jax.shard_map(
        per_device, mesh=mesh, in_specs=placed, out_specs=P("dp", "mp"), check_vma=False
    )
```

```python
import functools

import jax
import jax.numpy as jnp
import numpy as np
from jax import lax
from jax.experimental import pallas as pl
from jax.experimental.pallas import tpu as pltpu
from jax.sharding import PartitionSpec as P

epsilon = 1e-05
redundancy_weight = 0.0051
loss_scale = 512.0
DP = 32
MP = 16
Y = 8
X = 4
GROUPS = [list(range(Y)), list(range(Y, MP))]
SAME_CORE = [list(range(core, DP, 2)) for core in range(2)]
SAME_X = [list(range(x * DP // X, (x + 1) * DP // X)) for x in range(X)]
X_SLOTS = np.array([0, 2, 3, 1])
Z_SLOTS = np.array([0, 3, 2, 1])
ALONG_X = [(8 * int(k),) for k in X_SLOTS[1:]]
ALONG_Z = [(2 * int(k),) for k in Z_SLOTS[1:]]
STRIDED_Z = [(0, 8), (4,), (4, 8)]


def swap(array, data, model=0):
    mask = data * MP + model
    return lax.ppermute(array, ("dp", "mp"), [(i, i ^ mask) for i in range(DP * MP)])


def partner(array):
    return swap(array, 2)


def gather(block, masks, *later):
    parts = [block] + [swap(block, *mask) for mask in masks]
    if later:
        parts[1], *later = lax.optimization_barrier((parts[1], *later))
    return jnp.stack(parts), *later


def add(blocks, masks, *later):
    parts = [blocks[0]] + [swap(blocks[k + 1], *mask) for k, mask in enumerate(masks)]
    parts, later = lax.optimization_barrier((parts, later))
    return sum(part.astype(jnp.float32) for part in parts), *later


def project_kernel(last, order_ref, inputs_ref, own_ref, other_ref, *refs):
    out_ref = refs[-1]
    blocks, depth, _ = own_ref.shape
    result = refs[0][...] if last else None
    for core, weight_ref in enumerate((own_ref, other_ref)):
        for k in range(blocks):
            start = pl.multiple_of(order_ref[core * blocks + k] * depth, depth)
            part = jnp.dot(
                inputs_ref[:, pl.ds(start, depth)], weight_ref[k], preferred_element_type=jnp.float32
            )
            result = part if result is None else result + part
    if not last:
        out_ref[...] = result
        return
    features = result.T
    rows = features.shape[1]
    out_ref[:, :rows] = features
    for j in range(DP):
        k = 8 * (j ^ 2)
        out_ref[8 * j : 8 * j + 8, rows:] = features[k : k + 8, rows // 2 :]


def project(order, inputs, own, other, *before):
    rows, feat = inputs.shape[0], own.shape[2]
    vmem = pl.BlockSpec(memory_space=pltpu.VMEM)
    return pl.pallas_call(
        functools.partial(project_kernel, bool(before)),
        in_specs=[pl.BlockSpec(memory_space=pltpu.SMEM)] + [vmem] * (3 + len(before)),
        out_specs=vmem,
        out_shape=jax.ShapeDtypeStruct((feat, rows // 2 * 3) if before else (rows, feat), jnp.float32),
        compiler_params=pltpu.CompilerParams(vmem_limit_bytes=16 * 1024 * 1024),
        cost_estimate=pl.CostEstimate(
            flops=4 * rows * feat * own.shape[0] * own.shape[1],
            bytes_accessed=6 * 1024 * 1024,
            transcendentals=0,
        ),
    )(order, inputs, own, other, *before)


def weight_kernel(targets_ref, grad_ref, columns_ref, *refs):
    before, outs = refs[:-X], refs[-X:]
    slices, devices, share, wide = columns_ref.shape
    rows = wide // X
    half = slices // 2
    features = grad_ref.shape[0]
    for k in range(X):
        target = pl.ds(pl.multiple_of(targets_ref[k] * rows, rows), rows)
        pieces = [
            columns_ref[half * view : half * (view + 1), d, :, target].reshape(half * share, rows)
            for view in range(2)
            for d in range(devices)
        ]
        columns = jnp.concatenate(pieces, axis=0)
        result = jnp.dot(grad_ref[...], columns, preferred_element_type=jnp.float32)
        if before:
            outs[k][:features] = before[k][...]
            outs[k][features:] = result
        else:
            outs[k][...] = result


def weight_half(targets, grad, columns, *before):
    half, depth = grad.shape
    wide = columns.shape[3]
    features = 2 * half if before else half
    vmem = pl.BlockSpec(memory_space=pltpu.VMEM)
    return pl.pallas_call(
        weight_kernel,
        in_specs=[pl.BlockSpec(memory_space=pltpu.SMEM)] + [vmem] * (2 + len(before)),
        out_specs=[vmem] * X,
        out_shape=[jax.ShapeDtypeStruct((features, wide // X), jnp.float32)] * X,
        compiler_params=pltpu.CompilerParams(vmem_limit_bytes=16 * 1024 * 1024),
        cost_estimate=pl.CostEstimate(
            flops=2 * half * depth * wide, bytes_accessed=5 * 1024 * 1024, transcendentals=0
        ),
    )(targets, grad, columns, *before)


def finish_kernel(position_ref, *refs):
    *terms, out_ref, total_ref = refs
    total_ref[...] = (terms[0][...] + terms[1][...]) + (terms[2][...] + terms[3][...])
    blocks = [total_ref[pl.ds(pl.multiple_of(position_ref[j] * 8, 8), 8)] for j in range(DP)]
    out_ref[...] = jnp.concatenate(blocks, axis=0).T


def finish(position, terms):
    features, rows = terms[0].shape
    vmem = pl.BlockSpec(memory_space=pltpu.VMEM)
    return pl.pallas_call(
        finish_kernel,
        in_specs=[pl.BlockSpec(memory_space=pltpu.SMEM)] + [vmem] * len(terms),
        out_specs=vmem,
        out_shape=jax.ShapeDtypeStruct((rows, features), jnp.float32),
        scratch_shapes=[pltpu.VMEM((features, rows), jnp.float32)],
        compiler_params=pltpu.CompilerParams(vmem_limit_bytes=16 * 1024 * 1024),
    )(position, *terms)


def per_device(inputs, weight):
    views, images, width = inputs.shape
    total = images * DP
    data_index = lax.axis_index("dp")
    model_index = lax.axis_index("mp")
    feat = weight.shape[1]
    block = feat // DP
    rows = width // DP
    flat = inputs.reshape(views * images, width)

    place = np.arange(DP)
    distance = place >> 4 | X_SLOTS[place >> 2 & 3] << 3 | Z_SLOTS[place & 3] << 1
    position = (data_index & 1 ^ jnp.asarray(place & 1, jnp.int32)) << 4 | jnp.asarray(place >> 1, jnp.int32)

    share = views * images // Y
    mine = lax.dynamic_slice_in_dim(flat, lax.rem(model_index, Y) * share, share, axis=0)
    pieces = mine.reshape(share, X, DP // X, rows).transpose(2, 0, 1, 3).reshape(DP // X, share, X * rows)
    along_z = gather(weight, ALONG_Z)[0]
    parts = [along_z] + [swap(along_z, *mask) for mask in ALONG_X]
    projected = ()
    for k in (0, 2):
        weight_own, pieces = lax.optimization_barrier((jnp.stack(parts[k : k + 2]), pieces))
        weight_other = swap(weight_own, 1)
        blocks = np.concatenate([4 * k + np.arange(8), 16 + 4 * k + np.arange(8)])
        half = (DP // 4, rows, feat)
        order = data_index ^ jnp.asarray(distance[blocks], jnp.int32)
        halves = weight_own.reshape(half), weight_other.reshape(half)
        projected = (project(order, flat, *halves, *projected),)
    projected = projected[0]

    own = lax.all_to_all(
        projected.reshape(DP, block, (views + 1) * images), "dp", split_axis=0, concat_axis=0
    ).reshape(DP, block, views + 1, images)
    average = jnp.sum(own, axis=(0, 3), keepdims=True) / total
    centered = own - average
    variance = jnp.sum(centered * centered, axis=(0, 3), keepdims=True) / total
    inverse = lax.rsqrt(variance + epsilon)
    normed = (centered * inverse).astype(jnp.bfloat16).transpose(2, 1, 0, 3).reshape(views + 1, block, total)
    inverse = inverse.reshape(block, views + 1).T[:views, :, None]

    first, pair, pieces = lax.optimization_barrier((normed[0], normed[1:], pieces))
    slices = lax.all_to_all(
        pieces, "dp", split_axis=0, concat_axis=0, axis_index_groups=SAME_X
    )
    columns_b = lax.all_gather(pair, "mp", axis=0, axis_index_groups=GROUPS)
    columns_b = columns_b.reshape(MP * block, total)
    rows_own, slices = gather(gather(first, STRIDED_Z)[0], ALONG_X, slices)
    rows_own, columns_b = lax.optimization_barrier((rows_own, columns_b))
    columns = lax.all_gather(slices, "mp", axis=0, axis_index_groups=GROUPS)
    rows_other = swap(rows_own, 1).reshape(feat // 2, total)
    rows_own = rows_own.reshape(feat // 2, total)

    def gradient_of(rows_a, with_diagonal):
        correlation = (
            lax.dot_general(rows_a, columns_b, (((1,), (1,)), ((), ())), preferred_element_type=jnp.float32)
            / total
        )
        inner = 2.0 * redundancy_weight * correlation
        if with_diagonal:
            row = lax.broadcasted_iota(jnp.int32, correlation.shape, 0)
            column = lax.broadcasted_iota(jnp.int32, correlation.shape, 1)
            diagonal = (row < block) & (column == lax.rem(model_index, Y) * 2 * block + row)
            inner = inner + diagonal.astype(jnp.float32) * (2.0 * (correlation - 1.0) - inner)
        return (loss_scale * inner).astype(jnp.bfloat16)

    corr_own = gradient_of(rows_own, True)
    corr_other = gradient_of(rows_other, False)

    def times(lhs, rhs, dims):
        return lax.dot_general(lhs, rhs, (dims, ((), ())), preferred_element_type=jnp.float32) / total

    terms_other = times(corr_other, columns_b, ((1,), (0,))).astype(jnp.bfloat16)
    corr_other, terms_other = lax.optimization_barrier((corr_other, terms_other))
    half = (feat // 2, Y, 2, block)
    sides = [
        corr.reshape(half).transpose(2, 0, 1, 3).reshape(2, feat // 2, Y * block)
        for corr in (corr_own, corr_other)
    ]
    terms_b = [
        times(sides[0][k], rows_own, ((0,), (0,))) + times(sides[1][k], rows_other, ((0,), (0,)))
        for k in (0, 1)
    ]
    away = terms_b[1].astype(jnp.bfloat16)
    corr_own, corr_other, away = lax.optimization_barrier((corr_own, corr_other, away))
    terms_b = (terms_b[0] + partner(away).astype(jnp.float32)).astype(jnp.bfloat16)
    terms_b = lax.all_to_all(
        terms_b.reshape(Y, block, total), "mp", split_axis=0, concat_axis=0, axis_index_groups=GROUPS
    )
    terms_own = times(corr_own, columns_b, ((1,), (0,)))
    shape = (4, 4, block, total)
    terms_own, terms_other = terms_own.reshape(shape), swap(terms_other.reshape(shape), 1)
    both = [(terms_own[k] + terms_other[k].astype(jnp.float32)).astype(jnp.bfloat16) for k in range(X)]
    along_x = add(both, ALONG_X)[0].astype(jnp.bfloat16)
    grad_a, terms_b = add(along_x, STRIDED_Z, terms_b)
    grads = jnp.stack([grad_a, jnp.sum(terms_b.astype(jnp.float32), axis=0)])
    wide = normed[:views].astype(jnp.float32)
    grad_mean = jnp.sum(grads, axis=2, keepdims=True) / total
    cross_mean = jnp.sum(grads * wide, axis=2, keepdims=True) / total
    grad_proj = ((grads - grad_mean - wide * cross_mean) * inverse).astype(jnp.bfloat16)
    images_x = total // X
    depth = views * images_x
    blocks = [
        jnp.concatenate([grad_proj[v, :, x * images_x : (x + 1) * images_x] for v in range(views)], axis=1)
        for x in range(X)
    ]
    grad_own = lax.all_to_all(
        jnp.broadcast_to(jnp.stack(blocks)[:, None], (X, DP // X // 2, block, depth)).reshape(
            DP // 2, block, depth
        ),
        "dp",
        split_axis=0,
        concat_axis=0,
        axis_index_groups=SAME_CORE,
    )
    grad_own, columns = lax.optimization_barrier((grad_own, columns))
    grad_other = swap(grad_own, 1)
    targets = data_index >> 3 ^ jnp.asarray(X_SLOTS, jnp.int32)
    terms = weight_half(targets, grad_own.reshape(feat // 2, depth), columns)
    terms = weight_half(targets, grad_other.reshape(feat // 2, depth), columns, *terms)
    return finish(position, [terms[0]] + [swap(terms[k + 1], *mask) for k, mask in enumerate(ALONG_X)])


def solution(mesh):
    placed = (P(None, "dp", None), P("dp", "mp"))
    return jax.shard_map(
        per_device, mesh=mesh, in_specs=placed, out_specs=P("dp", "mp"), check_vma=False
    )
```
